32 devices in a mesh: dp: 16 (over z, y, core), head: 2 (over x).
Axes of the slice: x: 2, y: 2, z: 4, core: 2. Of those that a mesh axis runs over, the one named last changes fastest.
Arguments:
- tokens: bfloat16 [32768, 768], P(('dp', 'head')), may hold values from -6 to 6
- labels: int32 [64, 512], P('dp'), may hold values from 0 to 3, never falling along the last dimension, each value on 1 to 256 neighbouring positions
- micro_counts: int32 [16], P('dp'), may hold values from 1 to 4, as said below
- w_query: bfloat16 [768, 768], P(None, 'head'), may hold values from -0.4375 to 0.4375
- b_query: bfloat16 [768], P('head'), may hold values from -3 to 3
- w_key: bfloat16 [768, 768], P(None, 'head'), may hold values from -0.21875 to 0.21875
- w_value: bfloat16 [768, 768], P(None, 'head'), may hold values from -0.21875 to 0.21875
- b_value: bfloat16 [768], P('head'), may hold values from -3 to 3
- w_out: bfloat16 [768, 768], replicated, may hold values from -0.625 to 0.625
- b_out: float32 [768], replicated, may hold values from -2 to 2
- gain_one: float32 [768], replicated, may hold values from 0.5 to 1.5
- shift_one: float32 [768], replicated, may hold values from -2 to 2
- w_up: bfloat16 [768, 3072], replicated, may hold values from -0.21875 to 0.21875
- b_up: float32 [3072], replicated, may hold values from -2 to 2
- w_down: bfloat16 [3072, 768], replicated, may hold values from -0.109375 to 0.109375
- b_down: float32 [768], replicated, may hold values from -2 to 2
- gain_two: float32 [768], replicated, may hold values from 0.5 to 1.5
- shift_two: float32 [768], replicated, may hold values from -2 to 2
- cotangent: bfloat16 [32768, 768], P(('dp', 'head')), may hold values from -6 to 6
Outputs:
- layer_output: bfloat16 [32768, 768], P(('dp', 'head'))
- grad_tokens: float32 [32768, 768], P(('dp', 'head'))
- grad_w_query: float32 [768, 768], P(None, 'head')
- grad_b_query: float32 [768], P('head')
- grad_w_key: float32 [768, 768], P(None, 'head')
- grad_w_value: float32 [768, 768], P(None, 'head')
- grad_b_value: float32 [768], P('head')
- grad_w_out: float32 [768, 768], replicated
- grad_b_out: float32 [768], replicated
- grad_gain_one: float32 [768], replicated
- grad_shift_one: float32 [768], replicated
- grad_w_up: float32 [768, 3072], P(None, ('dp', 'head'))
- grad_b_up: float32 [3072], replicated
- grad_w_down: float32 [3072, 768], P(('dp', 'head'))
- grad_b_down: float32 [768], replicated
- grad_gain_two: float32 [768], replicated
- grad_shift_two: float32 [768], replicated
The draws below stay inside these ranges and needn't reach their ends.
Inputs may be any that keep to these rules, and one draw needn't show every extreme that they name: `micro_counts`: each entry counts the leading micro-batches of its data group, of 4; some group has 4 and some has 1. `labels`: document numbers never fall along a sequence; a document has at most 256 positions.
All inputs are finite; a program needn't handle non-finite values.
Results may differ from the reference program's by a relative error of at most 0.014.
The reference program's roundings to bfloat16 on the way count: a program that leaves them out, or rounds other values in their place, can miss the bound.
Values may be sent and summed in bfloat16 or wider, within the bound.
No kernel may reach another device: no remote copies, remote signals or barrier semaphores. Data moves between devices by JAX's collectives and lax.ppermute only.
A program may use at most 192 MiB of HBM per device.

```python
import math
import jax
import jax.numpy as jnp
import numpy as np
from jax import lax

D = 768
HEADS = 12
HEAD_DIM = 64
FF = 3072
SEQ_LEN = 512
MICRO = 4
SEQ_DEV = 2
TOK_DEV = 1024
SEQS = 64
TOKENS = 32768
N_DP = 16
N_HEAD = 2


def draw_micro_counts(key, part):
    key = jax.random.fold_in(key, 11)
    first_key, second_key = jax.random.split(key)
    counts = jax.random.randint(first_key, (N_DP,), 1, MICRO + 1)
    order = jax.random.permutation(second_key, N_DP)
    counts = counts.at[order[0]].set(MICRO)
    counts = counts.at[order[1]].set(1)
    return counts.astype(jnp.int32)


def block_levels(key, extent, pieces, least, high):
    level = 1.0
    for dim, blocks in pieces:
        draws = jax.random.uniform(jax.random.fold_in(jax.random.fold_in(key, 6), dim), (blocks,), jnp.float32, least / len(pieces), high / len(pieces))
        level = level * jnp.repeat(jnp.exp(draws), extent[dim] // blocks).reshape((-1,) + (1,) * (len(extent) - 1 - dim))
    return level


def length_profile(number_of, total, bound, skew):
    portions = [(1 << 20) // math.isqrt(rank ** skew) + 1 for rank in range(2, number_of + 1)]
    spare, holding = total - bound - (number_of - 1), [1] * (number_of - 1)
    while spare > 0:
        candidates = [i for i in range(number_of - 1) if holding[i] < bound]
        mass, left = sum([portions[i] for i in candidates]), spare
        for i in candidates:
            extra = min(bound - holding[i], max(1, left * portions[i] // mass), spare)
            holding[i] = holding[i] + extra
            spare = spare - extra
    return np.array([bound] + holding)


def uneven_parts(own_key, number_of, total, limit, slope):
    if number_of == 2:
        one = jax.random.randint(own_key, (), max(1, total - limit), min(limit, total - 1) + 1)
        return jnp.stack([one, total - one])
    lengths = jnp.asarray(length_profile(number_of, total, limit, slope), jnp.int32)
    pairs = (number_of - 1) // 2
    donor, taker = lengths[1:1 + 2 * pairs:2], lengths[2:2 + 2 * pairs:2]
    room = jnp.minimum(donor - 1, limit - taker)
    moved = jax.random.randint(jax.random.fold_in(own_key, 1), (pairs,), 0, 1 << 20) % (room + 1)
    lengths = lengths.at[1:1 + 2 * pairs:2].set(donor - moved).at[2:2 + 2 * pairs:2].set(taker + moved)
    return lengths[jax.random.permutation(jax.random.fold_in(own_key, 2), number_of)]


def centred(rng, extent, deviation, most, shards=(), kind=jnp.bfloat16):
    values = deviation * jax.random.normal(rng, extent, jnp.float32)
    if shards:
        values = values * block_levels(rng, extent, shards, -0.22, 0.18)
    return jnp.clip(values, -most, most).astype(kind)


def setup_inputs(seed: int = 0) -> dict:
    arg_keys = jax.random.split(jax.random.key(seed), 20)
    tokens = centred(arg_keys[0], (TOKENS, D), 1.0, 6.0, ((0, 32),))
    labels = jax.vmap(lambda own: jnp.searchsorted(jnp.cumsum(uneven_parts(own, 4, SEQ_LEN, SEQ_LEN // 2, 0)), jnp.arange(SEQ_LEN), side="right"))(jax.random.split(arg_keys[1], SEQS)).reshape((SEQS, SEQ_LEN)).astype(jnp.int32)
    micro_counts = draw_micro_counts(jax.random.fold_in(arg_keys[19], 71), 0)
    w_query = centred(arg_keys[3], (D, D), (D // 4) ** -0.5, 0.4375, ((1, 2),))
    b_query = centred(arg_keys[4], (D,), 0.5, 3.0, ((0, 2),))
    w_key = centred(arg_keys[5], (D, D), D ** -0.5, 0.21875, ((1, 2),))
    w_value = centred(arg_keys[6], (D, D), D ** -0.5, 0.21875, ((1, 2),))
    b_value = centred(arg_keys[7], (D,), 0.5, 3.0, ((0, 2),))
    w_out = centred(arg_keys[8], (D, D), (D // 8) ** -0.5, 0.625)
    b_out = centred(arg_keys[9], (D,), 0.3, 2.0, (), jnp.float32)
    gain_one = jnp.clip(1.0 + 0.1 * jax.random.normal(arg_keys[10], (D,), jnp.float32), 0.5, 1.5)
    shift_one = centred(arg_keys[11], (D,), 0.3, 2.0, (), jnp.float32)
    w_up = centred(arg_keys[12], (D, FF), D ** -0.5, 0.21875)
    b_up = centred(arg_keys[13], (FF,), 0.3, 2.0, (), jnp.float32)
    w_down = centred(arg_keys[14], (FF, D), FF ** -0.5, 0.109375)
    b_down = centred(arg_keys[15], (D,), 0.3, 2.0, (), jnp.float32)
    gain_two = jnp.clip(1.0 + 0.1 * jax.random.normal(arg_keys[16], (D,), jnp.float32), 0.5, 1.5)
    shift_two = centred(arg_keys[17], (D,), 0.3, 2.0, (), jnp.float32)
    cotangent = centred(arg_keys[18], (TOKENS, D), 1.0, 6.0, ((0, 32),))
    return dict(tokens=tokens, labels=labels, micro_counts=micro_counts, w_query=w_query, b_query=b_query, w_key=w_key, w_value=w_value, b_value=b_value, w_out=w_out, b_out=b_out, gain_one=gain_one, shift_one=shift_one, w_up=w_up, b_up=b_up, w_down=w_down, b_down=b_down, gain_two=gain_two, shift_two=shift_two, cotangent=cotangent)


@jax.custom_vjp
def low(v):
    return lax.optimization_barrier(v.astype(jnp.bfloat16)).astype(jnp.float32)

@jax.custom_vjp
def low_back(v):
    return v

def low_keep(v):
    return (low(v), None)

def low_pass(kept, grad):
    return (grad,)

def back_keep(v):
    return (v, None)

def back_low(kept, grad):
    return (low(grad),)
low.defvjp(low_keep, low_pass)
low_back.defvjp(back_keep, back_low)
highest = lax.Precision.HIGHEST
norm_eps = 1e-05

def matmul(left, right):
    return jnp.dot(left, right, precision=highest, preferred_element_type=jnp.float32)

def layer_norm(values, gain, shift):
    average = lax.optimization_barrier(jnp.mean(values, axis=-1, keepdims=True))
    centered = values - average
    variance = lax.optimization_barrier(jnp.mean(centered * centered, axis=-1, keepdims=True))
    return centered * lax.rsqrt(variance + norm_eps) * gain + shift

def attend_one(inputs):
    query_rows, key_rows, value_rows, marks = inputs
    scores = jnp.einsum('qhd,khd->hqk', query_rows, key_rows, precision=highest) * 0.125
    scores = low_back(scores)
    allowed = marks[:, None] == marks[None, :]
    scores = jnp.where(allowed[None], scores, -1000000000.0)
    softened = jax.nn.softmax(scores, axis=-1)
    return jnp.einsum('hqk,khd->qhd', low(softened), value_rows, precision=highest)

def group_forward(rows, marks, w_query, b_query, w_key, w_value, b_value, w_out, b_out, gain_one, shift_one, w_up, b_up, w_down, b_down, gain_two, shift_two):
    entry = low(rows)
    query_rows = low(low_back(matmul(entry, w_query) + b_query))
    key_rows = low(low_back(matmul(entry, w_key)))
    value_rows = low(low_back(matmul(entry, w_value) + b_value))
    shape_four = (marks.shape[0], SEQ_LEN, HEADS, HEAD_DIM)
    context = lax.map(jax.checkpoint(attend_one), (query_rows.reshape(shape_four), key_rows.reshape(shape_four), value_rows.reshape(shape_four), marks))
    context = low(low_back(context.reshape(rows.shape[0], D)))
    attended = low_back(matmul(context, w_out)) + b_out
    hidden = layer_norm(rows + attended, gain_one, shift_one)
    inner = low_back(matmul(low(hidden), w_up) + b_up)
    activated = low(jax.nn.gelu(inner, approximate=False))
    branch = low_back(matmul(activated, w_down)) + b_down
    return layer_norm(hidden + branch, gain_two, shift_two)

def reference(tokens, labels, micro_counts, w_query, b_query, w_key, w_value, b_value, w_out, b_out, gain_one, shift_one, w_up, b_up, w_down, b_down, gain_two, shift_two, cotangent):
    group_rows = TOK_DEV * N_HEAD
    group_seqs = SEQ_DEV * N_HEAD
    params = tuple((item.astype(jnp.float32) for item in (w_query, b_query, w_key, w_value, b_value, w_out, b_out, gain_one, shift_one, w_up, b_up, w_down, b_down, gain_two, shift_two)))
    rows_all = tokens.astype(jnp.float32).reshape(N_DP, group_rows, D)
    cot_all = cotangent.astype(jnp.float32).reshape(N_DP, group_rows, D)
    marks_all = labels.reshape(N_DP, group_seqs, SEQ_LEN)
    micro_index = jnp.arange(group_rows, dtype=jnp.int32) % SEQ_LEN // (SEQ_LEN // MICRO)

    def step(totals, inputs):
        rows, marks, count, cot_group = inputs
        live = (micro_index < count).astype(jnp.float32)

        def forward(entry, *weights):
            return group_forward(entry, marks, *weights)
        result, pullback = jax.vjp(forward, rows, *params)
        grads = pullback(cot_group * live[:, None])
        totals = tuple((acc + item for acc, item in zip(totals, grads[1:])))
        return (totals, (result.astype(jnp.bfloat16), grads[0]))
    start = tuple((jnp.zeros_like(item) for item in params))
    totals, (outputs, input_grads) = lax.scan(step, start, (rows_all, marks_all, micro_counts, cot_all))
    return (outputs.reshape(TOKENS, D), input_grads.reshape(TOKENS, D), totals[0], totals[1], totals[2], totals[3], totals[4], totals[5], totals[6], totals[7], totals[8], totals[9], totals[10], totals[11], totals[12], totals[13], totals[14])
```

```python
import functools

import jax
import jax.numpy as jnp
from jax import lax
from jax.experimental import pallas as pl
from jax.experimental.pallas import tpu as pltpu
from jax.sharding import PartitionSpec as P

HEAD_DIM = 64
MICRO = 4
F32 = jnp.float32
BF16 = jnp.bfloat16
NORM_EPS = 1e-05
MASK = 2.0**30
AXES = ("dp", "head")


def dims(left, right, left_dim, right_dim):
    return lax.dot_general(
        left, right, (((left_dim,), (right_dim,)), ((), ())), preferred_element_type=F32
    )


def matmul(left, right):
    return jnp.dot(left, right, preferred_element_type=F32)


def query_marks(labels, shape):
    lane = lax.broadcasted_iota(jnp.int32, shape, 1)
    return jnp.where((lane & 63) == labels, 1.0, 0.0).astype(BF16)


def key_marks(labels, shape):
    lane = lax.broadcasted_iota(jnp.int32, shape, 1) & 63
    return jnp.where((lane < 4) & (lane != labels), -MASK, 0.0).astype(BF16)


def attend_forward(q_ref, k_ref, v_ref, lab_ref, out_ref, log_ref):
    labels = lab_ref[0]
    shape = (labels.shape[0], 128)
    low = lax.broadcasted_iota(jnp.int32, shape, 1) < HEAD_DIM
    q_extra, k_extra = query_marks(labels, shape), key_marks(labels, shape)
    q = q_ref[...] * jnp.asarray(0.125, BF16)
    k, v = k_ref[...], v_ref[...]
    outs = []
    for t in range(2):
        mine = low if t == 0 else jnp.logical_not(low)
        scores = dims(jnp.where(mine, k, k_extra), jnp.where(mine, q, q_extra), 1, 1)
        largest = jnp.max(scores, axis=0, keepdims=True)
        soft = jnp.exp(scores - largest)
        total = jnp.sum(soft, axis=0, keepdims=True)
        out = dims(v, soft.astype(BF16), 0, 0)
        outs.append(out[t * HEAD_DIM : (t + 1) * HEAD_DIM] * (1.0 / total))
        log_ref[0, 0, t : t + 1] = largest + jnp.log(total)
    out_ref[...] = jnp.concatenate(outs, axis=0).T.astype(BF16)


def run_attend_forward(qkv, labels, seq):
    rows = qkv.shape[0]
    pairs = qkv.shape[1] // (3 * 128)
    part = lambda which: pl.BlockSpec((seq, 128), lambda s, p: (s, which * pairs + p))
    return pl.pallas_call(
        attend_forward,
        grid=(rows // seq, pairs),
        in_specs=[part(0), part(1), part(2), pl.BlockSpec((1, seq, 1), lambda s, p: (s, 0, 0))],
        out_specs=[part(0), pl.BlockSpec((1, 1, 2, seq), lambda s, p: (s, p, 0, 0))],
        out_shape=[
            jax.ShapeDtypeStruct((rows, pairs * 128), BF16),
            jax.ShapeDtypeStruct((rows // seq, pairs, 2, seq), F32),
        ],
        compiler_params=pltpu.CompilerParams(vmem_limit_bytes=40 << 20),
        cost_estimate=pl.CostEstimate(
            flops=rows * pairs * 2 * seq * 256 * 2 * 2, bytes_accessed=4 << 20, transcendentals=0
        ),
        name="attend_forward",
    )(qkv, qkv, qkv, labels)


def attend_backward(
    q_ref, k_ref, v_ref, out_ref, grad_ref, lab_ref, log_ref, dq_ref, dk_ref, dv_ref
):
    labels = lab_ref[0]
    shape = (labels.shape[0], 128)
    low = lax.broadcasted_iota(jnp.int32, shape, 1) < HEAD_DIM
    q_extra, k_extra = query_marks(labels, shape), key_marks(labels, shape)
    q = q_ref[...] * jnp.asarray(0.125, BF16)
    k, v, grad = k_ref[...], v_ref[...], grad_ref[...]
    zero = jnp.zeros_like(q)
    inner = (grad.astype(F32) * out_ref[...].astype(F32)).T
    dqs, dks, dvs = [], [], []
    for t in range(2):
        mine = low if t == 0 else jnp.logical_not(low)
        half = slice(t * HEAD_DIM, (t + 1) * HEAD_DIM)
        scores = dims(jnp.where(mine, k, k_extra), jnp.where(mine, q, q_extra), 1, 1)
        soft = jnp.exp(scores - log_ref[0, 0, t : t + 1])
        grad_soft = dims(v, jnp.where(mine, grad, zero), 1, 1)
        row_inner = jnp.sum(inner[half], axis=0, keepdims=True)
        grad_scores = (soft * (grad_soft - row_inner)).astype(BF16)
        dvs.append(dims(soft.astype(BF16), grad, 1, 0))
        dks.append(dims(grad_scores, q, 1, 0))
        dqs.append(dims(k, grad_scores, 0, 0)[half])
    dv_ref[...] = jnp.where(low, dvs[0], dvs[1]).astype(BF16)
    dk_ref[...] = jnp.where(low, dks[0], dks[1]).astype(BF16)
    dq_ref[...] = (jnp.concatenate(dqs, axis=0).T * 0.125).astype(BF16)


def run_attend_backward(qkv, out, grad, labels, logsum, seq):
    rows = qkv.shape[0]
    pairs = qkv.shape[1] // (3 * 128)
    part = lambda which: pl.BlockSpec((seq, 128), lambda s, p: (s, which * pairs + p))
    shape = jax.ShapeDtypeStruct((rows, pairs * 128), BF16)
    return pl.pallas_call(
        attend_backward,
        grid=(rows // seq, pairs),
        in_specs=[
            part(0),
            part(1),
            part(2),
            part(0),
            part(0),
            pl.BlockSpec((1, seq, 1), lambda s, p: (s, 0, 0)),
            pl.BlockSpec((1, 1, 2, seq), lambda s, p: (s, p, 0, 0)),
        ],
        out_specs=[part(0)] * 3,
        out_shape=[shape] * 3,
        compiler_params=pltpu.CompilerParams(vmem_limit_bytes=40 << 20),
        cost_estimate=pl.CostEstimate(
            flops=rows * pairs * 2 * seq * 256 * 2 * 3, bytes_accessed=8 << 20, transcendentals=0
        ),
        name="attend_backward",
    )(qkv, qkv, qkv, out, grad, labels, logsum)


def gelu_pair(inner):
    t = 1.0 / (1.0 + (0.3275911 * 0.7071067811865476) * jnp.abs(inner))
    bell = jnp.exp(-0.5 * (inner * inner))
    poly = 0.7107068705 + t * (-0.7265760135 + t * 0.5307027145)
    tail = t * (0.127414796 + t * (-0.142248368 + t * poly)) * bell
    phi = jnp.where(inner >= 0, 1.0 - tail, tail)
    return inner * phi, phi + inner * (bell * 0.3989422804014327)


def norm_parts(values):
    centered = values - jnp.mean(values, axis=-1, keepdims=True)
    factor = lax.rsqrt(jnp.mean(centered * centered, axis=-1, keepdims=True) + NORM_EPS)
    return centered * factor, factor


def norm_back(grad_out, normed, factor, gain):
    scaled = grad_out * gain
    return factor * (
        scaled
        - jnp.mean(scaled, axis=-1, keepdims=True)
        - normed * jnp.mean(scaled * normed, axis=-1, keepdims=True)
    )


def feed_forward(
    chunk,
    ctx_a,
    ctx_b,
    tokens,
    w_out,
    w_up,
    w_down,
    vectors,
    b_up,
    cotangent,
    live,
    y_ref,
    hidden_ref,
    normed_ref,
    factor_ref,
    act_ref,
    slope_ref,
    mid_ref,
    sums_ref,
):
    b_out, gain_one, shift_one, b_down, gain_two, shift_two = [
        vectors[i : i + 1] for i in range(6)
    ]
    context = jnp.concatenate([ctx_a[...], ctx_b[...]], axis=1)
    normed_one, factor_one = norm_parts(
        tokens[...].astype(F32) + matmul(context, w_out[...]) + b_out
    )
    normed_ref[...] = normed_one
    factor_ref[...] = factor_one
    hidden = normed_one * gain_one + shift_one
    hidden_low = hidden.astype(BF16)
    hidden_ref[...] = hidden_low
    total = hidden + b_down
    for j in range(w_up.shape[1] // chunk):
        cols = slice(j * chunk, (j + 1) * chunk)
        activated, slope = gelu_pair(matmul(hidden_low, w_up[:, cols]) + b_up[:, cols])
        activated = activated.astype(BF16)
        act_ref[:, cols] = activated
        slope_ref[:, cols] = slope.astype(BF16)
        total = total + matmul(activated, w_down[cols, :])
    normed_two, factor_two = norm_parts(total)
    y_ref[...] = (normed_two * gain_two + shift_two).astype(BF16)
    grad_y = cotangent[...].astype(F32) * live[...]
    grad_mid = norm_back(grad_y, normed_two, factor_two, gain_two)
    mid_ref[...] = grad_mid

    @pl.when(pl.program_id(0) == 0)
    def _():
        sums_ref[...] = jnp.zeros_like(sums_ref)

    sums_ref[0:1] += jnp.sum(grad_y * normed_two, axis=0, keepdims=True)
    sums_ref[1:2] += jnp.sum(grad_y, axis=0, keepdims=True)
    sums_ref[2:3] += jnp.sum(grad_mid, axis=0, keepdims=True)


def run_feed_forward(
    ctx_a, ctx_b, tokens, w_out, w_up, w_down, vectors, b_up, cotangent, live, block=256, chunk=512
):
    rows, width = tokens.shape
    ff = w_up.shape[1]
    half = ctx_a.shape[1]
    token = lambda cols: pl.BlockSpec((block, cols), lambda i: (i, 0))
    held = lambda shape: pl.BlockSpec(shape, lambda i: (0, 0), pipeline_mode=pl.Buffered(1))
    out = jax.ShapeDtypeStruct
    return pl.pallas_call(
        functools.partial(feed_forward, chunk),
        grid=(rows // block,),
        in_specs=[
            token(half),
            token(half),
            token(width),
            held(w_out.shape),
            held(w_up.shape),
            held(w_down.shape),
            held(vectors.shape),
            held(b_up.shape),
            token(width),
            token(1),
        ],
        out_specs=[
            token(width),
            token(width),
            token(width),
            token(1),
            token(ff),
            token(ff),
            token(width),
            pl.BlockSpec((8, width), lambda i: (0, 0)),
        ],
        out_shape=[
            out((rows, width), BF16),
            out((rows, width), BF16),
            out((rows, width), F32),
            out((rows, 1), F32),
            out((rows, ff), BF16),
            out((rows, ff), BF16),
            out((rows, width), F32),
            out((8, width), F32),
        ],
        compiler_params=pltpu.CompilerParams(vmem_limit_bytes=56 << 20),
        cost_estimate=pl.CostEstimate(
            flops=4 * rows * width * (width + 2 * ff), bytes_accessed=30 << 20, transcendentals=0
        ),
        name="feed_forward",
    )(ctx_a, ctx_b, tokens, w_out, w_up, w_down, vectors, b_up, cotangent, live)


def feed_backward(
    groups,
    group_rows,
    core_ref,
    act,
    slope,
    mid,
    w_down,
    w_up,
    hidden,
    ctx_a,
    ctx_b,
    w_out,
    normed,
    factor,
    gain_one,
    down_keep,
    down_send,
    up_keep,
    up_send,
    b_up_ref,
    first_ref,
    grad_ctx_a,
    grad_ctx_b,
    w_out_ref,
    sums_ref,
    mid_low,
    grad_hidden,
):
    step = pl.program_id(0)
    core = core_ref[0]

    @pl.when(step == 0)
    def _():
        grad_mid = mid[...]
        mid_low[...] = grad_mid.astype(BF16)
        grad_hidden[...] = grad_mid

    def put(result, keep, send):
        result = result.reshape(groups, 2, group_rows, result.shape[-1])
        keep[...] = jnp.where(core == 0, result[:, 0], result[:, 1]).astype(BF16)
        send[...] = jnp.where(core == 0, result[:, 1], result[:, 0]).astype(BF16)

    put(dims(act[...], mid_low[...], 0, 0), down_keep, down_send)
    grad_inner = dims(mid_low[...], w_down[...], 1, 1) * slope[...].astype(F32)
    grad_inner = grad_inner.astype(BF16)
    b_up_ref[...] = jnp.sum(grad_inner.astype(F32), axis=0, keepdims=True)
    put(dims(grad_inner, hidden[...], 0, 0), up_keep, up_send)
    grad_hidden[...] += dims(grad_inner, w_up[...], 1, 1)

    @pl.when(step == pl.num_programs(0) - 1)
    def _():
        grad, normed_one = grad_hidden[...], normed[...]
        grad_first = norm_back(grad, normed_one, factor[...], gain_one[...])
        first_ref[...] = grad_first
        sums_ref[0:1] = jnp.sum(grad * normed_one, axis=0, keepdims=True)
        sums_ref[1:2] = jnp.sum(grad, axis=0, keepdims=True)
        sums_ref[2:3] = jnp.sum(grad_first, axis=0, keepdims=True)
        first_low = grad_first.astype(BF16)
        grad_ctx = dims(first_low, w_out[...], 1, 1).astype(BF16)
        half = grad_ctx_a.shape[1]
        grad_ctx_a[...] = grad_ctx[:, :half]
        grad_ctx_b[...] = grad_ctx[:, half:]
        w_out_ref[:half] = dims(ctx_a[...], first_low, 0, 0).astype(BF16)
        w_out_ref[half:] = dims(ctx_b[...], first_low, 0, 0).astype(BF16)


def run_feed_backward(
    core,
    act,
    slope,
    mid,
    w_down,
    w_up,
    hidden,
    ctx_a,
    ctx_b,
    w_out,
    normed,
    factor,
    gain_one,
    rows_dev,
    block=384,
):
    rows, width = mid.shape
    ff = w_up.shape[1]
    half = ctx_a.shape[1]
    group_rows = 2 * rows_dev
    groups = block // (2 * group_rows)
    held = lambda shape: pl.BlockSpec(shape, lambda i, c: (0, 0), pipeline_mode=pl.Buffered(1))
    columns = pl.BlockSpec((rows, block), lambda i, c: (0, i))
    pieces = pl.BlockSpec((groups, group_rows, width), lambda i, c: (i, 0, 0))
    out = jax.ShapeDtypeStruct
    piece_shape = out((ff // (2 * group_rows), group_rows, width), BF16)
    return pl.pallas_call(
        functools.partial(feed_backward, groups, group_rows),
        grid_spec=pltpu.PrefetchScalarGridSpec(
            num_scalar_prefetch=1,
            grid=(ff // block,),
            in_specs=[
                columns,
                columns,
                held((rows, width)),
                pl.BlockSpec((block, width), lambda i, c: (i, 0)),
                pl.BlockSpec((width, block), lambda i, c: (0, i)),
                held((rows, width)),
                held((rows, half)),
                held((rows, half)),
                held((width, width)),
                held((rows, width)),
                held((rows, 1)),
                held((1, width)),
            ],
            out_specs=[
                pieces,
                pieces,
                pieces,
                pieces,
                pl.BlockSpec((1, block), lambda i, c: (0, i)),
                held((rows, width)),
                held((rows, half)),
                held((rows, half)),
                held((width, width)),
                held((8, width)),
            ],
            scratch_shapes=[pltpu.VMEM((rows, width), BF16), pltpu.VMEM((rows, width), F32)],
        ),
        out_shape=[
            piece_shape,
            piece_shape,
            piece_shape,
            piece_shape,
            out((1, ff), F32),
            out((rows, width), F32),
            out((rows, half), BF16),
            out((rows, half), BF16),
            out((width, width), BF16),
            out((8, width), F32),
        ],
        compiler_params=pltpu.CompilerParams(vmem_limit_bytes=56 << 20),
        cost_estimate=pl.CostEstimate(
            flops=2 * rows * width * (4 * ff + 2 * width), bytes_accessed=50 << 20, transcendentals=0
        ),
        name="feed_backward",
    )(
        core, act, slope, mid, w_down, w_up, hidden, ctx_a, ctx_b, w_out, normed, factor, gain_one
    )


class Cube:
    def __init__(self, mesh):
        self.n_dp, self.n_head = mesh.shape["dp"], mesh.shape["head"]
        self.size = self.n_dp * self.n_head
        self.n_bits = self.size.bit_length() - 1
        self.index = lax.axis_index("dp") * self.n_head + lax.axis_index("head")

    def bit(self, which):
        return (self.index >> which) & 1

    def swap(self, value, which):
        pairs = [(i, i ^ (1 << which)) for i in range(self.size)]
        return lax.ppermute(value, AXES, pairs)

    def halve(self, value, axis, which):
        mine = self.bit(which)
        send = lax.dynamic_index_in_dim(value, 1 - mine, axis, keepdims=False)
        keep = lax.dynamic_index_in_dim(value, mine, axis, keepdims=False)
        return keep + self.swap(send, which)

    def double(self, value, which):
        value = lax.optimization_barrier(value)
        return value + self.swap(value, which)

    def join(self, value, which):
        other = self.swap(value, which)
        first = self.bit(which) == 0
        return jnp.concatenate(
            [jnp.where(first, value, other), jnp.where(first, other, value)], axis=0
        )

    def scatter_pieces(self, keep, send, order, rows_dev):
        value = keep + self.swap(send, 1)
        bits = list(range(self.n_bits - 1, 1, -1)) + [0]
        value = value.reshape((2,) * len(bits) + (rows_dev, value.shape[-1]))
        for which in order:
            value = self.halve(value, bits.index(which), which)
            bits.remove(which)
        return value

    def reduce_rows(self, value, order):
        halved = []
        for which in order:
            rows = value.shape[0]
            if rows % 32 == 0:
                value = self.halve(value.reshape(2, rows // 2, value.shape[1]), 0, which)
                halved.append(which)
            else:
                value = self.double(value, which)
        return value, halved

    def gather_rows(self, value, halved):
        for which in reversed(halved):
            value = self.join(value, which)
        return value


def shards(
    mesh,
    tokens,
    labels,
    micro_counts,
    w_query,
    b_query,
    w_key,
    w_value,
    b_value,
    w_out,
    b_out,
    gain_one,
    shift_one,
    w_up,
    b_up,
    w_down,
    b_down,
    gain_two,
    shift_two,
    cotangent,
):
    cube = Cube(mesh)
    rows, width = tokens.shape
    seq = labels.shape[1]
    half = w_query.shape[1]
    ff = w_up.shape[1]
    head, core = cube.bit(0), cube.bit(1)
    upper = list(range(2, cube.n_bits))

    own_w = jnp.concatenate([w_query, w_key, w_value], axis=1)
    part = lax.dynamic_index_in_dim(own_w.reshape(2, width // 2, 3 * half), core, 0, False)
    peer_w = cube.join(cube.swap(part, 0), 1)
    own_b = jnp.concatenate([b_query, jnp.zeros_like(b_query), b_value])
    peer_b = cube.swap(own_b, 0)
    own_rows = lax.dynamic_slice_in_dim(w_out, head * half, half, 0)
    peer_rows = lax.dynamic_slice_in_dim(w_out, (1 - head) * half, half, 0)
    w_out_turned = jnp.concatenate([own_rows, peer_rows], axis=0)
    n_seq = rows // seq
    marks = lax.dynamic_slice_in_dim(labels, head * n_seq, n_seq, 0)[:, :, None]
    position = jnp.arange(rows, dtype=jnp.int32) % seq
    live = (position // (seq // MICRO) < micro_counts[0]).astype(F32)[:, None]
    vectors = jnp.stack(
        [b_out, gain_one, shift_one, b_down, gain_two, shift_two, b_down, b_down]
    )

    def project(weight, offset):
        return (matmul(tokens, weight) + offset.astype(F32)).astype(BF16)

    own_qkv = project(own_w, own_b)
    own_ctx, own_log = run_attend_forward(own_qkv, marks, seq)
    peer_qkv = project(peer_w, peer_b)
    peer_ctx, peer_log = run_attend_forward(peer_qkv, marks, seq)

    layer_output, hidden_low, normed_one, factor_one, activated, slope, grad_mid, sums_two = (
        run_feed_forward(
            own_ctx,
            peer_ctx,
            tokens,
            w_out_turned,
            w_up,
            w_down,
            vectors,
            b_up[None],
            cotangent,
            live,
        )
    )
    rows_dev = ff // cube.size
    (
        down_keep,
        down_send,
        up_keep,
        up_send,
        grad_b_up,
        grad_first,
        own_grad_ctx,
        peer_grad_ctx,
        out_local,
        sums_one,
    ) = run_feed_backward(
        core[None],
        activated,
        slope,
        grad_mid,
        w_down,
        w_up,
        hidden_low,
        own_ctx,
        peer_ctx,
        w_out_turned,
        normed_one,
        factor_one,
        gain_one[None],
        rows_dev,
    )
    down_slice = cube.scatter_pieces(down_keep, down_send, [0] + upper, rows_dev)
    up_slice = cube.scatter_pieces(up_keep, up_send, [2, 0] + upper[1:], rows_dev)
    grad_w_down = down_slice.astype(F32)
    grad_w_up = up_slice.astype(F32).T

    small = jnp.concatenate(
        [sums_one[:3], sums_two[:3], grad_b_up.reshape(ff // width, width)], axis=0
    )
    for which in [1, 0] + upper:
        small = cube.double(small, which)

    out_own = out_local[:half] + cube.swap(out_local[half:], 0)
    out_own, halved = cube.reduce_rows(out_own, [1] + upper)
    out_own = cube.gather_rows(out_own, halved)
    out_peer = cube.swap(out_own, 0)
    grad_w_out = jnp.concatenate(
        [jnp.where(head == 0, out_own, out_peer), jnp.where(head == 0, out_peer, out_own)], axis=0
    ).astype(F32)

    def backward(qkv, ctx, grad_ctx, logsum):
        grads = run_attend_backward(qkv, ctx, grad_ctx, marks, logsum, seq)
        bias = jnp.stack([jnp.sum(grads[0].astype(F32), 0), jnp.sum(grads[2].astype(F32), 0)])
        grads = jnp.concatenate(grads, axis=1)
        return grads, bias, dims(tokens, grads, 0, 0).astype(BF16)

    peer_grads, peer_bias, peer_local = backward(peer_qkv, peer_ctx, peer_grad_ctx, peer_log)
    own_grads, own_bias, own_local = backward(own_qkv, own_ctx, own_grad_ctx, own_log)
    from_peer = cube.halve(peer_local.reshape(2, width // 2, 3 * half), 0, 1)
    own_sum = cube.halve(own_local.reshape(2, width // 2, 3 * half), 0, 1)
    own_sum = own_sum + cube.swap(from_peer, 0)
    own_sum, halved = cube.reduce_rows(own_sum, upper)
    own_sum = cube.gather_rows(own_sum, [1] + halved).astype(F32)
    grad_w_query, grad_w_key, grad_w_value = jnp.split(own_sum, 3, axis=1)
    bias = own_bias + cube.swap(peer_bias, 0)
    for which in [1] + upper:
        bias = cube.double(bias, which)

    grad_tokens = grad_first + dims(own_grads, own_w, 1, 1) + dims(peer_grads, peer_w, 1, 1)
    return (
        layer_output,
        grad_tokens,
        grad_w_query,
        bias[0],
        grad_w_key,
        grad_w_value,
        bias[1],
        grad_w_out,
        small[2],
        small[0],
        small[1],
        grad_w_up,
        small[6:].reshape(ff),
        grad_w_down,
        small[5],
        small[3],
        small[4],
    )


def solution(mesh):
    rows = P(("dp", "head"), None)
    placed = (rows, P("dp", None), P("dp"), P(None, "head"), P("head"), P(None, "head"))
    placed += (P(None, "head"), P("head")) + (P(),) * 10 + (rows,)
    columns = P(None, "head")
    out_specs = (rows, rows, columns, P("head"), columns, columns, P("head"))
    out_specs += (P(),) * 4 + (P(None, ("dp", "head")), P(), rows, P(), P(), P())
    return jax.shard_map(
        functools.partial(shards, mesh),
        mesh=mesh,
        in_specs=placed,
        out_specs=out_specs,
        check_vma=False,
    )
```

```python
import functools

import jax
import jax.numpy as jnp
from jax import lax
from jax.experimental import pallas as pl
from jax.experimental.pallas import tpu as pltpu
from jax.sharding import PartitionSpec as P

HEAD_DIM = 64
MICRO = 4
F32 = jnp.float32
BF16 = jnp.bfloat16
NORM_EPS = 1e-05
MASK = 2.0**30
AXES = ("dp", "head")


def dims(left, right, left_dim, right_dim):
    return lax.dot_general(
        left, right, (((left_dim,), (right_dim,)), ((), ())), preferred_element_type=F32
    )


def matmul(left, right):
    return jnp.dot(left, right, preferred_element_type=F32)


def query_marks(labels, shape):
    lane = lax.broadcasted_iota(jnp.int32, shape, 1)
    return jnp.where((lane & 63) == labels, 1.0, 0.0).astype(BF16)


def key_marks(labels, shape):
    lane = lax.broadcasted_iota(jnp.int32, shape, 1) & 63
    return jnp.where((lane < 4) & (lane != labels), -MASK, 0.0).astype(BF16)


def attend_forward(q_ref, k_ref, v_ref, lab_ref, out_ref, log_ref):
    labels = lab_ref[0]
    shape = (labels.shape[0], 128)
    low = lax.broadcasted_iota(jnp.int32, shape, 1) < HEAD_DIM
    q_extra, k_extra = query_marks(labels, shape), key_marks(labels, shape)
    q = q_ref[...] * jnp.asarray(0.125, BF16)
    k, v = k_ref[...], v_ref[...]
    outs = []
    for t in range(2):
        mine = low if t == 0 else jnp.logical_not(low)
        scores = dims(jnp.where(mine, k, k_extra), jnp.where(mine, q, q_extra), 1, 1)
        largest = jnp.max(scores, axis=0, keepdims=True)
        soft = jnp.exp(scores - largest)
        total = jnp.sum(soft, axis=0, keepdims=True)
        out = dims(v, soft.astype(BF16), 0, 0)
        outs.append(out[t * HEAD_DIM : (t + 1) * HEAD_DIM] * (1.0 / total))
        log_ref[0, 0, t : t + 1] = largest + jnp.log(total)
    out_ref[...] = jnp.concatenate(outs, axis=0).T.astype(BF16)


def run_attend_forward(qkv, labels, seq):
    rows = qkv.shape[0]
    pairs = qkv.shape[1] // (3 * 128)
    part = lambda which: pl.BlockSpec((seq, 128), lambda s, p: (s, which * pairs + p))
    return pl.pallas_call(
        attend_forward,
        grid=(rows // seq, pairs),
        in_specs=[part(0), part(1), part(2), pl.BlockSpec((1, seq, 1), lambda s, p: (s, 0, 0))],
        out_specs=[part(0), pl.BlockSpec((1, 1, 2, seq), lambda s, p: (s, p, 0, 0))],
        out_shape=[
            jax.ShapeDtypeStruct((rows, pairs * 128), BF16),
            jax.ShapeDtypeStruct((rows // seq, pairs, 2, seq), F32),
        ],
        compiler_params=pltpu.CompilerParams(vmem_limit_bytes=40 << 20),
        cost_estimate=pl.CostEstimate(
            flops=rows * pairs * 2 * seq * 256 * 2 * 2, bytes_accessed=4 << 20, transcendentals=0
        ),
        name="attend_forward",
    )(qkv, qkv, qkv, labels)


def attend_backward(
    core_ref,
    q_ref,
    k_ref,
    v_ref,
    out_ref,
    grad_ref,
    lab_ref,
    log_ref,
    x_keep,
    x_send,
    grads_ref,
    keep_ref,
    send_ref,
    keep_sum,
    send_sum,
    bias_sum,
):
    step, pair = pl.program_id(0), pl.program_id(1)
    labels = lab_ref[0]
    shape = (labels.shape[0], 128)
    low = lax.broadcasted_iota(jnp.int32, shape, 1) < HEAD_DIM
    q_extra, k_extra = query_marks(labels, shape), key_marks(labels, shape)
    q = q_ref[...] * jnp.asarray(0.125, BF16)
    k, v, grad = k_ref[...], v_ref[...], grad_ref[...]
    zero = jnp.zeros_like(q)
    inner = (grad.astype(F32) * out_ref[...].astype(F32)).T
    dqs, dks, dvs = [], [], []
    for t in range(2):
        mine = low if t == 0 else jnp.logical_not(low)
        half = slice(t * HEAD_DIM, (t + 1) * HEAD_DIM)
        scores = dims(jnp.where(mine, k, k_extra), jnp.where(mine, q, q_extra), 1, 1)
        soft = jnp.exp(scores - log_ref[0, 0, t : t + 1])
        grad_soft = dims(v, jnp.where(mine, grad, zero), 1, 1)
        row_inner = jnp.sum(inner[half], axis=0, keepdims=True)
        grad_scores = (soft * (grad_soft - row_inner)).astype(BF16)
        dvs.append(dims(soft.astype(BF16), grad, 1, 0))
        dks.append(dims(grad_scores, q, 1, 0))
        dqs.append(dims(k, grad_scores, 0, 0)[half])
    n_pairs = pl.num_programs(1)
    found = (
        (jnp.concatenate(dqs, axis=0).T * 0.125).astype(BF16),
        jnp.where(low, dks[0], dks[1]).astype(BF16),
        jnp.where(low, dvs[0], dvs[1]).astype(BF16),
    )
    for i, value in enumerate(found):
        place = pl.multiple_of((i * n_pairs + pair) * 128, 128)
        grads_ref[:, pl.ds(place, 128)] = value

    @pl.when(pair == n_pairs - 1)
    def _():
        grads = grads_ref[...]
        keep, send = dims(x_keep[...], grads, 0, 0), dims(x_send[...], grads, 0, 0)
        bias = jnp.sum(grads.astype(F32), axis=0, keepdims=True)

        @pl.when(step == 0)
        def _():
            keep_sum[...] = keep
            send_sum[...] = send
            bias_sum[...] = bias

        @pl.when(step > 0)
        def _():
            keep_sum[...] += keep
            send_sum[...] += send
            bias_sum[...] += bias

        @pl.when(step == pl.num_programs(0) - 1)
        def _():
            cols = grads.shape[1]
            total = bias_sum[...]
            third = cols // 3
            parts = [total[:, i * 128 : (i + 1) * 128] for i in range(cols // 128)]
            parts = parts[: third // 128] + parts[2 * third // 128 :]
            rows = jnp.concatenate(parts, axis=0)
            rows = jnp.concatenate(
                [rows, jnp.zeros((keep_ref.shape[0] - rows.shape[0], 128), F32)], axis=0
            ).astype(BF16)
            for ref, value in ((keep_ref, keep_sum), (send_ref, send_sum)):
                ref[:, :cols] = value[...].astype(BF16)
                ref[:, cols:] = rows


def run_attend_backward(core, qkv, out, grad, labels, logsum, tokens, seq):
    rows, cols = qkv.shape
    pairs = cols // (3 * 128)
    half = tokens.shape[1] // 2
    part = lambda which: pl.BlockSpec((seq, 128), lambda s, p, c: (s, which * pairs + p))
    weight = jax.ShapeDtypeStruct((half, cols + 128), BF16)
    whole = pl.BlockSpec((half, cols + 128), lambda s, p, c: (0, 0))
    return pl.pallas_call(
        attend_backward,
        grid_spec=pltpu.PrefetchScalarGridSpec(
            num_scalar_prefetch=1,
            grid=(rows // seq, pairs),
            in_specs=[
                part(0),
                part(1),
                part(2),
                part(0),
                part(0),
                pl.BlockSpec((1, seq, 1), lambda s, p, c: (s, 0, 0)),
                pl.BlockSpec((1, 1, 2, seq), lambda s, p, c: (s, p, 0, 0)),
                pl.BlockSpec((seq, half), lambda s, p, c: (s, c[0])),
                pl.BlockSpec((seq, half), lambda s, p, c: (s, 1 - c[0])),
            ],
            out_specs=[pl.BlockSpec((seq, cols), lambda s, p, c: (s, 0)), whole, whole],
            scratch_shapes=[
                pltpu.VMEM((half, cols), F32),
                pltpu.VMEM((half, cols), F32),
                pltpu.VMEM((1, cols), F32),
            ],
        ),
        out_shape=[jax.ShapeDtypeStruct((rows, cols), BF16), weight, weight],
        compiler_params=pltpu.CompilerParams(vmem_limit_bytes=40 << 20),
        cost_estimate=pl.CostEstimate(
            flops=rows * pairs * 2 * seq * 256 * 2 * 3, bytes_accessed=8 << 20, transcendentals=0
        ),
        name="attend_backward",
    )(core, qkv, qkv, qkv, out, grad, labels, logsum, tokens, tokens)


def gelu_pair(inner):
    phi = 0.5 + 0.5 * lax.erf(inner * 0.7071067811865476)
    bell = jnp.exp(-0.5 * (inner * inner))
    return inner * phi, phi + inner * (bell * 0.3989422804014327)


def norm_parts(values):
    centered = values - jnp.mean(values, axis=-1, keepdims=True)
    factor = lax.rsqrt(jnp.mean(centered * centered, axis=-1, keepdims=True) + NORM_EPS)
    return centered * factor, factor


def norm_back(grad_out, normed, factor, gain):
    scaled = grad_out * gain
    return factor * (
        scaled
        - jnp.mean(scaled, axis=-1, keepdims=True)
        - normed * jnp.mean(scaled * normed, axis=-1, keepdims=True)
    )


def held(shape):
    return pl.BlockSpec(shape, lambda i, *_: (0,) * len(shape), pipeline_mode=pl.Buffered(1))


def add_sums(ref, *values):
    @pl.when(pl.program_id(0) == 0)
    def _():
        ref[...] = jnp.zeros_like(ref)

    for i, value in enumerate(values):
        ref[i : i + 1] += jnp.sum(value, axis=0, keepdims=True)


def feed_forward(
    seq,
    chunk,
    count,
    ctx_a,
    ctx_b,
    tokens,
    w_out,
    w_up,
    w_down,
    vectors,
    b_up,
    cotangent,
    y_ref,
    hidden_ref,
    normed_ref,
    factor_ref,
    act_ref,
    slope_ref,
    mid_ref,
    mid_low_ref,
    sums_ref,
):
    b_out, gain_one, shift_one, b_down, gain_two, shift_two = [
        vectors[i : i + 1] for i in range(6)
    ]
    context = jnp.concatenate([ctx_a[...], ctx_b[...]], axis=1)
    normed_one, factor_one = norm_parts(
        tokens[...].astype(F32) + matmul(context, w_out[...]) + b_out
    )
    normed_ref[...] = normed_one
    factor_ref[...] = jnp.broadcast_to(factor_one, factor_ref.shape)
    hidden = normed_one * gain_one + shift_one
    hidden_low = hidden.astype(BF16)
    hidden_ref[...] = hidden_low
    total = hidden + b_down
    for j in range(w_up.shape[1] // chunk):
        cols = slice(j * chunk, (j + 1) * chunk)
        activated, slope = gelu_pair(matmul(hidden_low, w_up[:, cols]) + b_up[:, cols])
        activated = activated.astype(BF16)
        act_ref[:, cols] = activated
        slope_ref[:, cols] = slope.astype(BF16)
        total = total + matmul(activated, w_down[cols, :])
    normed_two, factor_two = norm_parts(total)
    y_ref[...] = (normed_two * gain_two + shift_two).astype(BF16)
    block = tokens.shape[0]
    place = pl.program_id(0) * block + lax.broadcasted_iota(jnp.int32, (block, 1), 0)
    live = (place % seq // (seq // MICRO) < count[0]).astype(F32)
    grad_y = cotangent[...].astype(F32) * live
    grad_mid = norm_back(grad_y, normed_two, factor_two, gain_two)
    mid_ref[...] = grad_mid
    mid_low_ref[...] = grad_mid.astype(BF16)
    add_sums(sums_ref, grad_y * normed_two, grad_y, grad_mid)


def run_feed_forward(
    seq, count, ctx_a, ctx_b, tokens, w_out, w_up, w_down, vectors, b_up, cotangent, block=256
):
    rows, width = tokens.shape
    ff = w_up.shape[1]
    half = ctx_a.shape[1]
    token = lambda cols: pl.BlockSpec((block, cols), lambda i, c: (i, 0))
    out, near = jax.ShapeDtypeStruct, pltpu.VMEM
    return pl.pallas_call(
        functools.partial(feed_forward, seq, 1024),
        grid_spec=pltpu.PrefetchScalarGridSpec(
            num_scalar_prefetch=1,
            grid=(rows // block,),
            in_specs=[
                token(half),
                token(half),
                token(width),
                held(w_out.shape),
                held(w_up.shape),
                held(w_down.shape),
                held(vectors.shape),
                held(b_up.shape),
                token(width),
            ],
            out_specs=[token(c) for c in (width, width, width, 128, ff, ff, width, width)]
            + [pl.BlockSpec((8, width), lambda i, c: (0, 0))],
        ),
        out_shape=[
            out((rows, width), BF16),
            near((rows, width), BF16),
            out((rows, width), F32),
            out((rows, 128), F32),
            near((rows, ff), BF16),
            near((rows, ff), BF16),
            out((rows, width), F32),
            near((rows, width), BF16),
            out((8, width), F32),
        ],
        compiler_params=pltpu.CompilerParams(vmem_limit_bytes=34 << 20),
        cost_estimate=pl.CostEstimate(
            flops=4 * rows * width * (width + 2 * ff), bytes_accessed=30 << 20, transcendentals=0
        ),
        name="feed_forward",
    )(count, ctx_a, ctx_b, tokens, w_out, w_up, w_down, vectors, b_up, cotangent)


def weight_pieces(groups, group_rows, core_ref, left, right, keep, send):
    core = core_ref[0]
    result = dims(left[...], right[...], 0, 0)
    result = result.reshape(groups, 2, group_rows, result.shape[-1])
    keep[...] = jnp.where(core == 0, result[:, 0], result[:, 1]).astype(BF16)
    send[...] = jnp.where(core == 0, result[:, 1], result[:, 0]).astype(BF16)


def run_weight_pieces(core, left, right, rows_dev, block=768):
    rows, ff = left.shape
    width = right.shape[1]
    group_rows = 2 * rows_dev
    groups = block // (2 * group_rows)
    piece = pl.BlockSpec((groups, group_rows, width), lambda i, c: (i, 0, 0))
    shape = jax.ShapeDtypeStruct((ff // (2 * group_rows), group_rows, width), BF16)
    return pl.pallas_call(
        functools.partial(weight_pieces, groups, group_rows),
        grid_spec=pltpu.PrefetchScalarGridSpec(
            num_scalar_prefetch=1,
            grid=(ff // block,),
            in_specs=[pl.BlockSpec((rows, block), lambda i, c: (0, i)), held((rows, width))],
            out_specs=[piece, piece],
        ),
        out_shape=[shape, shape],
        compiler_params=pltpu.CompilerParams(vmem_limit_bytes=24 << 20),
        cost_estimate=pl.CostEstimate(
            flops=4 * rows * width * ff, bytes_accessed=12 << 20, transcendentals=0
        ),
        name="weight_pieces",
    )(core, left, right)


def inner_gradient(mid_low, w_down, slope, *refs):
    out, sums = refs[-2:]
    grad = (dims(mid_low[...], w_down[...], 1, 1) * slope[...].astype(F32)).astype(BF16)
    out[...] = grad
    sums[...] = jnp.sum(grad.astype(F32), axis=0, keepdims=True)


def run_inner_gradient(mid_low, w_down, slope, part, parts, before=None, block=768):
    rows, width = mid_low.shape
    ff = w_down.shape[0]
    steps = ff // parts // block
    columns = pl.BlockSpec((rows, block), lambda i: (0, part * steps + i))
    args = [mid_low, w_down, slope] + ([] if before is None else [before])
    return pl.pallas_call(
        inner_gradient,
        grid=(steps,),
        in_specs=[
            held((rows, width)),
            pl.BlockSpec((block, width), lambda i: (part * steps + i, 0)),
            columns,
        ]
        + [pl.BlockSpec(memory_space=pl.ANY)] * (len(args) - 3),
        out_specs=[columns, pl.BlockSpec((1, block), lambda i: (0, i))],
        out_shape=[
            pltpu.VMEM((rows, ff), BF16),
            jax.ShapeDtypeStruct((1, ff // parts), F32),
        ],
        input_output_aliases={3: 0} if before is not None else {},
        compiler_params=pltpu.CompilerParams(vmem_limit_bytes=24 << 20),
        cost_estimate=pl.CostEstimate(
            flops=4 * rows * width * ff // parts, bytes_accessed=16 << 20, transcendentals=0
        ),
        name="inner_gradient",
    )(*args)


def first_gradient(
    grad_inner,
    mid,
    w_up,
    w_out,
    ctx_a,
    ctx_b,
    normed,
    factor,
    gain_one,
    first_ref,
    grad_ctx_a,
    grad_ctx_b,
    w_out_ref,
    sums_ref,
    total,
):
    step = pl.program_id(0)
    grad = mid[...] + dims(grad_inner[...], w_up[...], 1, 1)
    normed_one = normed[...]
    grad_first = norm_back(grad, normed_one, factor[:, :1], gain_one[...])
    first_ref[...] = grad_first
    add_sums(sums_ref, grad * normed_one, grad, grad_first)
    first_low = grad_first.astype(BF16)
    grad_ctx = dims(first_low, w_out[...], 1, 1).astype(BF16)
    half = grad_ctx_a.shape[1]
    grad_ctx_a[...] = grad_ctx[:, :half]
    grad_ctx_b[...] = grad_ctx[:, half:]

    @pl.when(step == 0)
    def _():
        total[...] = jnp.zeros_like(total)

    context = jnp.concatenate([ctx_a[...], ctx_b[...]], axis=1)
    total[...] += dims(context, first_low, 0, 0)

    @pl.when(step == pl.num_programs(0) - 1)
    def _():
        w_out_ref[...] = total[...].astype(BF16)


def run_first_gradient(
    grad_inner, mid, w_up, w_out, ctx_a, ctx_b, normed, factor, gain_one, block=256
):
    rows, width = mid.shape
    ff = w_up.shape[1]
    half = ctx_a.shape[1]
    token = lambda cols: pl.BlockSpec((block, cols), lambda i: (i, 0))
    out = jax.ShapeDtypeStruct
    return pl.pallas_call(
        first_gradient,
        grid=(rows // block,),
        in_specs=[
            token(ff),
            token(width),
            held(w_up.shape),
            held(w_out.shape),
            token(half),
            token(half),
            token(width),
            token(128),
            held((1, width)),
        ],
        out_specs=[token(width), token(half), token(half), held((width, width)), held((8, width))],
        out_shape=[
            out((rows, width), F32),
            out((rows, half), BF16),
            out((rows, half), BF16),
            out((width, width), BF16),
            out((8, width), F32),
        ],
        scratch_shapes=[pltpu.VMEM((width, width), F32)],
        compiler_params=pltpu.CompilerParams(vmem_limit_bytes=32 << 20),
        cost_estimate=pl.CostEstimate(
            flops=4 * rows * width * (ff + 2 * width), bytes_accessed=24 << 20, transcendentals=0
        ),
        name="first_gradient",
    )(grad_inner, mid, w_up, w_out, ctx_a, ctx_b, normed, factor, gain_one)


class Cube:
    def __init__(self, mesh):
        self.size = mesh.shape["dp"] * mesh.shape["head"]
        self.n_bits = self.size.bit_length() - 1
        self.upper = list(range(2, self.n_bits))
        self.index = lax.axis_index("dp") * mesh.shape["head"] + lax.axis_index("head")

    def bit(self, which):
        return (self.index >> which) & 1

    def swap(self, value, which):
        pairs = [(i, i ^ (1 << which)) for i in range(self.size)]
        return lax.ppermute(value, AXES, pairs)

    def half(self, value, axis, which, mine):
        bit = self.bit(which) if mine else 1 - self.bit(which)
        return lax.dynamic_index_in_dim(value, bit, axis, keepdims=False)

    def join(self, value, other, which):
        first = self.bit(which) == 0
        return jnp.concatenate(
            [jnp.where(first, value, other), jnp.where(first, other, value)], axis=0
        )


    def scatter_pieces(self, keep, send, rows_dev):
        (other,) = yield [(send, 1)]
        value = keep + other
        bits = list(range(self.n_bits - 1, 1, -1)) + [0]
        value = value.reshape((2,) * len(bits) + (rows_dev, value.shape[-1]))
        middle = value.shape[-1] // 2
        values = [value[..., :middle], value[..., middle:]]
        orders = [[0, 2], [2, 0]]
        left = [list(bits), list(bits)]
        while orders[0]:
            steps = [order.pop(0) for order in orders]
            axes = [held_bits.index(step) for held_bits, step in zip(left, steps)]
            others = yield [
                (self.half(value, axis, step, False), step)
                for value, axis, step in zip(values, axes, steps)
            ]
            values = [
                self.half(value, axis, step, True) + other
                for value, axis, step, other in zip(values, axes, steps, others)
            ]
            for held_bits, step in zip(left, steps):
                held_bits.remove(step)
        value, bits = jnp.concatenate(values, axis=-1), left[0]
        for step in self.upper[1:]:
            axis = bits.index(step)
            (other,) = yield [(self.half(value, axis, step, False), step)]
            value = self.half(value, axis, step, True) + other
            bits.remove(step)
        return value

    def reduce_rows(self, value, order):
        halved = []
        for which in order:
            rows = value.shape[0]
            if rows % 32 == 0:
                value = value.reshape(2, rows // 2, value.shape[1])
                (other,) = yield [(self.half(value, 0, which, False), which)]
                value = self.half(value, 0, which, True) + other
                halved.append(which)
            else:
                value = lax.optimization_barrier(value)
                (other,) = yield [(value, which)]
                value = value + other
        return value, halved

    def gather_rows(self, value, halved):
        for which in reversed(halved):
            (other,) = yield [(value, which)]
            value = self.join(value, other, which)
        return value

    def sum_out(self, own, peer):
        rows, width = own.shape
        value = jnp.concatenate([own, peer], axis=1).reshape(2, rows // 2, 2 * width)
        (other,) = yield [(self.half(value, 0, 1, False), 1)]
        value = self.half(value, 0, 1, True) + other
        value, halved = yield from self.reduce_rows(value, self.upper)
        (other,) = yield [(value[:, width:], 0)]
        value = value[:, :width] + other
        (other,) = yield [(value, 0)]
        value = jnp.concatenate([value, other], axis=1)
        value = yield from self.gather_rows(value, [1] + halved)
        return value[:, :width], value[:, width:]

    def peer_piece(self, keep, send, middle):
        (other,) = yield [(send, 1)]
        value = keep + other
        rows = value.shape[0] // 2
        right = value[:, middle:].reshape(2, rows, -1)
        left, other = yield [(value[:, :middle], 0), (self.half(right, 0, 2, False), 2)]
        right = self.half(right, 0, 2, True) + other
        (right,) = yield [(right, 0)]
        return left, right

    def own_piece(self, keep, send, middle, peer):
        (other,) = yield [(send, 1)]
        value = keep + other
        value = jnp.concatenate([value[:, :middle] + peer.result[0], value[:, middle:]], axis=1)
        value = value.reshape(2, value.shape[0] // 2, value.shape[1])
        (other,) = yield [(self.half(value, 0, 2, False), 2)]
        value = self.half(value, 0, 2, True) + other
        value = jnp.concatenate([value[:, :middle], value[:, middle:] + peer.result[1]], axis=1)
        value, halved = yield from self.reduce_rows(value, self.upper[1:])
        return (yield from self.gather_rows(value, [1, 2] + halved))


class Stream:
    def __init__(self, cube, steps):
        self.cube, self.steps, self.result = cube, steps, None
        self.wants = None
        self.advance(None)

    def advance(self, got):
        try:
            self.wants = self.steps.send(got)
        except StopIteration as stop:
            self.wants, self.result = None, stop.value

    def swaps(self):
        return tuple(self.cube.swap(value, which) for value, which in self.wants)


def tick(streams, work, *carry):
    streams = [stream for stream in streams if stream.wants is not None]
    moved = tuple(stream.swaps() for stream in streams)
    moved, work, carry = lax.optimization_barrier((moved, work, carry))
    for stream, got in zip(streams, moved):
        stream.advance(list(got))
    return (work, *carry)


def shards(
    mesh,
    tokens,
    labels,
    micro_counts,
    w_query,
    b_query,
    w_key,
    w_value,
    b_value,
    w_out,
    b_out,
    gain_one,
    shift_one,
    w_up,
    b_up,
    w_down,
    b_down,
    gain_two,
    shift_two,
    cotangent,
):
    cube = Cube(mesh)
    rows, width = tokens.shape
    seq = labels.shape[1]
    half = w_query.shape[1]
    ff = w_up.shape[1]
    head, core = cube.bit(0), cube.bit(1)

    own_w = jnp.concatenate([w_query, w_key, w_value], axis=1)
    part = lax.dynamic_index_in_dim(own_w.reshape(2, width // 2, 3 * half), core, 0, False)
    own_rows = lax.dynamic_slice_in_dim(w_out, head * half, half, 0)
    peer_rows = lax.dynamic_slice_in_dim(w_out, (1 - head) * half, half, 0)
    w_out_turned = jnp.concatenate([own_rows, peer_rows], axis=0)
    n_seq = rows // seq
    marks = lax.dynamic_slice_in_dim(labels, head * n_seq, n_seq, 0)[:, :, None]
    vectors = jnp.stack(
        [b_out, gain_one, shift_one, b_down, gain_two, shift_two, b_down, b_down]
    )

    def project(weight, offset):
        return (matmul(tokens, weight) + offset.astype(F32)).astype(BF16)

    own_b = jnp.concatenate([b_query, jnp.zeros_like(b_query), b_value])
    own_qkv = project(own_w, own_b)
    own_ctx, own_log = run_attend_forward(own_qkv, marks, seq)
    arrived, peer_b, own_ctx = lax.optimization_barrier(
        (cube.swap(part, 0), cube.swap(own_b, 0), own_ctx)
    )
    peer_w = cube.join(arrived, cube.swap(arrived, 1), 1)
    peer_qkv = project(peer_w, peer_b)
    peer_ctx, peer_log = run_attend_forward(peer_qkv, marks, seq)

    (
        layer_output,
        hidden_low,
        normed_one,
        factor_one,
        activated,
        slope,
        grad_mid,
        mid_low,
        sums_two,
    ) = run_feed_forward(
        seq,
        micro_counts,
        own_ctx,
        peer_ctx,
        tokens,
        w_out_turned,
        w_up,
        w_down,
        vectors,
        b_up[None],
        cotangent,
    )
    rows_dev = ff // cube.size
    cores = core[None]
    stream = lambda steps: Stream(cube, steps)

    keep, send = run_weight_pieces(cores, activated, mid_low, rows_dev)
    (keep, send), mid_low = tick([], (keep, send), mid_low)
    down = stream(cube.scatter_pieces(keep, send, rows_dev))
    inner_one = run_inner_gradient(mid_low, w_down, slope, 0, 2)
    (grad_inner, b_up_one), mid_low = tick([down], tuple(inner_one), mid_low)
    grad_inner, b_up_two = run_inner_gradient(mid_low, w_down, slope, 1, 2, grad_inner)
    keep, send = run_weight_pieces(cores, grad_inner, hidden_low, rows_dev)
    (keep, send), grad_inner, b_up_two = tick([down], (keep, send), grad_inner, b_up_two)
    up = stream(cube.scatter_pieces(keep, send, rows_dev))
    first = run_first_gradient(
        grad_inner,
        grad_mid,
        w_up,
        w_out_turned,
        own_ctx,
        peer_ctx,
        normed_one,
        factor_one,
        gain_one[None],
    )
    (first,) = tick([down, up], tuple(first))
    grad_first, own_grad_ctx, peer_grad_ctx, out_local, sums_one = first

    small = [sums_one[:3], sums_two[:3], b_up_one.reshape(-1, width), b_up_two.reshape(-1, width)]
    small = jnp.concatenate(small, axis=0).astype(BF16)
    n_small = small.shape[0]
    small = small.reshape(2, -1, 128)
    side = small.shape[1]
    small = jnp.pad(small, ((0, 0), (0, half - side), (0, 0)))
    out = stream(
        cube.sum_out(
            jnp.concatenate([out_local[:half], cube.half(small, 0, 0, True)], axis=1),
            jnp.concatenate([out_local[half:], cube.half(small, 0, 0, False)], axis=1),
        )
    )

    def backward(qkv, ctx, grad_ctx, logsum):
        return tuple(
            run_attend_backward(cores, qkv, ctx, grad_ctx, marks, logsum, tokens, seq)
        )

    middle = (3 * half + 128) // 256 * 128
    found = backward(peer_qkv, peer_ctx, peer_grad_ctx, peer_log)
    (peer_grads, keep, send), own_grad_ctx = tick([up, down, out], found, own_grad_ctx)
    peer = stream(cube.peer_piece(keep, send, middle))
    grad_tokens = grad_first + dims(peer_grads, peer_w, 1, 1)
    grad_tokens, own_grad_ctx = tick([peer], grad_tokens, own_grad_ctx)
    found = backward(own_qkv, own_ctx, own_grad_ctx, own_log)
    (own_grads, keep, send), grad_tokens = tick([peer, up, out, down], found, grad_tokens)
    own = stream(cube.own_piece(keep, send, middle, peer))
    grad_tokens = grad_tokens + dims(own_grads, own_w, 1, 1)
    (grad_tokens,) = tick([peer, own, up, out], grad_tokens)
    streams = [own, up, out, down]
    while any(stream.wants is not None for stream in streams):
        tick(streams, ())

    weights = own.result
    grad_w_query, grad_w_key, grad_w_value = [
        weights[:, i * half : (i + 1) * half].astype(F32) for i in range(3)
    ]
    bias = weights[: 2 * half // 128, 3 * half :].astype(F32).reshape(2, half)
    mine, other = out.result
    first = head == 0
    both = jnp.concatenate(
        [jnp.where(first, mine, other), jnp.where(first, other, mine)], axis=0
    ).astype(F32)
    small = jnp.concatenate([both[:side, width:], both[half : half + side, width:]], axis=0)
    small = small.reshape(n_small, width)
    return (
        layer_output,
        grad_tokens,
        grad_w_query,
        bias[0],
        grad_w_key,
        grad_w_value,
        bias[1],
        both[:, :width],
        small[2],
        small[0],
        small[1],
        up.result.astype(F32).T,
        small[6:].reshape(ff),
        down.result.astype(F32),
        small[5],
        small[3],
        small[4],
    )


def solution(mesh):
    rows = P(("dp", "head"), None)
    placed = (rows, P("dp", None), P("dp"), P(None, "head"), P("head"), P(None, "head"))
    placed += (P(None, "head"), P("head")) + (P(),) * 10 + (rows,)
    columns = P(None, "head")
    out_specs = (rows, rows, columns, P("head"), columns, columns, P("head"))
    out_specs += (P(),) * 4 + (P(None, ("dp", "head")), P(), rows, P(), P(), P())
    return jax.shard_map(
        functools.partial(shards, mesh),
        mesh=mesh,
        in_specs=placed,
        out_specs=out_specs,
        check_vma=False,
    )
```

```python
import functools

import jax
import jax.numpy as jnp
from jax import lax
from jax.experimental import pallas as pl
from jax.experimental.pallas import tpu as pltpu
from jax.sharding import PartitionSpec as P

HEAD_DIM = 64
MICRO = 4
F32 = jnp.float32
BF16 = jnp.bfloat16
NORM_EPS = 1e-05
MASK = 2.0**30
AXES = ("dp", "head")


def dims(left, right, left_dim, right_dim):
    return lax.dot_general(
        left, right, (((left_dim,), (right_dim,)), ((), ())), preferred_element_type=F32
    )


def matmul(left, right):
    return jnp.dot(left, right, preferred_element_type=F32)


def far(value):
    return pltpu.with_memory_space_constraint(value, pltpu.HBM)


def query_marks(labels, shape):
    lane = lax.broadcasted_iota(jnp.int32, shape, 1)
    return jnp.where((lane & 63) == labels, 1.0, 0.0).astype(BF16)


def key_marks(labels, shape):
    lane = lax.broadcasted_iota(jnp.int32, shape, 1) & 63
    return jnp.where((lane < 4) & (lane != labels), -MASK, 0.0).astype(BF16)


def pick_rows(core_ref, w_query, w_key, w_value, *outs):
    start = 0
    for out in outs:
        width = out.shape[1] // 3
        for i, weight in enumerate((w_query, w_key, w_value)):
            out[:, i * width : (i + 1) * width] = weight[:, start : start + width]
        start += width


def run_pick_rows(core, w_query, w_key, w_value):
    width, half = w_query.shape
    rows = pl.BlockSpec((width // 2, half), lambda i, c: (c[0], 0))
    shapes = [(width // 2, 3 * (half - 128)), (width // 2, 3 * 128)]
    return pl.pallas_call(
        pick_rows,
        grid_spec=pltpu.PrefetchScalarGridSpec(
            num_scalar_prefetch=1,
            grid=(1,),
            in_specs=[rows] * 3,
            out_specs=[pl.BlockSpec(shape, lambda i, c: (0, 0)) for shape in shapes],
        ),
        out_shape=[jax.ShapeDtypeStruct(shape, BF16) for shape in shapes],
        name="pick_rows",
    )(core, far(w_query), far(w_key), far(w_value))


def attend_pair(pair, pairs, lab_ref, qkv_ref, out_ref, log_ref):
    labels = lab_ref[0]
    shape = (labels.shape[0], 128)
    low = lax.broadcasted_iota(jnp.int32, shape, 1) < HEAD_DIM
    q_extra, k_extra = query_marks(labels, shape), key_marks(labels, shape)
    q, k, v = [
        qkv_ref[:, pl.ds(pl.multiple_of((i * pairs + pair) * 128, 128), 128)] for i in range(3)
    ]
    q = q * jnp.asarray(0.125, BF16)
    outs = []
    for t in range(2):
        mine = low if t == 0 else jnp.logical_not(low)
        scores = dims(jnp.where(mine, k, k_extra), jnp.where(mine, q, q_extra), 1, 1)
        largest = jnp.max(scores, axis=0, keepdims=True)
        soft = jnp.exp(scores - largest)
        total = jnp.sum(soft, axis=0, keepdims=True)
        out = dims(v, soft.astype(BF16), 0, 0)
        outs.append(out[t * HEAD_DIM : (t + 1) * HEAD_DIM] * (1.0 / total))
        log_ref[0, 0, t : t + 1] = largest + jnp.log(total)
    out_ref[...] = jnp.concatenate(outs, axis=0).T.astype(BF16)


def attend_own(core_ref, x, w_query, w_key, w_value, bias, lab_ref, *outs):
    qkv_ref = outs[0]
    pair, pairs = pl.program_id(1), pl.num_programs(1)

    @pl.when(pair == 0)
    def _():
        width = w_query.shape[1]
        for i, weight in enumerate((w_query, w_key, w_value)):
            cols = slice(i * width, (i + 1) * width)
            value = matmul(x[...], weight[...]) + bias[:, cols].astype(F32)
            qkv_ref[:, cols] = value.astype(BF16)

    attend_pair(pair, pairs, lab_ref, *outs)


def attend_peer(core_ref, x_mine, x_other, w_mine, w_other, bias, lab_ref, *outs):
    qkv_ref = outs[0]
    pair, pairs = pl.program_id(1), pl.num_programs(1)

    @pl.when(pair == 0)
    def _():
        value = matmul(x_mine[...], w_mine[...]) + matmul(x_other[...], w_other[...])
        qkv_ref[...] = (value + bias[...].astype(F32)).astype(BF16)

    attend_pair(pair, pairs, lab_ref, *outs)


def run_attend_forward(core, tokens, weights, bias, labels, seq, own):
    rows, depth = tokens.shape
    cols = bias.shape[1]
    pairs = cols // (3 * 128)
    if own:
        xs = [pl.BlockSpec((seq, depth), lambda s, p, c: (s, 0))]
    else:
        xs = [
            pl.BlockSpec((seq, depth // 2), lambda s, p, c: (s, c[0])),
            pl.BlockSpec((seq, depth // 2), lambda s, p, c: (s, 1 - c[0])),
        ]
    fixed = [
        pl.BlockSpec(weight.shape, lambda s, p, c: (0, 0), pipeline_mode=pl.Buffered(1))
        for weight in (*weights, bias)
    ]
    return pl.pallas_call(
        attend_own if own else attend_peer,
        grid_spec=pltpu.PrefetchScalarGridSpec(
            num_scalar_prefetch=1,
            grid=(rows // seq, pairs),
            in_specs=xs + fixed + [pl.BlockSpec((1, seq, 1), lambda s, p, c: (s, 0, 0))],
            out_specs=[
                pl.BlockSpec((seq, cols), lambda s, p, c: (s, 0)),
                pl.BlockSpec((seq, 128), lambda s, p, c: (s, p)),
                pl.BlockSpec((1, 1, 2, seq), lambda s, p, c: (s, p, 0, 0)),
            ],
        ),
        out_shape=[
            pltpu.HBM((rows, cols), BF16),
            pltpu.HBM((rows, cols // 3), BF16),
            jax.ShapeDtypeStruct((rows // seq, pairs, 2, seq), F32),
        ],
        compiler_params=pltpu.CompilerParams(vmem_limit_bytes=14 << 20),
        cost_estimate=pl.CostEstimate(
            flops=rows * pairs * 2 * seq * 256 * 2 * 3, bytes_accessed=8 << 20, transcendentals=0
        ),
        name="attend_forward",
    )(core, *[tokens] * len(xs), *weights, bias, labels)


def attend_backward(
    core_ref,
    q_ref,
    k_ref,
    v_ref,
    out_ref,
    grad_ref,
    lab_ref,
    log_ref,
    x_keep,
    x_send,
    *refs,
):
    refs = list(refs)
    before = refs.pop(0) if len(refs) == 8 else None
    grads_ref, keep_ref, send_ref, bias_ref, keep_sum, send_sum, bias_sum = refs
    step, pair = pl.program_id(0), pl.program_id(1)
    labels = lab_ref[0]
    shape = (labels.shape[0], 128)
    low = lax.broadcasted_iota(jnp.int32, shape, 1) < HEAD_DIM
    q_extra, k_extra = query_marks(labels, shape), key_marks(labels, shape)
    q = q_ref[...] * jnp.asarray(0.125, BF16)
    k, v, grad = k_ref[...], v_ref[...], grad_ref[...]
    zero = jnp.zeros_like(q)
    inner = (grad.astype(F32) * out_ref[...].astype(F32)).T
    dqs, dks, dvs = [], [], []
    for t in range(2):
        mine = low if t == 0 else jnp.logical_not(low)
        half = slice(t * HEAD_DIM, (t + 1) * HEAD_DIM)
        scores = dims(jnp.where(mine, k, k_extra), jnp.where(mine, q, q_extra), 1, 1)
        soft = jnp.exp(scores - log_ref[0, 0, t : t + 1])
        grad_soft = dims(v, jnp.where(mine, grad, zero), 1, 1)
        row_inner = jnp.sum(inner[half], axis=0, keepdims=True)
        grad_scores = (soft * (grad_soft - row_inner)).astype(BF16)
        dvs.append(dims(soft.astype(BF16), grad, 1, 0))
        dks.append(dims(grad_scores, q, 1, 0))
        dqs.append(dims(k, grad_scores, 0, 0)[half])
    n_pairs = pl.num_programs(1)
    found = (
        (jnp.concatenate(dqs, axis=0).T * 0.125).astype(BF16),
        jnp.where(low, dks[0], dks[1]).astype(BF16),
        jnp.where(low, dvs[0], dvs[1]).astype(BF16),
    )
    for i, value in enumerate(found):
        place = pl.multiple_of((i * n_pairs + pair) * 128, 128)
        grads_ref[:, pl.ds(place, 128)] = value

    @pl.when(pair == n_pairs - 1)
    def _():
        grads = grads_ref[...]
        keep, send = dims(x_keep[...], grads, 0, 0), dims(x_send[...], grads, 0, 0)
        bias = jnp.sum(grads.astype(F32), axis=0, keepdims=True)

        @pl.when(step == 0)
        def _():
            keep_sum[...] = keep
            send_sum[...] = send
            bias_sum[...] = bias

        @pl.when(step > 0)
        def _():
            keep_sum[...] += keep
            send_sum[...] += send
            bias_sum[...] += bias

        @pl.when(step == pl.num_programs(0) - 1)
        def _():
            cols = grads.shape[1]
            bias_ref[...] = bias_sum[...]
            for ref, value in ((keep_ref, keep_sum), (send_ref, send_sum)):
                ref[:, :cols] = value[...].astype(BF16)
            if before is not None:
                rows = []
                for sums in (bias_sum[...], before[...]):
                    third = sums.shape[1] // 3
                    for start in (0, 2 * third):
                        for k in range(third // 128):
                            rows.append(sums[:, start + k * 128 : start + (k + 1) * 128])
                fill = keep_ref.shape[0] - len(rows)
                rows = jnp.concatenate(rows + [jnp.zeros((fill, 128), F32)], axis=0)
                for ref in (keep_ref, send_ref):
                    ref[:, cols:] = rows.astype(BF16)


def run_attend_backward(
    core, qkv, out, grad, labels, logsum, tokens, seq, first, count, before=None
):
    rows = qkv.shape[0]
    pairs = qkv.shape[1] // (3 * 128)
    cols = 3 * 128 * count
    half = tokens.shape[1] // 2
    wide = cols if before is None else cols + 128
    part = lambda which: pl.BlockSpec((seq, 128), lambda s, p, c: (s, which * pairs + first + p))
    weight = jax.ShapeDtypeStruct((half, wide), BF16)
    fixed = lambda shape: pl.BlockSpec(shape, lambda s, p, c: (0, 0))
    return pl.pallas_call(
        attend_backward,
        grid_spec=pltpu.PrefetchScalarGridSpec(
            num_scalar_prefetch=1,
            grid=(rows // seq, count),
            in_specs=[
                part(0),
                part(1),
                part(2),
                part(0),
                part(0),
                pl.BlockSpec((1, seq, 1), lambda s, p, c: (s, 0, 0)),
                pl.BlockSpec((1, 1, 2, seq), lambda s, p, c: (s, first + p, 0, 0)),
                pl.BlockSpec((seq, half), lambda s, p, c: (s, c[0])),
                pl.BlockSpec((seq, half), lambda s, p, c: (s, 1 - c[0])),
            ]
            + ([] if before is None else [fixed(before.shape)]),
            out_specs=[
                pl.BlockSpec((seq, cols), lambda s, p, c: (s, 0)),
                fixed((half, wide)),
                fixed((half, wide)),
                fixed((1, cols)),
            ],
            scratch_shapes=[
                pltpu.VMEM((half, cols), F32),
                pltpu.VMEM((half, cols), F32),
                pltpu.VMEM((1, cols), F32),
            ],
        ),
        out_shape=[
            pltpu.HBM((rows, cols), BF16),
            weight,
            weight,
            jax.ShapeDtypeStruct((1, cols), F32),
        ],
        compiler_params=pltpu.CompilerParams(vmem_limit_bytes=18 << 20),
        cost_estimate=pl.CostEstimate(
            flops=rows * count * 2 * seq * 256 * 2 * 3, bytes_accessed=8 << 20, transcendentals=0
        ),
        name="attend_backward",
    )(
        core,
        *[far(qkv)] * 3,
        far(out),
        far(grad),
        labels,
        logsum,
        tokens,
        tokens,
        *([] if before is None else [before]),
    )


def gelu_pair(inner):
    phi = 0.5 + 0.5 * lax.erf(inner * 0.7071067811865476)
    bell = jnp.exp(-0.5 * (inner * inner))
    return inner * phi, phi + inner * (bell * 0.3989422804014327)


def norm_parts(values):
    centered = values - jnp.mean(values, axis=-1, keepdims=True)
    factor = lax.rsqrt(jnp.mean(centered * centered, axis=-1, keepdims=True) + NORM_EPS)
    return centered * factor, factor


def norm_back(grad_out, normed, factor, gain):
    scaled = grad_out * gain
    return factor * (
        scaled
        - jnp.mean(scaled, axis=-1, keepdims=True)
        - normed * jnp.mean(scaled * normed, axis=-1, keepdims=True)
    )


def feed_layer(seq, chunk, n_tok, n_hid, n_ctx, place_ref, count_ref, *refs):
    contexts, refs = refs[:n_ctx], refs[n_ctx:]
    tokens, cotangent, w_out, w_up, w_down, vectors, b_up = refs[:7]
    y_ref, down_keep, down_send, up_keep, up_send, first_ref = refs[7:13]
    grad_ctxs, (out_keep, out_send) = refs[13 : 13 + n_ctx], refs[13 + n_ctx : 15 + n_ctx]
    act, slope, normed, factor, hidden, mid, mid_low, total, sums, b_up_sum = refs[15 + n_ctx :]
    step = pl.program_id(0)
    block = tokens.shape[0]
    core, head = place_ref[0], place_ref[1]
    b_out, gain_one, shift_one, b_down, gain_two, shift_two = [
        vectors[i : i + 1] for i in range(6)
    ]

    def add(row, *values):
        for i, value in enumerate(values):
            sums[row + i : row + i + 1] += jnp.sum(value, axis=0, keepdims=True)

    @pl.when(step == 0)
    def _():
        sums[...] = jnp.zeros_like(sums)
        total[...] = jnp.zeros_like(total)

    @pl.when(step < n_tok)
    def _():
        start = pl.multiple_of(step * block, block)
        here = pl.ds(start, block)
        context = jnp.concatenate([ctx[...] for ctx in contexts], axis=1)
        normed_one, factor_one = norm_parts(
            tokens[...].astype(F32) + matmul(context, w_out[...]) + b_out
        )
        normed[here] = normed_one
        factor[here] = jnp.broadcast_to(factor_one, (block, 128))
        hidden_here = normed_one * gain_one + shift_one
        hidden_low = hidden_here.astype(BF16)
        hidden[here] = hidden_low
        sum_two = hidden_here + b_down
        for j in range(w_up.shape[1] // chunk):
            cols = slice(j * chunk, (j + 1) * chunk)
            activated, gradient = gelu_pair(matmul(hidden_low, w_up[:, cols]) + b_up[:, cols])
            activated = activated.astype(BF16)
            act[here, cols] = activated
            slope[here, cols] = gradient.astype(BF16)
            sum_two = sum_two + matmul(activated, w_down[cols, :])
        normed_two, factor_two = norm_parts(sum_two)
        y_ref[...] = (normed_two * gain_two + shift_two).astype(BF16)
        place = start + lax.broadcasted_iota(jnp.int32, (block, 1), 0)
        live = (place % seq // (seq // MICRO) < count_ref[0]).astype(F32)
        grad_y = cotangent[...].astype(F32) * live
        grad_mid = norm_back(grad_y, normed_two, factor_two, gain_two)
        mid[here] = grad_mid
        mid_low[here] = grad_mid.astype(BF16)
        add(3, grad_y * normed_two, grad_y, grad_mid)

    @pl.when((step >= n_tok) & (step < n_tok + n_hid))
    def _():
        width = act.shape[1] // n_hid
        here = pl.ds(pl.multiple_of((step - n_tok) * width, width), width)

        def put(result, keep, send):
            groups, group_rows, _ = keep.shape
            result = result.reshape(groups, 2, group_rows, result.shape[-1])
            keep[...] = jnp.where(core == 0, result[:, 0], result[:, 1]).astype(BF16)
            send[...] = jnp.where(core == 0, result[:, 1], result[:, 0]).astype(BF16)

        put(dims(act[:, here], mid_low[...], 0, 0), down_keep, down_send)
        grad = dims(mid_low[...], w_down[here, :], 1, 1) * slope[:, here].astype(F32)
        grad = grad.astype(BF16)
        slope[:, here] = grad
        b_up_sum[:, here] = jnp.sum(grad.astype(F32), axis=0, keepdims=True)
        put(dims(grad, hidden[...], 0, 0), up_keep, up_send)

    @pl.when(step >= n_tok + n_hid)
    def _():
        start = pl.multiple_of((step - n_tok - n_hid) * block, block)
        here = pl.ds(start, block)
        grad = mid[here] + dims(slope[here], w_up[...], 1, 1)
        normed_one = normed[here]
        grad_first = norm_back(grad, normed_one, factor[here, :1], gain_one)
        first_ref[...] = grad_first
        add(0, grad * normed_one, grad, grad_first)
        first_low = grad_first.astype(BF16)
        grad_ctx = dims(first_low, w_out[...], 1, 1).astype(BF16)
        start = 0
        for ref in grad_ctxs:
            ref[...] = grad_ctx[:, start : start + ref.shape[1]]
            start += ref.shape[1]
        context = jnp.concatenate([ctx[...] for ctx in contexts], axis=1)
        total[...] += dims(context, first_low, 0, 0)

    @pl.when(step == pl.num_programs(0) - 1)
    def _():
        lanes = [sums[i : i + 1] for i in range(6)] + [b_up_sum[...]]
        lanes = [
            row[:, k * 128 : (k + 1) * 128] for row in lanes for k in range(row.shape[1] // 128)
        ]
        n_side = len(lanes) // 2
        rows, d = out_keep.shape[1], total.shape[1]
        fill = jnp.zeros((rows - n_side, 128), F32)
        sides = [
            jnp.concatenate(part + [fill], axis=0) for part in (lanes[:n_side], lanes[n_side:])
        ]
        for i in range(2):
            side = jnp.where(head == i, sides[0], sides[1]).astype(BF16)
            for ref, which in ((out_keep, core), (out_send, 1 - core)):
                place = pl.multiple_of((2 * i + which) * rows, rows)
                ref[i, :, :d] = total[pl.ds(place, rows)].astype(BF16)
                ref[i, :, d:] = side


def run_feed_layer(
    seq,
    place,
    count,
    contexts,
    tokens,
    cotangent,
    w_out,
    w_up,
    w_down,
    vectors,
    b_up,
    rows_dev,
    block=256,
    width=768,
    chunk=1024,
):
    rows, d = tokens.shape
    ff = w_up.shape[1]
    group_rows = 2 * rows_dev
    groups = width // (2 * group_rows)
    n_tok, n_hid = rows // block, ff // width
    held = lambda shape: pl.BlockSpec(
        shape, lambda i, *_: (0,) * len(shape), pipeline_mode=pl.Buffered(1)
    )
    early = lambda cols: pl.BlockSpec(
        (block, cols), lambda i, *_: (jnp.minimum(i, n_tok - 1), 0)
    )
    late = lambda cols: pl.BlockSpec(
        (block, cols), lambda i, *_: (jnp.maximum(i - n_tok - n_hid, 0), 0)
    )
    twice = lambda cols: pl.BlockSpec(
        (block, cols),
        lambda i, *_: (jnp.where(i < n_tok, i, jnp.maximum(i - n_tok - n_hid, 0)), 0),
    )
    piece = pl.BlockSpec(
        (groups, group_rows, d), lambda i, *_: (jnp.clip(i - n_tok, 0, n_hid - 1), 0, 0)
    )
    out = jax.ShapeDtypeStruct
    pieces = out((ff // (2 * group_rows), group_rows, d), BF16)
    widths = [ctx.shape[1] for ctx in contexts]
    out_half = (2, d // 4, d + 128)
    return pl.pallas_call(
        functools.partial(feed_layer, seq, chunk, n_tok, n_hid, len(contexts)),
        grid_spec=pltpu.PrefetchScalarGridSpec(
            num_scalar_prefetch=2,
            grid=(2 * n_tok + n_hid,),
            in_specs=[twice(w) for w in widths]
            + [early(d), early(d)]
            + [held(value.shape) for value in (w_out, w_up, w_down, vectors, b_up)],
            out_specs=[early(d)]
            + [piece] * 4
            + [late(d)]
            + [late(w) for w in widths]
            + [held(out_half)] * 2,
            scratch_shapes=[
                pltpu.VMEM((rows, ff), BF16),
                pltpu.VMEM((rows, ff), BF16),
                pltpu.VMEM((rows, d), F32),
                pltpu.VMEM((rows, 128), F32),
                pltpu.VMEM((rows, d), BF16),
                pltpu.VMEM((rows, d), F32),
                pltpu.VMEM((rows, d), BF16),
                pltpu.VMEM((d, d), F32),
                pltpu.VMEM((8, d), F32),
                pltpu.VMEM((1, ff), F32),
            ],
        ),
        out_shape=[out((rows, d), BF16)]
        + [pieces] * 4
        + [pltpu.HBM((rows, d), F32)]
        + [pltpu.HBM((rows, w), BF16) for w in widths]
        + [out(out_half, BF16)] * 2,
        compiler_params=pltpu.CompilerParams(vmem_limit_bytes=58 << 20),
        cost_estimate=pl.CostEstimate(
            flops=4 * rows * d * (3 * d + 6 * ff), bytes_accessed=60 << 20, transcendentals=0
        ),
        name="feed_layer",
    )(
        place,
        count,
        *[far(ctx) for ctx in contexts],
        tokens,
        cotangent,
        w_out,
        far(w_up),
        far(w_down),
        vectors,
        b_up,
    )


class Cube:
    def __init__(self, mesh):
        self.size = mesh.shape["dp"] * mesh.shape["head"]
        self.n_bits = self.size.bit_length() - 1
        self.upper = list(range(2, self.n_bits))
        self.index = lax.axis_index("dp") * mesh.shape["head"] + lax.axis_index("head")

    def bit(self, which):
        return (self.index >> which) & 1

    def swap(self, value, which):
        pairs = [(i, i ^ (1 << which)) for i in range(self.size)]
        return lax.ppermute(value, AXES, pairs)

    def half(self, value, axis, which, mine):
        bit = self.bit(which) if mine else 1 - self.bit(which)
        return lax.dynamic_index_in_dim(value, bit, axis, keepdims=False)

    def join(self, value, other, which):
        first = self.bit(which) == 0
        return jnp.concatenate(
            [jnp.where(first, value, other), jnp.where(first, other, value)], axis=0
        )


    def core_pieces(self, keep, send, rows_dev):
        (other,) = yield [(send, 1)]
        shape = (2,) * (self.n_bits - 1) + (rows_dev, keep.shape[-1])
        return [keep.reshape(shape), other.reshape(shape)]

    def pieces(self, terms, cols, order):
        bits = list(range(self.n_bits - 1, 1, -1)) + [0]
        terms = [term[..., cols] for term in terms]
        for step in order:
            axis = bits.index(step)
            (other,) = yield [(sum(self.half(term, axis, step, False) for term in terms), step)]
            terms = [self.half(term, axis, step, True) for term in terms] + [other]
            bits.remove(step)
            if len(terms) > 3:
                terms = [sum(terms)]
        return sum(terms)

    def last_pieces(self, values, order):
        value = jnp.concatenate(values, axis=-1)
        bits = sorted(order, reverse=True)
        for step in order:
            axis = bits.index(step)
            (other,) = yield [(self.half(value, axis, step, False), step)]
            value = self.half(value, axis, step, True) + other
            bits.remove(step)
        return value

    def reduce_rows(self, value, order):
        halved = []
        for which in order:
            rows = value.shape[0]
            if rows % 32 == 0 and rows > 96:
                value = value.reshape(2, rows // 2, value.shape[1])
                (other,) = yield [(self.half(value, 0, which, False), which)]
                value = self.half(value, 0, which, True) + other
                halved.append(which)
            else:
                value = lax.optimization_barrier(value)
                (other,) = yield [(value, which)]
                value = value + other
        return value, halved

    def gather_rows(self, value, halved):
        for which in reversed(halved):
            (other,) = yield [(value, which)]
            value = self.join(value, other, which)
        return value

    def sum_out(self, keep, send):
        (other,) = yield [(send, 1)]
        value = keep + other
        (other,) = yield [(value[1], 0)]
        value, halved = yield from self.reduce_rows(value[0] + other, self.upper)
        value = yield from self.gather_rows(value, halved)
        (other,) = yield [(value, 0)]
        value = jnp.concatenate([value, other], axis=1)
        value = yield from self.gather_rows(value, [1])
        return value[:, : value.shape[1] // 2], value[:, value.shape[1] // 2 :]

    def core_rows(self, keep, send):
        (other,) = yield [(send, 1)]
        return keep + other

    def peer_rows(self, parts):
        value = jnp.concatenate(parts, axis=1)
        value = value.reshape(2, value.shape[0] // 2, value.shape[1])
        (other,) = yield [(self.half(value, 0, 2, False), 2)]
        value = self.half(value, 0, 2, True) + other
        (other,) = yield [(value, 0)]
        return other

    def own_rows(self, parts, peer):
        value = jnp.concatenate(parts, axis=1)
        value = value.reshape(2, value.shape[0] // 2, value.shape[1])
        (other,) = yield [(self.half(value, 0, 2, False), 2)]
        value = self.half(value, 0, 2, True) + other + peer.result
        value, halved = yield from self.reduce_rows(value, self.upper[1:])
        value = yield from self.gather_rows(value, [2] + halved)
        (other,) = yield [(value, 1)]
        return value, other


class Stream:
    def __init__(self, cube, steps):
        self.cube, self.steps, self.result = cube, steps, None
        self.wants = None
        self.advance(None)

    def advance(self, got):
        try:
            self.wants = self.steps.send(got)
        except StopIteration as stop:
            self.wants, self.result = None, stop.value

    def values(self):
        return tuple(value for value, _ in self.wants)

    def swaps(self):
        return tuple(self.cube.swap(value, which) for value, which in self.wants)


def tick(streams, work, *carry, wait=()):
    streams = [stream for stream in streams if stream.wants is not None]
    wait = [stream for stream in wait if stream.wants is not None and stream not in streams]
    moved = tuple(stream.swaps() for stream in streams)
    later = [stream.values() for stream in wait]
    moved, work, carry, later = lax.optimization_barrier((moved, work, carry, later))
    for stream, got in zip(streams, moved):
        stream.advance(list(got))
    for stream, values in zip(wait, later):
        stream.wants = [(value, which) for value, (_, which) in zip(values, stream.wants)]
    return (work, *carry)


def finish_own(pairs, core_ref, mine, other, w_query, w_key, w_value, bias):
    rows = mine.shape[0]
    early = (pairs - 1) * 128
    last = 3 * early + 128
    for value, which in ((mine, core_ref[0]), (other, 1 - core_ref[0])):
        here = pl.ds(pl.multiple_of(which * rows, rows), rows)
        for i, out in enumerate((w_query, w_key, w_value)):
            out[here, :early] = value[:, i * early : (i + 1) * early].astype(F32)
            out[here, early:] = value[:, last + i * 128 : last + (i + 1) * 128].astype(F32)
    bias[...] = mine[: bias.shape[0], 3 * early : last].astype(F32)


def run_finish_own(core, mine, other, pairs):
    rows = mine.shape[0]
    out = jax.ShapeDtypeStruct
    return pl.pallas_call(
        functools.partial(finish_own, pairs),
        grid_spec=pltpu.PrefetchScalarGridSpec(
            num_scalar_prefetch=1,
            grid=(1,),
            in_specs=[pl.BlockSpec(mine.shape, lambda i, c: (0, 0))] * 2,
            out_specs=[pl.BlockSpec((2 * rows, pairs * 128), lambda i, c: (0, 0))] * 3
            + [pl.BlockSpec((16, 128), lambda i, c: (0, 0))],
        ),
        out_shape=[out((2 * rows, pairs * 128), F32)] * 3 + [out((16, 128), F32)],
        compiler_params=pltpu.CompilerParams(vmem_limit_bytes=24 << 20),
        name="finish_own",
    )(core, mine, other)


def shards(
    mesh,
    tokens,
    labels,
    micro_counts,
    w_query,
    b_query,
    w_key,
    w_value,
    b_value,
    w_out,
    b_out,
    gain_one,
    shift_one,
    w_up,
    b_up,
    w_down,
    b_down,
    gain_two,
    shift_two,
    cotangent,
):
    cube = Cube(mesh)
    rows, width = tokens.shape
    seq = labels.shape[1]
    half = w_query.shape[1]
    pairs = half // 128
    ff = w_up.shape[1]
    head, core = cube.bit(0), cube.bit(1)
    place = jnp.stack([core, head])
    cores = core[None]

    part_a, part_b = run_pick_rows(cores, w_query, w_key, w_value)
    own_bias = jnp.concatenate([b_query, jnp.zeros_like(b_query), b_value])[None]
    n_seq = rows // seq
    marks = lax.dynamic_slice_in_dim(labels, head * n_seq, n_seq, 0)[:, :, None]
    own_w = w_query, w_key, w_value
    own_qkv, own_ctx, own_log = run_attend_forward(
        cores, tokens, own_w, own_bias, marks, seq, True
    )
    mine_a, peer_bias, own_ctx, own_w = lax.optimization_barrier(
        (cube.swap(part_a, 0), cube.swap(own_bias, 0), own_ctx, own_w)
    )
    early = [peer_bias[:, i * half : (i + 1) * half - 128] for i in range(3)]
    last = [peer_bias[:, (i + 1) * half - 128 : (i + 1) * half] for i in range(3)]
    bias_a, bias_b = jnp.concatenate(early, axis=1), jnp.concatenate(last, axis=1)
    other_a = cube.swap(mine_a, 1)
    qkv_a, ctx_a, log_a = run_attend_forward(
        cores, tokens, (mine_a, other_a), bias_a, marks, seq, False
    )
    mine_b, ctx_a = lax.optimization_barrier((cube.swap(part_b, 0), ctx_a))
    other_b = cube.swap(mine_b, 1)
    qkv_b, ctx_b, log_b = run_attend_forward(
        cores, tokens, (mine_b, other_b), bias_b, marks, seq, False
    )
    own_rows = lax.dynamic_slice_in_dim(w_out, head * half, half, 0)
    peer_rows = lax.dynamic_slice_in_dim(w_out, (1 - head) * half, half, 0)
    w_out_turned = jnp.concatenate([own_rows, peer_rows], axis=0)
    vectors = jnp.stack(
        [b_out, gain_one, shift_one, b_down, gain_two, shift_two, b_down, b_down]
    )
    rows_dev = ff // cube.size
    (
        layer_output,
        down_keep,
        down_send,
        up_keep,
        up_send,
        grad_first,
        own_grad_ctx,
        grad_ctx_a,
        grad_ctx_b,
        out_keep,
        out_send,
    ) = run_feed_layer(
        seq,
        place,
        micro_counts,
        (own_ctx, ctx_a, ctx_b),
        tokens,
        cotangent,
        w_out_turned,
        w_up,
        w_down,
        vectors,
        b_up[None],
        rows_dev,
    )

    stream = lambda steps: Stream(cube, steps)
    down = stream(cube.core_pieces(down_keep, down_send, rows_dev))
    up = stream(cube.core_pieces(up_keep, up_send, rows_dev))
    out = stream(cube.sum_out(out_keep, out_send))
    left, right = slice(None, width // 2), slice(width // 2, None)


    def backward(qkv, ctx, grad_ctx, logsum, first, count, before=None):
        return tuple(
            run_attend_backward(
                cores, qkv, ctx, grad_ctx, marks, logsum, tokens, seq, first, count, before
            )
        )

    def input_gradient(grads, mine, other):
        return dims(grads, cube.join(mine, other, 1), 1, 1)

    def own_weight(first, count):
        cols = slice(first * 128, (first + count) * 128)
        return jnp.concatenate([weight[:, cols] for weight in own_w], axis=1)

    far_bits = cube.upper[1:]
    found = backward(qkv_b, ctx_b, grad_ctx_b, log_b, 0, 1)
    (grads_b, keep_b, send_b, sums_b), grad_ctx_a = tick(
        [down, out], found, grad_ctx_a, wait=[up]
    )
    down_a = stream(cube.pieces(down.result, left, [3, 0, 2]))
    down_b = stream(cube.pieces(down.result, right, [3, 2, 0]))
    core_b = stream(cube.core_rows(keep_b, send_b))
    found = backward(qkv_a, ctx_a, grad_ctx_a, log_a, 0, pairs - 1, sums_b)
    (grads_a, keep_a, send_a, _), own_grad_ctx = tick(
        [core_b, up, out], found, own_grad_ctx, wait=[down_a, down_b]
    )
    up_a = stream(cube.pieces(up.result, left, [0, 2]))
    up_b = stream(cube.pieces(up.result, right, [2, 0]))
    core_a = stream(cube.core_rows(keep_a, send_a))
    found = backward(own_qkv, own_ctx, own_grad_ctx, own_log, pairs - 1, 1)
    (own_grads_b, keep_b, send_b, sums_b), own_grad_ctx = tick(
        [core_a, down_a, up_a, up_b], found, own_grad_ctx, wait=[down_b, out]
    )
    peer = stream(cube.peer_rows([core_a.result, core_b.result]))
    own_core_b = stream(cube.core_rows(keep_b, send_b))
    found = backward(own_qkv, own_ctx, own_grad_ctx, own_log, 0, pairs - 1, sums_b)
    (own_grads_a, keep_a, send_a, _), grads_a, grads_b, grad_first = tick(
        [own_core_b, down_a, down_b, out, peer],
        found,
        grads_a,
        grads_b,
        grad_first,
        wait=[up_a, up_b],
    )
    own_core_a = stream(cube.core_rows(keep_a, send_a))
    grad_tokens = grad_first + input_gradient(grads_a, mine_a, other_a)
    grad_tokens = grad_tokens + input_gradient(grads_b, mine_b, other_b)
    everything = [down_a, down_b, up_a, up_b, out, peer]
    grad_tokens, own_grads_a, own_grads_b = tick(
        [own_core_a, out], grad_tokens, own_grads_a, own_grads_b, wait=everything
    )
    own = stream(cube.own_rows([own_core_a.result, own_core_b.result], peer))
    grad_tokens = grad_tokens + dims(own_grads_a, own_weight(0, pairs - 1), 1, 1)
    grad_tokens = grad_tokens + dims(own_grads_b, own_weight(pairs - 1, 1), 1, 1)
    (grad_tokens,) = tick([peer, own, out], grad_tokens, wait=everything)
    tick([own, up_a, up_b], (), wait=everything)
    up_far = stream(cube.last_pieces([up_a.result, up_b.result], far_bits))
    tick([own, down_b, out, up_far], (), wait=everything)
    tick([own, down_a, down_b], (), wait=everything + [up_far])
    down_far = stream(cube.last_pieces([down_a.result, down_b.result], far_bits[1:]))
    streams = [own, up_far, down_far, out]
    while any(stream.wants is not None for stream in streams):
        tick(streams, ())

    grad_w_query, grad_w_key, grad_w_value, bias = run_finish_own(cores, *own.result, pairs)
    last = 2 * (pairs - 1)
    bias = [
        jnp.concatenate([bias[i * (pairs - 1) : (i + 1) * (pairs - 1)], bias[last + i : last + i + 1]])
        for i in range(2)
    ]
    mine, other = out.result
    first = head == 0
    both = jnp.concatenate(
        [jnp.where(first, mine, other), jnp.where(first, other, mine)], axis=0
    ).astype(F32)
    side = (ff + 6 * width) // 256
    small = jnp.concatenate([both[:side, width:], both[half : half + side, width:]], axis=0)
    small = small.reshape(-1, width)
    return (
        layer_output,
        grad_tokens,
        grad_w_query,
        bias[0].reshape(half),
        grad_w_key,
        grad_w_value,
        bias[1].reshape(half),
        both[:, :width],
        small[2],
        small[0],
        small[1],
        up_far.result.astype(F32).T,
        small[6:].reshape(ff),
        down_far.result.astype(F32),
        small[5],
        small[3],
        small[4],
    )


def solution(mesh):
    rows = P(("dp", "head"), None)
    placed = (rows, P("dp", None), P("dp"), P(None, "head"), P("head"), P(None, "head"))
    placed += (P(None, "head"), P("head")) + (P(),) * 10 + (rows,)
    columns = P(None, "head")
    out_specs = (rows, rows, columns, P("head"), columns, columns, P("head"))
    out_specs += (P(),) * 4 + (P(None, ("dp", "head")), P(), rows, P(), P(), P())
    return jax.shard_map(
        functools.partial(shards, mesh),
        mesh=mesh,
        in_specs=placed,
        out_specs=out_specs,
        check_vma=False,
    )
```

```python
import functools

import jax
import jax.numpy as jnp
from jax import lax
from jax.experimental import pallas as pl
from jax.experimental.pallas import tpu as pltpu
from jax.sharding import PartitionSpec as P

HEAD_DIM = 64
MICRO = 4
F32 = jnp.float32
BF16 = jnp.bfloat16
NORM_EPS = 1e-05
MASK = 2.0**30
AXES = ("dp", "head")


def dims(left, right, left_dim, right_dim):
    return lax.dot_general(
        left, right, (((left_dim,), (right_dim,)), ((), ())), preferred_element_type=F32
    )


def matmul(left, right):
    return jnp.dot(left, right, preferred_element_type=F32)


def far(value):
    return pltpu.with_memory_space_constraint(value, pltpu.HBM)


def query_marks(labels, shape):
    lane = lax.broadcasted_iota(jnp.int32, shape, 1)
    return jnp.where((lane & 63) == labels, 1.0, 0.0).astype(BF16)


def key_marks(labels, shape):
    lane = lax.broadcasted_iota(jnp.int32, shape, 1) & 63
    return jnp.where((lane < 4) & (lane != labels), -MASK, 0.0).astype(BF16)


def pick_rows(core_ref, w_query, w_key, w_value, out):
    half = w_query.shape[1]
    for i, weight in enumerate((w_query, w_key, w_value)):
        out[:, i * half : (i + 1) * half] = weight[...]


def run_pick_rows(core, w_query, w_key, w_value):
    width, half = w_query.shape
    rows = pl.BlockSpec((width // 2, half), lambda i, c: (c[0], 0))
    return pl.pallas_call(
        pick_rows,
        grid_spec=pltpu.PrefetchScalarGridSpec(
            num_scalar_prefetch=1,
            grid=(1,),
            in_specs=[rows] * 3,
            out_specs=pl.BlockSpec((width // 2, 3 * half), lambda i, c: (0, 0)),
        ),
        out_shape=jax.ShapeDtypeStruct((width // 2, 3 * half), BF16),
        name="pick_rows",
    )(core, far(w_query), far(w_key), far(w_value))


def attend_pairs(lab_ref, qkv_ref, out_ref, log_ref):
    labels = lab_ref[0]
    shape = (labels.shape[0], 128)
    half = out_ref.shape[1]
    low = lax.broadcasted_iota(jnp.int32, shape, 1) < HEAD_DIM
    q_extra, k_extra = query_marks(labels, shape), key_marks(labels, shape)
    for pair in range(half // 128):
        q, k, v = [
            qkv_ref[:, i * half + pair * 128 : i * half + (pair + 1) * 128] for i in range(3)
        ]
        q = q * jnp.asarray(0.125, BF16)
        outs = []
        for t in range(2):
            mine = low if t == 0 else jnp.logical_not(low)
            scores = dims(jnp.where(mine, k, k_extra), jnp.where(mine, q, q_extra), 1, 1)
            largest = jnp.max(scores, axis=0, keepdims=True)
            soft = jnp.exp(scores - largest)
            total = jnp.sum(soft, axis=0, keepdims=True)
            out = dims(v, soft.astype(BF16), 0, 0)
            outs.append(out[t * HEAD_DIM : (t + 1) * HEAD_DIM] * (1.0 / total))
            log_ref[0, pair, t : t + 1] = largest + jnp.log(total)
        out_ref[:, pair * 128 : (pair + 1) * 128] = jnp.concatenate(outs, axis=0).T.astype(BF16)


def attend_own(core_ref, x, w_query, w_key, w_value, bias, lab_ref, *outs):
    qkv_ref = outs[0]
    width = w_query.shape[1]
    for i, weight in enumerate((w_query, w_key, w_value)):
        cols = slice(i * width, (i + 1) * width)
        value = matmul(x[...], weight[...]) + bias[:, cols].astype(F32)
        qkv_ref[:, cols] = value.astype(BF16)
    attend_pairs(lab_ref, *outs)


def attend_peer(core_ref, x_mine, x_other, w_mine, w_other, bias, lab_ref, *outs):
    qkv_ref = outs[0]
    width = qkv_ref.shape[1] // 3
    for i in range(3):
        cols = slice(i * width, (i + 1) * width)
        value = matmul(x_mine[...], w_mine[:, cols]) + matmul(x_other[...], w_other[:, cols])
        qkv_ref[:, cols] = (value + bias[:, cols].astype(F32)).astype(BF16)
    attend_pairs(lab_ref, *outs)


def run_attend_forward(core, tokens, weights, bias, labels, seq, own):
    rows, depth = tokens.shape
    cols = bias.shape[1]
    pairs = cols // (3 * 128)
    if own:
        xs = [pl.BlockSpec((seq, depth), lambda s, c: (s, 0))]
    else:
        xs = [
            pl.BlockSpec((seq, depth // 2), lambda s, c: (s, c[0])),
            pl.BlockSpec((seq, depth // 2), lambda s, c: (s, 1 - c[0])),
        ]
    fixed = [
        pl.BlockSpec(weight.shape, lambda s, c: (0, 0), pipeline_mode=pl.Buffered(1))
        for weight in (*weights, bias)
    ]
    return pl.pallas_call(
        attend_own if own else attend_peer,
        grid_spec=pltpu.PrefetchScalarGridSpec(
            num_scalar_prefetch=1,
            grid=(rows // seq,),
            in_specs=xs + fixed + [pl.BlockSpec((1, seq, 1), lambda s, c: (s, 0, 0))],
            out_specs=[
                pl.BlockSpec((seq, cols), lambda s, c: (s, 0)),
                pl.BlockSpec((seq, cols // 3), lambda s, c: (s, 0)),
                pl.BlockSpec((1, pairs, 2, seq), lambda s, c: (s, 0, 0, 0)),
            ],
        ),
        out_shape=[
            pltpu.HBM((rows, cols), BF16),
            pltpu.HBM((rows, cols // 3), BF16),
            jax.ShapeDtypeStruct((rows // seq, pairs, 2, seq), F32),
        ],
        compiler_params=pltpu.CompilerParams(vmem_limit_bytes=24 << 20),
        cost_estimate=pl.CostEstimate(
            flops=rows * pairs * 2 * seq * 256 * 2 * 3, bytes_accessed=8 << 20, transcendentals=0
        ),
        name="attend_forward",
    )(core, *[tokens] * len(xs), *weights, bias, labels)


def attend_backward(
    first,
    count,
    lone,
    core_ref,
    q_ref,
    k_ref,
    v_ref,
    out_ref,
    grad_ref,
    lab_ref,
    log_ref,
    x_keep,
    x_send,
    *refs,
):
    refs = list(refs)
    before = refs.pop(0) if len(refs) == 8 else None
    grads_ref, keep_ref, send_ref, bias_ref, keep_sum, send_sum, bias_sum = refs
    early = count - 1 if lone else count
    step = pl.program_id(0)
    labels = lab_ref[0]
    shape = (labels.shape[0], 128)
    low = lax.broadcasted_iota(jnp.int32, shape, 1) < HEAD_DIM
    q_extra, k_extra = query_marks(labels, shape), key_marks(labels, shape)
    for pair in range(count):
        cols = slice((first + pair) * 128, (first + pair + 1) * 128)
        q = q_ref[:, cols] * jnp.asarray(0.125, BF16)
        k, v, grad = k_ref[:, cols], v_ref[:, cols], grad_ref[:, cols]
        zero = jnp.zeros_like(q)
        inner = (grad.astype(F32) * out_ref[:, cols].astype(F32)).T
        dqs, dks, dvs = [], [], []
        for t in range(2):
            mine = low if t == 0 else jnp.logical_not(low)
            half = slice(t * HEAD_DIM, (t + 1) * HEAD_DIM)
            scores = dims(jnp.where(mine, k, k_extra), jnp.where(mine, q, q_extra), 1, 1)
            soft = jnp.exp(scores - log_ref[0, first + pair, t : t + 1])
            grad_soft = dims(v, jnp.where(mine, grad, zero), 1, 1)
            row_inner = jnp.sum(inner[half], axis=0, keepdims=True)
            grad_scores = (soft * (grad_soft - row_inner)).astype(BF16)
            dvs.append(dims(soft.astype(BF16), grad, 1, 0))
            dks.append(dims(grad_scores, q, 1, 0))
            dqs.append(dims(k, grad_scores, 0, 0)[half])
        found = (
            (jnp.concatenate(dqs, axis=0).T * 0.125).astype(BF16),
            jnp.where(low, dks[0], dks[1]).astype(BF16),
            jnp.where(low, dvs[0], dvs[1]).astype(BF16),
        )
        for i, value in enumerate(found):
            place = i * early + pair if pair < early else 3 * early + i
            grads_ref[:, place * 128 : (place + 1) * 128] = value

    grads = grads_ref[...]
    keep, send = dims(x_keep[...], grads, 0, 0), dims(x_send[...], grads, 0, 0)
    bias = jnp.sum(grads.astype(F32), axis=0, keepdims=True)

    @pl.when(step == 0)
    def _():
        keep_sum[...] = keep
        send_sum[...] = send
        bias_sum[...] = bias

    @pl.when(step > 0)
    def _():
        keep_sum[...] += keep
        send_sum[...] += send
        bias_sum[...] += bias

    @pl.when(step == pl.num_programs(0) - 1)
    def _():
        cols = 3 * early * 128
        bias_ref[...] = bias_sum[...]
        sides = [bias_sum[:, :cols]]
        if lone:
            sides.append(bias_sum[:, cols:])
        if before is not None:
            sides.append(before[...])
        rows = []
        for sums in sides:
            third = sums.shape[1] // 3
            for start in (0, 2 * third):
                for k in range(third // 128):
                    rows.append(sums[:, start + k * 128 : start + (k + 1) * 128])
        fill = jnp.zeros((keep_ref.shape[0] - len(rows), 128), F32)
        rows = jnp.concatenate(rows + [fill], axis=0).astype(BF16)
        for ref, value in ((keep_ref, keep_sum), (send_ref, send_sum)):
            ref[:, :cols] = value[:, :cols].astype(BF16)
            if len(sides) > 1:
                ref[:, cols : cols + 128] = rows
            if lone:
                ref[:, cols + 128 :] = value[:, cols:].astype(BF16)


def run_attend_backward(
    core, qkv, out, grad, labels, logsum, tokens, seq, first, count, before=None, lone=False
):
    rows = qkv.shape[0]
    pairs = qkv.shape[1] // (3 * 128)
    cols = 3 * 128 * count
    half = tokens.shape[1] // 2
    wide = cols + 128 if before is not None or lone else cols
    held_pairs, skip = (1, first) if count == 1 else (pairs, 0)
    part = lambda which: pl.BlockSpec(
        (seq, held_pairs * 128),
        lambda s, c: (s, (which * pairs + skip) // held_pairs),
    )
    weight = pltpu.HBM((half, wide), BF16)
    fixed = lambda shape: pl.BlockSpec(shape, lambda s, c: (0, 0))
    return pl.pallas_call(
        functools.partial(attend_backward, first - skip, count, lone),
        grid_spec=pltpu.PrefetchScalarGridSpec(
            num_scalar_prefetch=1,
            grid=(rows // seq,),
            in_specs=[
                part(0),
                part(1),
                part(2),
                part(0),
                part(0),
                pl.BlockSpec((1, seq, 1), lambda s, c: (s, 0, 0)),
                pl.BlockSpec((1, held_pairs, 2, seq), lambda s, c: (s, skip, 0, 0)),
                pl.BlockSpec((seq, half), lambda s, c: (s, c[0])),
                pl.BlockSpec((seq, half), lambda s, c: (s, 1 - c[0])),
            ]
            + ([] if before is None else [fixed(before.shape)]),
            out_specs=[
                pl.BlockSpec((seq, cols), lambda s, c: (s, 0)),
                fixed((half, wide)),
                fixed((half, wide)),
                fixed((1, cols)),
            ],
            scratch_shapes=[
                pltpu.VMEM((half, cols), F32),
                pltpu.VMEM((half, cols), F32),
                pltpu.VMEM((1, cols), F32),
            ],
        ),
        out_shape=[
            pltpu.HBM((rows, cols), BF16),
            weight,
            weight,
            jax.ShapeDtypeStruct((1, cols), F32),
        ],
        compiler_params=pltpu.CompilerParams(vmem_limit_bytes=26 << 20),
        cost_estimate=pl.CostEstimate(
            flops=rows * count * 2 * seq * 256 * 2 * 3, bytes_accessed=8 << 20, transcendentals=0
        ),
        name="attend_backward",
    )(
        core,
        *[far(qkv)] * 3,
        far(out),
        far(grad),
        labels,
        logsum,
        tokens,
        tokens,
        *([] if before is None else [before]),
    )


def gelu_pair(inner):
    phi = 0.5 + 0.5 * lax.erf(inner * 0.7071067811865476)
    bell = jnp.exp(-0.5 * (inner * inner))
    return inner * phi, phi + inner * (bell * 0.3989422804014327)


def norm_parts(values):
    centered = values - jnp.mean(values, axis=-1, keepdims=True)
    factor = lax.rsqrt(jnp.mean(centered * centered, axis=-1, keepdims=True) + NORM_EPS)
    return centered * factor, factor


def norm_back(grad_out, normed, factor, gain):
    scaled = grad_out * gain
    return factor * (
        scaled
        - jnp.mean(scaled, axis=-1, keepdims=True)
        - normed * jnp.mean(scaled * normed, axis=-1, keepdims=True)
    )


def feed_layer(seq, chunk, n_tok, n_hid, n_ctx, place_ref, count_ref, *refs):
    contexts, refs = refs[:n_ctx], refs[n_ctx:]
    tokens, cotangent, w_out_mine, w_out_other, w_up, w_down, vectors, b_up = refs[:8]
    y_ref, down, up, first_ref = refs[8], refs[9:13], refs[13:17], refs[17]
    grad_ctxs, (out_keep, out_send) = refs[18 : 18 + n_ctx], refs[18 + n_ctx : 20 + n_ctx]
    act, slope, normed, factor, hidden, mid, mid_low, total, sums, b_up_sum = refs[
        20 + n_ctx : 30 + n_ctx
    ]
    far_up, far_down = w_up, w_down
    w_up, w_down, w_out, up_sem, down_sem = refs[30 + n_ctx :]
    step = pl.program_id(0)
    block = tokens.shape[0]
    core, head = place_ref[0], place_ref[1]
    b_out, gain_one, shift_one, b_down, gain_two, shift_two = [
        vectors[i : i + 1] for i in range(6)
    ]

    def add(row, *values):
        for i, value in enumerate(values):
            sums[row + i : row + i + 1] += jnp.sum(value, axis=0, keepdims=True)

    @pl.when(step == 0)
    def _():
        pltpu.make_async_copy(far_up, w_up, up_sem).start()
        pltpu.make_async_copy(far_down, w_down, down_sem).start()
        w_out[: w_out_mine.shape[0]] = w_out_mine[...]
        w_out[w_out_mine.shape[0] :] = w_out_other[...]
        sums[...] = jnp.zeros_like(sums)
        total[...] = jnp.zeros_like(total)

    @pl.when(step < n_tok)
    def _():
        start = pl.multiple_of(step * block, block)
        here = pl.ds(start, block)
        context = jnp.concatenate([ctx[...] for ctx in contexts], axis=1)
        normed_one, factor_one = norm_parts(
            tokens[...].astype(F32) + matmul(context, w_out[...]) + b_out
        )
        normed[here] = normed_one
        factor[here] = jnp.broadcast_to(factor_one, (block, 128))
        hidden_here = normed_one * gain_one + shift_one
        hidden_low = hidden_here.astype(BF16)
        hidden[here] = hidden_low
        sum_two = hidden_here + b_down

        @pl.when(step == 0)
        def _():
            pltpu.make_async_copy(far_up, w_up, up_sem).wait()
            pltpu.make_async_copy(far_down, w_down, down_sem).wait()

        for j in range(w_up.shape[1] // chunk):
            cols = slice(j * chunk, (j + 1) * chunk)
            activated, gradient = gelu_pair(matmul(hidden_low, w_up[:, cols]) + b_up[:, cols])
            activated = activated.astype(BF16)
            act[here, cols] = activated
            slope[here, cols] = gradient.astype(BF16)
            sum_two = sum_two + matmul(activated, w_down[cols, :])
        normed_two, factor_two = norm_parts(sum_two)
        y_ref[...] = (normed_two * gain_two + shift_two).astype(BF16)
        place = start + lax.broadcasted_iota(jnp.int32, (block, 1), 0)
        live = (place % seq // (seq // MICRO) < count_ref[0]).astype(F32)
        grad_y = cotangent[...].astype(F32) * live
        grad_mid = norm_back(grad_y, normed_two, factor_two, gain_two)
        mid[here] = grad_mid
        mid_low[here] = grad_mid.astype(BF16)
        add(3, grad_y * normed_two, grad_y, grad_mid)

    @pl.when((step >= n_tok) & (step < n_tok + n_hid))
    def _():
        width = act.shape[1] // n_hid
        here = pl.ds(pl.multiple_of((step - n_tok) * width, width), width)

        def put(result, pieces):
            groups, group_rows, cols = pieces[0].shape
            result = result.reshape(groups, 2, group_rows, 2 * cols)
            for i in range(2):
                side = result[..., i * cols : (i + 1) * cols]
                pieces[i][...] = jnp.where(core == 0, side[:, 0], side[:, 1]).astype(BF16)
                pieces[2 + i][...] = jnp.where(core == 0, side[:, 1], side[:, 0]).astype(BF16)

        put(dims(act[:, here], mid_low[...], 0, 0), down)
        grad = dims(mid_low[...], w_down[here, :], 1, 1) * slope[:, here].astype(F32)
        grad = grad.astype(BF16)
        slope[:, here] = grad
        b_up_sum[:, here] = jnp.sum(grad.astype(F32), axis=0, keepdims=True)
        put(dims(grad, hidden[...], 0, 0), up)

    @pl.when(step >= n_tok + n_hid)
    def _():
        start = pl.multiple_of((step - n_tok - n_hid) * block, block)
        here = pl.ds(start, block)
        grad = mid[here] + dims(slope[here], w_up[...], 1, 1)
        normed_one = normed[here]
        grad_first = norm_back(grad, normed_one, factor[here, :1], gain_one)
        first_ref[...] = grad_first
        add(0, grad * normed_one, grad, grad_first)
        first_low = grad_first.astype(BF16)
        grad_ctx = dims(first_low, w_out[...], 1, 1).astype(BF16)
        start = 0
        for ref in grad_ctxs:
            ref[...] = grad_ctx[:, start : start + ref.shape[1]]
            start += ref.shape[1]
        context = jnp.concatenate([ctx[...] for ctx in contexts], axis=1)
        total[...] += dims(context, first_low, 0, 0)

    @pl.when(step == pl.num_programs(0) - 1)
    def _():
        lanes = [sums[i : i + 1] for i in range(6)] + [b_up_sum[...]]
        lanes = [
            row[:, k * 128 : (k + 1) * 128] for row in lanes for k in range(row.shape[1] // 128)
        ]
        n_side = len(lanes) // 2
        rows, d = out_keep.shape[1], total.shape[1]
        fill = jnp.zeros((rows - n_side, 128), F32)
        sides = [
            jnp.concatenate(part + [fill], axis=0) for part in (lanes[:n_side], lanes[n_side:])
        ]
        for i in range(2):
            side = jnp.where(head == i, sides[0], sides[1]).astype(BF16)
            for ref, which in ((out_keep, core), (out_send, 1 - core)):
                place = pl.multiple_of((2 * i + which) * rows, rows)
                ref[i, :, :d] = total[pl.ds(place, rows)].astype(BF16)
                ref[i, :, d:] = side


def run_feed_layer(
    seq,
    place,
    count,
    contexts,
    tokens,
    cotangent,
    w_out,
    w_up,
    w_down,
    vectors,
    b_up,
    rows_dev,
    block=256,
    width=768,
    chunk=1024,
):
    rows, d = tokens.shape
    ff = w_up.shape[1]
    group_rows = 2 * rows_dev
    groups = width // (2 * group_rows)
    n_tok, n_hid = rows // block, ff // width
    held = lambda shape: pl.BlockSpec(
        shape, lambda i, *_: (0,) * len(shape), pipeline_mode=pl.Buffered(1)
    )
    early = lambda cols: pl.BlockSpec(
        (block, cols), lambda i, *_: (jnp.minimum(i, n_tok - 1), 0)
    )
    late = lambda cols: pl.BlockSpec(
        (block, cols), lambda i, *_: (jnp.maximum(i - n_tok - n_hid, 0), 0)
    )
    twice = lambda cols: pl.BlockSpec(
        (block, cols),
        lambda i, *_: (jnp.where(i < n_tok, i, jnp.maximum(i - n_tok - n_hid, 0)), 0),
    )
    half_rows = lambda which: pl.BlockSpec(
        (d // 2, d), lambda i, place, _: (which(place), 0), pipeline_mode=pl.Buffered(1)
    )
    piece = pl.BlockSpec(
        (groups, group_rows, d // 2), lambda i, *_: (jnp.clip(i - n_tok, 0, n_hid - 1), 0, 0)
    )
    out = jax.ShapeDtypeStruct
    shape = (ff // (2 * group_rows), group_rows, d // 2)
    pieces = [pltpu.VMEM(shape, BF16)] * 4 + [pltpu.HBM(shape, BF16)] * 4
    widths = [ctx.shape[1] for ctx in contexts]
    out_half = (2, d // 4, d + 128)
    return pl.pallas_call(
        functools.partial(feed_layer, seq, chunk, n_tok, n_hid, len(contexts)),
        grid_spec=pltpu.PrefetchScalarGridSpec(
            num_scalar_prefetch=2,
            grid=(2 * n_tok + n_hid,),
            in_specs=[twice(w) for w in widths]
            + [early(d), early(d)]
            + [half_rows(lambda place: place[1]), half_rows(lambda place: 1 - place[1])]
            + [pl.BlockSpec(memory_space=pl.ANY)] * 2
            + [held(vectors.shape), held(b_up.shape)],
            out_specs=[early(d)]
            + [piece] * 8
            + [late(d)]
            + [late(w) for w in widths]
            + [held(out_half)] * 2,
            scratch_shapes=[
                pltpu.VMEM((rows, ff), BF16),
                pltpu.VMEM((rows, ff), BF16),
                pltpu.VMEM((rows, d), F32),
                pltpu.VMEM((rows, 128), F32),
                pltpu.VMEM((rows, d), BF16),
                pltpu.VMEM((rows, d), F32),
                pltpu.VMEM((rows, d), BF16),
                pltpu.VMEM((d, d), F32),
                pltpu.VMEM((8, d), F32),
                pltpu.VMEM((1, ff), F32),
                pltpu.VMEM(w_up.shape, BF16),
                pltpu.VMEM(w_down.shape, BF16),
                pltpu.VMEM(w_out.shape, BF16),
                pltpu.SemaphoreType.DMA,
                pltpu.SemaphoreType.DMA,
            ],
        ),
        out_shape=[out((rows, d), BF16)]
        + pieces
        + [pltpu.HBM((rows, d), F32)]
        + [pltpu.HBM((rows, w), BF16) for w in widths]
        + [pltpu.HBM(out_half, BF16)] * 2,
        compiler_params=pltpu.CompilerParams(vmem_limit_bytes=50 << 20),
        cost_estimate=pl.CostEstimate(
            flops=4 * rows * d * (3 * d + 6 * ff), bytes_accessed=60 << 20, transcendentals=0
        ),
        name="feed_layer",
    )(
        place,
        count,
        *[far(ctx) for ctx in contexts],
        tokens,
        cotangent,
        w_out,
        w_out,
        far(w_up),
        far(w_down),
        vectors,
        b_up,
    )


class Cube:
    def __init__(self, mesh):
        self.size = mesh.shape["dp"] * mesh.shape["head"]
        self.n_bits = self.size.bit_length() - 1
        self.upper = list(range(2, self.n_bits))
        self.index = lax.axis_index("dp") * mesh.shape["head"] + lax.axis_index("head")

    def bit(self, which):
        return (self.index >> which) & 1

    def swap(self, value, which):
        pairs = [(i, i ^ (1 << which)) for i in range(self.size)]
        return lax.ppermute(value, AXES, pairs)

    def half(self, value, axis, which, mine):
        bit = self.bit(which) if mine else 1 - self.bit(which)
        return lax.dynamic_index_in_dim(value, bit, axis, keepdims=False)

    def join(self, value, other, which):
        first = self.bit(which) == 0
        return jnp.concatenate(
            [jnp.where(first, value, other), jnp.where(first, other, value)], axis=0
        )


    def core_pieces(self, keep, send, rows_dev):
        others = yield [(part, 1) for part in send]
        shape = (2,) * (self.n_bits - 1) + (rows_dev, keep[0].shape[-1])
        return [[term.reshape(shape) for term in pair] for pair in zip(keep, others)]

    def pieces(self, terms, order, done=()):
        bits = [bit for bit in range(self.n_bits - 1, 1, -1) if bit not in done] + [0]
        for step in order:
            axis = bits.index(step)
            send, kept = [sum(self.half(term, axis, step, mine) for term in terms) for mine in (0, 1)]
            other, kept = yield [(send, step), (kept, None)]
            terms = [kept, other]
            bits.remove(step)
        return sum(terms)

    def last_pieces(self, values, order, bits):
        value = jnp.concatenate(values, axis=-1)
        bits = sorted(bits, reverse=True)
        for step in order:
            axis = bits.index(step)
            send, kept = [self.half(value, axis, step, mine) for mine in (0, 1)]
            other, kept = yield [(send, step), (kept, None)]
            value = kept + other
            bits.remove(step)
        return value

    def reduce_rows(self, value, order):
        halved = []
        for which in order:
            rows = value.shape[0]
            if rows % 32 == 0 and rows > 96:
                value = value.reshape(2, rows // 2, value.shape[1])
                (other,) = yield [(self.half(value, 0, which, False), which)]
                value = self.half(value, 0, which, True) + other
                halved.append(which)
            else:
                value = lax.optimization_barrier(value)
                (other,) = yield [(value, which)]
                value = value + other
        return value, halved

    def gather_rows(self, value, halved):
        for which in reversed(halved):
            (other,) = yield [(value, which)]
            value = self.join(value, other, which)
        return value

    def sum_out(self, keep, send):
        (other,) = yield [(send, 1)]
        value = keep + other
        (other,) = yield [(value[1], 0)]
        value, halved = yield from self.reduce_rows(value[0] + other, self.upper)
        value = yield from self.gather_rows(value, halved)
        (other,) = yield [(value, 0)]
        value = jnp.concatenate([value, other], axis=1)
        value = yield from self.gather_rows(value, [1])
        return value[:, : value.shape[1] // 2], value[:, value.shape[1] // 2 :]

    def core_rows(self, keep, send):
        (other,) = yield [(send, 1)]
        return keep + other

    def peer_rows(self, parts):
        value = jnp.concatenate(parts, axis=1)
        value = value.reshape(2, value.shape[0] // 2, value.shape[1])
        (other,) = yield [(self.half(value, 0, 2, False), 2)]
        value = self.half(value, 0, 2, True) + other
        (other,) = yield [(value, 0)]
        return other

    def own_rows(self, keep, send, peer):
        (other,) = yield [(send, 1)]
        value = keep + other
        value = value.reshape(2, value.shape[0] // 2, value.shape[1])
        (other,) = yield [(self.half(value, 0, 2, False), 2)]
        value = self.half(value, 0, 2, True) + other + peer.result
        value, halved = yield from self.reduce_rows(value, self.upper[1:])
        value = yield from self.gather_rows(value, [2] + halved)
        (other,) = yield [(value, 1)]
        return value, other


class Stream:
    def __init__(self, cube, steps):
        self.cube, self.steps, self.result = cube, steps, None
        self.wants = None
        self.advance(None)

    def advance(self, got):
        try:
            self.wants = self.steps.send(got)
        except StopIteration as stop:
            self.wants, self.result = None, stop.value

    def values(self):
        return tuple(value for value, _ in self.wants)

    def swaps(self):
        return tuple(
            value if which is None else self.cube.swap(value, which) for value, which in self.wants
        )


def tick(streams, work, *carry, wait=(), lazy=False):
    streams = [stream for stream in streams if stream.wants is not None]
    wait = [stream for stream in wait if stream.wants is not None and stream not in streams]
    moved = [list(stream.swaps()) for stream in streams]
    aside = []
    if lazy:
        for stream, got in zip(streams, moved):
            aside.append(
                {i: got[i] for i, (_, which) in enumerate(stream.wants) if which is None}
            )
            for i in aside[-1]:
                got[i] = ()
    later = [stream.values() for stream in wait]
    moved, work, carry, later = lax.optimization_barrier((moved, work, carry, later))
    for i, (stream, got) in enumerate(zip(streams, moved)):
        for place, value in (aside[i] if lazy else {}).items():
            got[place] = value
        stream.advance(got)
    for stream, values in zip(wait, later):
        stream.wants = [(value, which) for value, (_, which) in zip(values, stream.wants)]
    return (work, *carry)


def finish_own(pairs, core_ref, mine, other, w_query, w_key, w_value, bias):
    rows = mine.shape[0]
    early = (pairs - 1) * 128
    last = 3 * early + 128
    for value, which in ((mine, core_ref[0]), (other, 1 - core_ref[0])):
        here = pl.ds(pl.multiple_of(which * rows, rows), rows)
        for i, out in enumerate((w_query, w_key, w_value)):
            out[here, :early] = value[:, i * early : (i + 1) * early].astype(F32)
            out[here, early:] = value[:, last + i * 128 : last + (i + 1) * 128].astype(F32)
    bias[...] = mine[: bias.shape[0], 3 * early : last].astype(F32)


def run_finish_own(core, mine, other, pairs):
    rows = mine.shape[0]
    out = jax.ShapeDtypeStruct
    return pl.pallas_call(
        functools.partial(finish_own, pairs),
        grid_spec=pltpu.PrefetchScalarGridSpec(
            num_scalar_prefetch=1,
            grid=(1,),
            in_specs=[pl.BlockSpec(mine.shape, lambda i, c: (0, 0))] * 2,
            out_specs=[pl.BlockSpec((2 * rows, pairs * 128), lambda i, c: (0, 0))] * 3
            + [pl.BlockSpec((16, 128), lambda i, c: (0, 0))],
        ),
        out_shape=[out((2 * rows, pairs * 128), F32)] * 3 + [out((16, 128), F32)],
        compiler_params=pltpu.CompilerParams(vmem_limit_bytes=24 << 20),
        name="finish_own",
    )(core, mine, other)


def shards(
    mesh,
    tokens,
    labels,
    micro_counts,
    w_query,
    b_query,
    w_key,
    w_value,
    b_value,
    w_out,
    b_out,
    gain_one,
    shift_one,
    w_up,
    b_up,
    w_down,
    b_down,
    gain_two,
    shift_two,
    cotangent,
):
    cube = Cube(mesh)
    rows, width = tokens.shape
    seq = labels.shape[1]
    half = w_query.shape[1]
    pairs = half // 128
    ff = w_up.shape[1]
    head, core = cube.bit(0), cube.bit(1)
    place = jnp.stack([core, head])
    cores = core[None]

    part = run_pick_rows(cores, w_query, w_key, w_value)
    own_bias = jnp.concatenate([b_query, jnp.zeros_like(b_query), b_value])[None]
    n_seq = rows // seq
    marks = lax.dynamic_slice_in_dim(labels, head * n_seq, n_seq, 0)[:, :, None]
    own_w = w_query, w_key, w_value
    own_qkv, own_ctx, own_log = run_attend_forward(
        cores, tokens, own_w, own_bias, marks, seq, True
    )
    mine, peer_bias, own_ctx, own_w = lax.optimization_barrier(
        (cube.swap(part, 0), cube.swap(own_bias, 0), own_ctx, own_w)
    )
    other = cube.swap(mine, 1)
    peer_qkv, peer_ctx, peer_log = run_attend_forward(
        cores, tokens, (mine, other), peer_bias, marks, seq, False
    )
    vectors = jnp.stack(
        [b_out, gain_one, shift_one, b_down, gain_two, shift_two, b_down, b_down]
    )
    rows_dev = ff // cube.size
    (
        layer_output,
        *pieces,
        grad_first,
        own_grad_ctx,
        peer_grad_ctx,
        out_keep,
        out_send,
    ) = run_feed_layer(
        seq,
        place,
        micro_counts,
        (own_ctx, peer_ctx),
        tokens,
        cotangent,
        w_out,
        w_up,
        w_down,
        vectors,
        b_up[None],
        rows_dev,
    )

    stream = lambda steps: Stream(cube, steps)
    down = stream(cube.core_pieces(pieces[:2], pieces[2:4], rows_dev))
    up = stream(cube.core_pieces(pieces[4:6], pieces[6:], rows_dev))
    out = stream(cube.sum_out(out_keep, out_send))


    def backward(qkv, ctx, grad_ctx, logsum, first, count, before=None, lone=False):
        return tuple(
            run_attend_backward(
                cores, qkv, ctx, grad_ctx, marks, logsum, tokens, seq, first, count, before, lone
            )
        )

    def side_by_side(first, count, weights):
        cols = slice(first * 128, (first + count) * 128)
        return jnp.concatenate([weight[:, cols] for weight in weights], axis=1)

    def finish_out(mine, other):
        first = head == 0
        both = jnp.concatenate(
            [jnp.where(first, mine, other), jnp.where(first, other, mine)], axis=0
        ).astype(F32)
        side = (ff + 6 * width) // 256
        small = jnp.concatenate([both[:side, width:], both[half : half + side, width:]], axis=0)
        return both[:, :width], small.reshape(-1, width)

    far_bits = cube.upper[1:]
    found = backward(peer_qkv, peer_ctx, peer_grad_ctx, peer_log, pairs - 1, 1)
    (grads_b, keep_b, send_b, sums_b), peer_grad_ctx = tick(
        [down, out], found, peer_grad_ctx, wait=[up]
    )
    down_a = stream(cube.pieces(down.result[0], [0, 2]))
    down_b = stream(cube.pieces(down.result[1], [2, 0]))
    core_b = stream(cube.core_rows(keep_b, send_b))
    found = backward(peer_qkv, peer_ctx, peer_grad_ctx, peer_log, 0, pairs - 1, sums_b)
    (grads_a, keep_a, send_a, _), own_grad_ctx = tick(
        [core_b, up, out], found, own_grad_ctx, lazy=True
    )
    up_a = stream(cube.pieces(up.result[0], [3]))
    up_b = stream(cube.pieces(up.result[1], [3]))
    core_a = stream(cube.core_rows(keep_a, send_a))
    found = backward(own_qkv, own_ctx, own_grad_ctx, own_log, 0, pairs, None, True)
    (own_grads, keep, send, _), grads_a, grads_b, grad_first, parts = tick(
        [core_a, down_a, down_b, up_a, out],
        found,
        grads_a,
        grads_b,
        grad_first,
        (mine, other),
        wait=[up_b],
        lazy=True,
    )
    peer_w = [cube.join(*parts, 1)[:, i * half : (i + 1) * half] for i in range(3)]
    peer = stream(cube.peer_rows([core_a.result, core_b.result]))
    own = stream(cube.own_rows(keep, send, peer))
    grad_tokens = grad_first + dims(grads_a, side_by_side(0, pairs - 1, peer_w), 1, 1)
    grad_tokens = grad_tokens + dims(grads_b, side_by_side(pairs - 1, 1, peer_w), 1, 1)
    grad_tokens, own_grads, own_w = tick(
        [own, down_b, out, peer], grad_tokens, own_grads, own_w, wait=[down_a]
    )
    early = 3 * (half - 128)
    grad_tokens = grad_tokens + dims(own_grads[:, :early], side_by_side(0, pairs - 1, own_w), 1, 1)
    grad_tokens = grad_tokens + dims(own_grads[:, early:], side_by_side(pairs - 1, 1, own_w), 1, 1)
    (grad_tokens,) = tick([peer, own, out, up_b], grad_tokens, wait=[down_a])
    up_both = jnp.concatenate([up_a.result, up_b.result], axis=-1)
    up = stream(cube.pieces([up_both], [0, 2], far_bits[:1]))
    tick([own, down_a], (), wait=[out])
    down_far = stream(cube.last_pieces([down_a.result, down_b.result], far_bits[:1], far_bits))
    tick([own, out, up, down_far], ())
    tick([own, up, out], (), wait=[down_far])
    while out.wants is not None:
        tick([out], ())
    grad_w_out, small = finish_out(*out.result)
    values = [down_far.result, up.result]
    far = stream(cube.last_pieces(values, far_bits[1:], far_bits[1:]))
    ((grad_w_out, small),) = tick([own, far], (grad_w_out, small))
    streams = [own, far]
    while any(stream.wants is not None for stream in streams):
        tick(streams, ())
    grad_w_down, grad_w_up = far.result[:, :width].astype(F32), far.result[:, width:]

    grad_w_query, grad_w_key, grad_w_value, bias = run_finish_own(cores, *own.result, pairs)
    last = 2 * (pairs - 1)
    bias = [
        jnp.concatenate([bias[i * (pairs - 1) : (i + 1) * (pairs - 1)], bias[last + i : last + i + 1]])
        for i in range(2)
    ]
    return (
        layer_output,
        grad_tokens,
        grad_w_query,
        bias[0].reshape(half),
        grad_w_key,
        grad_w_value,
        bias[1].reshape(half),
        grad_w_out,
        small[2],
        small[0],
        small[1],
        grad_w_up.astype(F32).T,
        small[6:].reshape(ff),
        grad_w_down,
        small[5],
        small[3],
        small[4],
    )


def solution(mesh):
    rows = P(("dp", "head"), None)
    placed = (rows, P("dp", None), P("dp"), P(None, "head"), P("head"), P(None, "head"))
    placed += (P(None, "head"), P("head")) + (P(),) * 10 + (rows,)
    columns = P(None, "head")
    out_specs = (rows, rows, columns, P("head"), columns, columns, P("head"))
    out_specs += (P(),) * 4 + (P(None, ("dp", "head")), P(), rows, P(), P(), P())
    return jax.shard_map(
        functools.partial(shards, mesh),
        mesh=mesh,
        in_specs=placed,
        out_specs=out_specs,
        check_vma=False,
    )
```

```python
import functools

import jax
import jax.numpy as jnp
from jax import lax
from jax.experimental import pallas as pl
from jax.experimental.pallas import tpu as pltpu
from jax.sharding import PartitionSpec as P

HEAD_DIM = 64
MICRO = 4
F32 = jnp.float32
BF16 = jnp.bfloat16
NORM_EPS = 1e-05
MASK = 2.0**30
AXES = ("dp", "head")


def dims(left, right, left_dim, right_dim):
    return lax.dot_general(
        left, right, (((left_dim,), (right_dim,)), ((), ())), preferred_element_type=F32
    )


def matmul(left, right):
    return jnp.dot(left, right, preferred_element_type=F32)


def far(value):
    return pltpu.with_memory_space_constraint(value, pltpu.HBM)


def query_marks(labels, shape):
    lane = lax.broadcasted_iota(jnp.int32, shape, 1)
    return jnp.where((lane & 63) == labels, 1.0, 0.0).astype(BF16)


def key_marks(labels, shape):
    lane = lax.broadcasted_iota(jnp.int32, shape, 1) & 63
    return jnp.where((lane < 4) & (lane != labels), -MASK, 0.0).astype(BF16)


def pick_rows(core_ref, w_query, w_key, w_value, out):
    half = w_query.shape[1]
    for i, weight in enumerate((w_query, w_key, w_value)):
        out[:, i * half : (i + 1) * half] = weight[...]


def run_pick_rows(core, w_query, w_key, w_value):
    width, half = w_query.shape
    rows = pl.BlockSpec((width // 2, half), lambda i, c: (c[0], 0))
    return pl.pallas_call(
        pick_rows,
        grid_spec=pltpu.PrefetchScalarGridSpec(
            num_scalar_prefetch=1,
            grid=(1,),
            in_specs=[rows] * 3,
            out_specs=pl.BlockSpec((width // 2, 3 * half), lambda i, c: (0, 0)),
        ),
        out_shape=jax.ShapeDtypeStruct((width // 2, 3 * half), BF16),
        name="pick_rows",
    )(core, far(w_query), far(w_key), far(w_value))


def attend_pairs(lab_ref, qkv_ref, out_ref, log_ref):
    labels = lab_ref[0]
    shape = (labels.shape[0], 128)
    half = out_ref.shape[1]
    low = lax.broadcasted_iota(jnp.int32, shape, 1) < HEAD_DIM
    q_extra, k_extra = query_marks(labels, shape), key_marks(labels, shape)
    for pair in range(half // 128):
        q, k, v = [
            qkv_ref[:, i * half + pair * 128 : i * half + (pair + 1) * 128] for i in range(3)
        ]
        q = q * jnp.asarray(0.125, BF16)
        outs = []
        for t in range(2):
            mine = low if t == 0 else jnp.logical_not(low)
            scores = dims(jnp.where(mine, k, k_extra), jnp.where(mine, q, q_extra), 1, 1)
            largest = jnp.max(scores, axis=0, keepdims=True)
            soft = jnp.exp(scores - largest)
            total = jnp.sum(soft, axis=0, keepdims=True)
            out = dims(v, soft.astype(BF16), 0, 0)
            outs.append(out[t * HEAD_DIM : (t + 1) * HEAD_DIM] * (1.0 / total))
            log_ref[0, pair, t : t + 1] = largest + jnp.log(total)
        out_ref[:, pair * 128 : (pair + 1) * 128] = jnp.concatenate(outs, axis=0).T.astype(BF16)


def attend_own(core_ref, x, w_query, w_key, w_value, bias, lab_ref, *outs):
    qkv_ref = outs[0]
    width = w_query.shape[1]
    for i, weight in enumerate((w_query, w_key, w_value)):
        cols = slice(i * width, (i + 1) * width)
        value = matmul(x[...], weight[...]) + bias[:, cols].astype(F32)
        qkv_ref[:, cols] = value.astype(BF16)
    attend_pairs(lab_ref, *outs)


def attend_peer(core_ref, x_mine, x_other, w_mine, w_other, bias, lab_ref, *outs):
    qkv_ref = outs[0]
    width = qkv_ref.shape[1] // 3
    for i in range(3):
        cols = slice(i * width, (i + 1) * width)
        value = matmul(x_mine[...], w_mine[:, cols]) + matmul(x_other[...], w_other[:, cols])
        qkv_ref[:, cols] = (value + bias[:, cols].astype(F32)).astype(BF16)
    attend_pairs(lab_ref, *outs)


def run_attend_forward(core, tokens, weights, bias, labels, seq, own):
    rows, depth = tokens.shape
    cols = bias.shape[1]
    pairs = cols // (3 * 128)
    if own:
        xs = [pl.BlockSpec((seq, depth), lambda s, c: (s, 0))]
    else:
        xs = [
            pl.BlockSpec((seq, depth // 2), lambda s, c: (s, c[0])),
            pl.BlockSpec((seq, depth // 2), lambda s, c: (s, 1 - c[0])),
        ]
    fixed = [
        pl.BlockSpec(weight.shape, lambda s, c: (0, 0), pipeline_mode=pl.Buffered(1))
        for weight in (*weights, bias)
    ]
    return pl.pallas_call(
        attend_own if own else attend_peer,
        grid_spec=pltpu.PrefetchScalarGridSpec(
            num_scalar_prefetch=1,
            grid=(rows // seq,),
            in_specs=xs + fixed + [pl.BlockSpec((1, seq, 1), lambda s, c: (s, 0, 0))],
            out_specs=[
                pl.BlockSpec((seq, cols), lambda s, c: (s, 0)),
                pl.BlockSpec((seq, cols // 3), lambda s, c: (s, 0)),
                pl.BlockSpec((1, pairs, 2, seq), lambda s, c: (s, 0, 0, 0)),
            ],
        ),
        out_shape=[
            pltpu.HBM((rows, cols), BF16),
            pltpu.HBM((rows, cols // 3), BF16),
            jax.ShapeDtypeStruct((rows // seq, pairs, 2, seq), F32),
        ],
        compiler_params=pltpu.CompilerParams(vmem_limit_bytes=24 << 20),
        cost_estimate=pl.CostEstimate(
            flops=rows * pairs * 2 * seq * 256 * 2 * 3, bytes_accessed=8 << 20, transcendentals=0
        ),
        name="attend_forward",
    )(core, *[tokens] * len(xs), *weights, bias, labels)


def attend_backward(
    first,
    count,
    lone,
    core_ref,
    q_ref,
    k_ref,
    v_ref,
    out_ref,
    grad_ref,
    lab_ref,
    log_ref,
    x_keep,
    x_send,
    *refs,
):
    grads_ref, keep_ref, send_ref, bias_ref, keep_sum, send_sum, bias_sum = refs
    early = count - 1 if lone else count
    step = pl.program_id(0)
    labels = lab_ref[0]
    shape = (labels.shape[0], 128)
    low = lax.broadcasted_iota(jnp.int32, shape, 1) < HEAD_DIM
    q_extra, k_extra = query_marks(labels, shape), key_marks(labels, shape)
    for pair in range(count):
        cols = slice((first + pair) * 128, (first + pair + 1) * 128)
        q = q_ref[:, cols] * jnp.asarray(0.125, BF16)
        k, v, grad = k_ref[:, cols], v_ref[:, cols], grad_ref[:, cols]
        zero = jnp.zeros_like(q)
        inner = (grad.astype(F32) * out_ref[:, cols].astype(F32)).T
        dqs, dks, dvs = [], [], []
        for t in range(2):
            mine = low if t == 0 else jnp.logical_not(low)
            half = slice(t * HEAD_DIM, (t + 1) * HEAD_DIM)
            scores = dims(jnp.where(mine, k, k_extra), jnp.where(mine, q, q_extra), 1, 1)
            soft = jnp.exp(scores - log_ref[0, first + pair, t : t + 1])
            grad_soft = dims(v, jnp.where(mine, grad, zero), 1, 1)
            row_inner = jnp.sum(inner[half], axis=0, keepdims=True)
            grad_scores = (soft * (grad_soft - row_inner)).astype(BF16)
            dvs.append(dims(soft.astype(BF16), grad, 1, 0))
            dks.append(dims(grad_scores, q, 1, 0))
            dqs.append(dims(k, grad_scores, 0, 0)[half])
        found = (
            (jnp.concatenate(dqs, axis=0).T * 0.125).astype(BF16),
            jnp.where(low, dks[0], dks[1]).astype(BF16),
            jnp.where(low, dvs[0], dvs[1]).astype(BF16),
        )
        for i, value in enumerate(found):
            place = i * early + pair if pair < early else 3 * early + i
            grads_ref[:, place * 128 : (place + 1) * 128] = value

    grads = grads_ref[...]
    keep, send = dims(x_keep[...], grads, 0, 0), dims(x_send[...], grads, 0, 0)
    bias = jnp.sum(grads.astype(F32), axis=0, keepdims=True)

    @pl.when(step == 0)
    def _():
        keep_sum[...] = keep
        send_sum[...] = send
        bias_sum[...] = bias

    @pl.when(step > 0)
    def _():
        keep_sum[...] += keep
        send_sum[...] += send
        bias_sum[...] += bias

    @pl.when(step == pl.num_programs(0) - 1)
    def _():
        bias_ref[...] = bias_sum[...]
        keep_ref[...] = keep_sum[...].astype(BF16)
        send_ref[...] = send_sum[...].astype(BF16)


def run_attend_backward(
    core, qkv, out, grad, labels, logsum, tokens, seq, first, count, lone=False
):
    rows = qkv.shape[0]
    pairs = qkv.shape[1] // (3 * 128)
    cols = 3 * 128 * count
    half = tokens.shape[1] // 2
    held_pairs, skip = (1, first) if count == 1 else (pairs, 0)
    part = lambda which: pl.BlockSpec(
        (seq, held_pairs * 128),
        lambda s, c: (s, (which * pairs + skip) // held_pairs),
    )
    weight = (jax.ShapeDtypeStruct if lone else pltpu.HBM)((half, cols), BF16)
    fixed = lambda shape: pl.BlockSpec(shape, lambda s, c: (0, 0))
    return pl.pallas_call(
        functools.partial(attend_backward, first - skip, count, lone),
        grid_spec=pltpu.PrefetchScalarGridSpec(
            num_scalar_prefetch=1,
            grid=(rows // seq,),
            in_specs=[
                part(0),
                part(1),
                part(2),
                part(0),
                part(0),
                pl.BlockSpec((1, seq, 1), lambda s, c: (s, 0, 0)),
                pl.BlockSpec((1, held_pairs, 2, seq), lambda s, c: (s, skip, 0, 0)),
                pl.BlockSpec((seq, half), lambda s, c: (s, c[0])),
                pl.BlockSpec((seq, half), lambda s, c: (s, 1 - c[0])),
            ],
            out_specs=[
                pl.BlockSpec((seq, cols), lambda s, c: (s, 0)),
                fixed((half, cols)),
                fixed((half, cols)),
                fixed((1, cols)),
            ],
            scratch_shapes=[
                pltpu.VMEM((half, cols), F32),
                pltpu.VMEM((half, cols), F32),
                pltpu.VMEM((1, cols), F32),
            ],
        ),
        out_shape=[
            pltpu.HBM((rows, cols), BF16),
            weight,
            weight,
            jax.ShapeDtypeStruct((1, cols), F32),
        ],
        compiler_params=pltpu.CompilerParams(vmem_limit_bytes=26 << 20),
        cost_estimate=pl.CostEstimate(
            flops=rows * count * 2 * seq * 256 * 2 * 3, bytes_accessed=8 << 20, transcendentals=0
        ),
        name="attend_backward",
    )(
        core,
        *[far(qkv)] * 3,
        far(out),
        far(grad),
        labels,
        logsum,
        tokens,
        tokens,
    )


def gelu_pair(inner):
    phi = 0.5 + 0.5 * lax.erf(inner * 0.7071067811865476)
    bell = jnp.exp(-0.5 * (inner * inner))
    return inner * phi, phi + inner * (bell * 0.3989422804014327)


def norm_parts(values):
    centered = values - jnp.mean(values, axis=-1, keepdims=True)
    factor = lax.rsqrt(jnp.mean(centered * centered, axis=-1, keepdims=True) + NORM_EPS)
    return centered * factor, factor


def norm_back(grad_out, normed, factor, gain):
    scaled = grad_out * gain
    return factor * (
        scaled
        - jnp.mean(scaled, axis=-1, keepdims=True)
        - normed * jnp.mean(scaled * normed, axis=-1, keepdims=True)
    )


def feed_layer(seq, chunk, n_tok, n_hid, n_ctx, place_ref, count_ref, *refs):
    contexts, refs = refs[:n_ctx], refs[n_ctx:]
    tokens, cotangent, w_out_mine, w_out_other, w_up, w_down, vectors, b_up = refs[:8]
    y_ref, down, up, first_ref = refs[8], refs[9:13], refs[13:17], refs[17]
    grad_ctxs, (out_keep, out_send) = refs[18 : 18 + n_ctx], refs[18 + n_ctx : 20 + n_ctx]
    act, slope, normed, factor, hidden, mid, mid_low, total, sums, b_up_sum = refs[
        20 + n_ctx : 30 + n_ctx
    ]
    far_up, far_down = w_up, w_down
    w_up, w_down, w_out, up_sem, down_sem = refs[30 + n_ctx :]
    step = pl.program_id(0)
    block = tokens.shape[0]
    core, head = place_ref[0], place_ref[1]
    b_out, gain_one, shift_one, b_down, gain_two, shift_two = [
        vectors[i : i + 1] for i in range(6)
    ]

    def add(row, *values):
        for i, value in enumerate(values):
            sums[row + i : row + i + 1] += jnp.sum(value, axis=0, keepdims=True)

    @pl.when(step == 0)
    def _():
        pltpu.make_async_copy(far_up, w_up, up_sem).start()
        pltpu.make_async_copy(far_down, w_down, down_sem).start()
        w_out[: w_out_mine.shape[0]] = w_out_mine[...]
        w_out[w_out_mine.shape[0] :] = w_out_other[...]
        sums[...] = jnp.zeros_like(sums)
        total[...] = jnp.zeros_like(total)

    @pl.when(step < n_tok)
    def _():
        start = pl.multiple_of(step * block, block)
        here = pl.ds(start, block)
        context = jnp.concatenate([ctx[...] for ctx in contexts], axis=1)
        normed_one, factor_one = norm_parts(
            tokens[...].astype(F32) + matmul(context, w_out[...]) + b_out
        )
        normed[here] = normed_one
        factor[here] = jnp.broadcast_to(factor_one, (block, 128))
        hidden_here = normed_one * gain_one + shift_one
        hidden_low = hidden_here.astype(BF16)
        hidden[here] = hidden_low
        sum_two = hidden_here + b_down

        @pl.when(step == 0)
        def _():
            pltpu.make_async_copy(far_up, w_up, up_sem).wait()
            pltpu.make_async_copy(far_down, w_down, down_sem).wait()

        for j in range(w_up.shape[1] // chunk):
            cols = slice(j * chunk, (j + 1) * chunk)
            activated, gradient = gelu_pair(matmul(hidden_low, w_up[:, cols]) + b_up[:, cols])
            activated = activated.astype(BF16)
            act[here, cols] = activated
            slope[here, cols] = gradient.astype(BF16)
            sum_two = sum_two + matmul(activated, w_down[cols, :])
        normed_two, factor_two = norm_parts(sum_two)
        y_ref[...] = (normed_two * gain_two + shift_two).astype(BF16)
        place = start + lax.broadcasted_iota(jnp.int32, (block, 1), 0)
        live = (place % seq // (seq // MICRO) < count_ref[0]).astype(F32)
        grad_y = cotangent[...].astype(F32) * live
        grad_mid = norm_back(grad_y, normed_two, factor_two, gain_two)
        mid[here] = grad_mid
        mid_low[here] = grad_mid.astype(BF16)
        add(3, grad_y * normed_two, grad_y, grad_mid)

    @pl.when((step >= n_tok) & (step < n_tok + n_hid))
    def _():
        width = act.shape[1] // n_hid
        here = pl.ds(pl.multiple_of((step - n_tok) * width, width), width)

        def put(result, pieces):
            groups, group_rows, cols = pieces[0].shape
            result = result.reshape(groups, 2, group_rows, 2 * cols)
            for i in range(2):
                side = result[..., i * cols : (i + 1) * cols]
                pieces[i][...] = jnp.where(core == 0, side[:, 0], side[:, 1]).astype(BF16)
                pieces[2 + i][...] = jnp.where(core == 0, side[:, 1], side[:, 0]).astype(BF16)

        put(dims(act[:, here], mid_low[...], 0, 0), down)
        grad = dims(mid_low[...], w_down[here, :], 1, 1) * slope[:, here].astype(F32)
        grad = grad.astype(BF16)
        slope[:, here] = grad
        b_up_sum[:, here] = jnp.sum(grad.astype(F32), axis=0, keepdims=True)
        put(dims(grad, hidden[...], 0, 0), up)

    @pl.when(step >= n_tok + n_hid)
    def _():
        start = pl.multiple_of((step - n_tok - n_hid) * block, block)
        here = pl.ds(start, block)
        grad = mid[here] + dims(slope[here], w_up[...], 1, 1)
        normed_one = normed[here]
        grad_first = norm_back(grad, normed_one, factor[here, :1], gain_one)
        first_ref[...] = grad_first
        add(0, grad * normed_one, grad, grad_first)
        first_low = grad_first.astype(BF16)
        grad_ctx = dims(first_low, w_out[...], 1, 1).astype(BF16)
        start = 0
        for ref in grad_ctxs:
            ref[...] = grad_ctx[:, start : start + ref.shape[1]]
            start += ref.shape[1]
        context = jnp.concatenate([ctx[...] for ctx in contexts], axis=1)
        total[...] += dims(context, first_low, 0, 0)

    @pl.when(step == pl.num_programs(0) - 1)
    def _():
        lanes = [sums[i : i + 1] for i in range(6)] + [b_up_sum[...]]
        lanes = [
            row[:, k * 128 : (k + 1) * 128] for row in lanes for k in range(row.shape[1] // 128)
        ]
        n_side = len(lanes) // 2
        rows, d = out_keep.shape[1], total.shape[1]
        fill = jnp.zeros((rows - n_side, 128), F32)
        sides = [
            jnp.concatenate(part + [fill], axis=0) for part in (lanes[:n_side], lanes[n_side:])
        ]
        for i in range(2):
            side = jnp.where(head == i, sides[0], sides[1]).astype(BF16)
            for ref, which in ((out_keep, core), (out_send, 1 - core)):
                place = pl.multiple_of((2 * i + which) * rows, rows)
                ref[i, :, :d] = total[pl.ds(place, rows)].astype(BF16)
                ref[i, :, d:] = side


def run_feed_layer(
    seq,
    place,
    count,
    contexts,
    tokens,
    cotangent,
    w_out,
    w_up,
    w_down,
    vectors,
    b_up,
    rows_dev,
    block=256,
    width=768,
    chunk=1024,
):
    rows, d = tokens.shape
    ff = w_up.shape[1]
    group_rows = 2 * rows_dev
    groups = width // (2 * group_rows)
    n_tok, n_hid = rows // block, ff // width
    held = lambda shape: pl.BlockSpec(
        shape, lambda i, *_: (0,) * len(shape), pipeline_mode=pl.Buffered(1)
    )
    early = lambda cols: pl.BlockSpec(
        (block, cols), lambda i, *_: (jnp.minimum(i, n_tok - 1), 0)
    )
    late = lambda cols: pl.BlockSpec(
        (block, cols), lambda i, *_: (jnp.maximum(i - n_tok - n_hid, 0), 0)
    )
    twice = lambda cols: pl.BlockSpec(
        (block, cols),
        lambda i, *_: (jnp.where(i < n_tok, i, jnp.maximum(i - n_tok - n_hid, 0)), 0),
    )
    half_rows = lambda which: pl.BlockSpec(
        (d // 2, d), lambda i, place, _: (which(place), 0), pipeline_mode=pl.Buffered(1)
    )
    piece = pl.BlockSpec(
        (groups, group_rows, d // 2), lambda i, *_: (jnp.clip(i - n_tok, 0, n_hid - 1), 0, 0)
    )
    out = jax.ShapeDtypeStruct
    shape = (ff // (2 * group_rows), group_rows, d // 2)
    pieces = [pltpu.VMEM(shape, BF16)] * 4 + [pltpu.HBM(shape, BF16)] * 4
    widths = [ctx.shape[1] for ctx in contexts]
    out_half = (2, d // 4, d + 128)
    return pl.pallas_call(
        functools.partial(feed_layer, seq, chunk, n_tok, n_hid, len(contexts)),
        grid_spec=pltpu.PrefetchScalarGridSpec(
            num_scalar_prefetch=2,
            grid=(2 * n_tok + n_hid,),
            in_specs=[twice(w) for w in widths]
            + [early(d), early(d)]
            + [half_rows(lambda place: place[1]), half_rows(lambda place: 1 - place[1])]
            + [pl.BlockSpec(memory_space=pl.ANY)] * 2
            + [held(vectors.shape), held(b_up.shape)],
            out_specs=[early(d)]
            + [piece] * 8
            + [late(d)]
            + [late(w) for w in widths]
            + [held(out_half)] * 2,
            scratch_shapes=[
                pltpu.VMEM((rows, ff), BF16),
                pltpu.VMEM((rows, ff), BF16),
                pltpu.VMEM((rows, d), F32),
                pltpu.VMEM((rows, 128), F32),
                pltpu.VMEM((rows, d), BF16),
                pltpu.VMEM((rows, d), F32),
                pltpu.VMEM((rows, d), BF16),
                pltpu.VMEM((d, d), F32),
                pltpu.VMEM((8, d), F32),
                pltpu.VMEM((1, ff), F32),
                pltpu.VMEM(w_up.shape, BF16),
                pltpu.VMEM(w_down.shape, BF16),
                pltpu.VMEM(w_out.shape, BF16),
                pltpu.SemaphoreType.DMA,
                pltpu.SemaphoreType.DMA,
            ],
        ),
        out_shape=[out((rows, d), BF16)]
        + pieces
        + [pltpu.HBM((rows, d), F32)]
        + [pltpu.HBM((rows, w), BF16) for w in widths]
        + [pltpu.HBM(out_half, BF16)] * 2,
        compiler_params=pltpu.CompilerParams(vmem_limit_bytes=50 << 20),
        cost_estimate=pl.CostEstimate(
            flops=4 * rows * d * (3 * d + 6 * ff), bytes_accessed=60 << 20, transcendentals=0
        ),
        name="feed_layer",
    )(
        place,
        count,
        *[far(ctx) for ctx in contexts],
        tokens,
        cotangent,
        w_out,
        w_out,
        far(w_up),
        far(w_down),
        vectors,
        b_up,
    )


class Cube:
    def __init__(self, mesh):
        self.size = mesh.shape["dp"] * mesh.shape["head"]
        self.n_bits = self.size.bit_length() - 1
        self.upper = list(range(2, self.n_bits))
        self.index = lax.axis_index("dp") * mesh.shape["head"] + lax.axis_index("head")

    def bit(self, which):
        return (self.index >> which) & 1

    def swap(self, value, which):
        pairs = [(i, i ^ (1 << which)) for i in range(self.size)]
        return lax.ppermute(value, AXES, pairs)

    def half(self, value, axis, which, mine):
        bit = self.bit(which) if mine else 1 - self.bit(which)
        return lax.dynamic_index_in_dim(value, bit, axis, keepdims=False)

    def join(self, value, other, which):
        first = self.bit(which) == 0
        return jnp.concatenate(
            [jnp.where(first, value, other), jnp.where(first, other, value)], axis=0
        )


    def core_pieces(self, keep, send, rows_dev):
        others = yield [(part, 1) for part in send]
        shape = (2,) * (self.n_bits - 1) + (rows_dev, keep[0].shape[-1])
        return [[term.reshape(shape) for term in pair] for pair in zip(keep, others)]

    def pieces(self, terms, order, done=()):
        bits = [bit for bit in range(self.n_bits - 1, 1, -1) if bit not in done] + [0]
        for step in order:
            axis = bits.index(step)
            send, kept = [sum(self.half(term, axis, step, mine) for term in terms) for mine in (0, 1)]
            other, kept = yield [(send, step), (kept, None)]
            terms = [kept, other]
            bits.remove(step)
        return sum(terms)

    def last_pieces(self, values, order, bits):
        value = jnp.concatenate(values, axis=-1)
        bits = sorted(bits, reverse=True)
        for step in order:
            axis = bits.index(step)
            send, kept = [self.half(value, axis, step, mine) for mine in (0, 1)]
            other, kept = yield [(send, step), (kept, None)]
            value = kept + other
            bits.remove(step)
        return value

    def reduce_rows(self, value, order):
        halved = []
        for which in order:
            rows = value.shape[0]
            if rows % 32 == 0 and rows > 96:
                value = value.reshape(2, rows // 2, value.shape[1])
                (other,) = yield [(self.half(value, 0, which, False), which)]
                value = self.half(value, 0, which, True) + other
                halved.append(which)
            else:
                value = lax.optimization_barrier(value)
                (other,) = yield [(value, which)]
                value = value + other
        return value, halved

    def gather_rows(self, value, halved):
        for which in reversed(halved):
            (other,) = yield [(value, which)]
            value = self.join(value, other, which)
        return value

    def sum_out(self, keep, send):
        (other,) = yield [(send, 1)]
        (other_two,) = yield [(keep[1] + other[1], 0)]
        value, halved = yield from self.reduce_rows(keep[0] + other[0] + other_two, self.upper)
        value = yield from self.gather_rows(value, halved)
        (other,) = yield [(value, 0)]
        value = jnp.concatenate([value, other], axis=1)
        value = yield from self.gather_rows(value, [1])
        return value[:, : value.shape[1] // 2], value[:, value.shape[1] // 2 :]

    def core_rows(self, keep, send):
        (other,) = yield [(send, 1)]
        return keep + other

    def sum_bias(self, own, peer):
        (other,) = yield [(peer, 0)]
        value = own + other
        for which in [1] + self.upper:
            (other,) = yield [(value, which)]
            value = value + other
        return value

    def peer_rows(self, parts):
        value = jnp.concatenate(parts, axis=1)
        value = value.reshape(2, value.shape[0] // 2, value.shape[1])
        (other,) = yield [(self.half(value, 0, 2, False), 2)]
        value = self.half(value, 0, 2, True) + other
        (other,) = yield [(value, 0)]
        return other

    def own_rows(self, keep, send, peer):
        (other,) = yield [(send, 1)]
        value = keep + other
        value = value.reshape(2, value.shape[0] // 2, value.shape[1])
        (other,) = yield [(self.half(value, 0, 2, False), 2)]
        value = self.half(value, 0, 2, True) + other + peer.result
        value, halved = yield from self.reduce_rows(value, self.upper[1:])
        value = yield from self.gather_rows(value, [2] + halved)
        (other,) = yield [(value, 1)]
        return value, other


class Stream:
    def __init__(self, cube, steps):
        self.cube, self.steps, self.result = cube, steps, None
        self.wants = None
        self.advance(None)

    def advance(self, got):
        try:
            self.wants = self.steps.send(got)
        except StopIteration as stop:
            self.wants, self.result = None, stop.value

    def values(self):
        return tuple(value for value, _ in self.wants)

    def swaps(self):
        return tuple(
            value if which is None else self.cube.swap(value, which) for value, which in self.wants
        )


def tick(streams, work, *carry, wait=(), lazy=False):
    streams = [stream for stream in streams if stream.wants is not None]
    wait = [stream for stream in wait if stream.wants is not None and stream not in streams]
    moved = [list(stream.swaps()) for stream in streams]
    aside = []
    if lazy:
        for stream, got in zip(streams, moved):
            aside.append(
                {i: got[i] for i, (_, which) in enumerate(stream.wants) if which is None}
            )
            for i in aside[-1]:
                got[i] = ()
    later = [stream.values() for stream in wait]
    moved, work, carry, later = lax.optimization_barrier((moved, work, carry, later))
    for i, (stream, got) in enumerate(zip(streams, moved)):
        for place, value in (aside[i] if lazy else {}).items():
            got[place] = value
        stream.advance(got)
    for stream, values in zip(wait, later):
        stream.wants = [(value, which) for value, (_, which) in zip(values, stream.wants)]
    return (work, *carry)


def finish_own(core_ref, mine, other, w_query, w_key, w_value):
    rows = mine.shape[0]
    early = w_query.shape[1] - 128
    for value, which in ((mine, core_ref[0]), (other, 1 - core_ref[0])):
        here = pl.ds(pl.multiple_of(which * rows, rows), rows)
        for i, out in enumerate((w_query, w_key, w_value)):
            last = 3 * early + i * 128
            out[here, :early] = value[:, i * early : (i + 1) * early].astype(F32)
            out[here, early:] = value[:, last : last + 128].astype(F32)


def run_finish_own(core, mine, other):
    rows, cols = mine.shape
    return pl.pallas_call(
        finish_own,
        grid_spec=pltpu.PrefetchScalarGridSpec(
            num_scalar_prefetch=1,
            grid=(1,),
            in_specs=[pl.BlockSpec(mine.shape, lambda i, c: (0, 0))] * 2,
            out_specs=[pl.BlockSpec((2 * rows, cols // 3), lambda i, c: (0, 0))] * 3,
        ),
        out_shape=[jax.ShapeDtypeStruct((2 * rows, cols // 3), F32)] * 3,
        compiler_params=pltpu.CompilerParams(vmem_limit_bytes=24 << 20),
        name="finish_own",
    )(core, mine, other)


def shards(
    mesh,
    tokens,
    labels,
    micro_counts,
    w_query,
    b_query,
    w_key,
    w_value,
    b_value,
    w_out,
    b_out,
    gain_one,
    shift_one,
    w_up,
    b_up,
    w_down,
    b_down,
    gain_two,
    shift_two,
    cotangent,
):
    cube = Cube(mesh)
    rows, width = tokens.shape
    seq = labels.shape[1]
    half = w_query.shape[1]
    pairs = half // 128
    ff = w_up.shape[1]
    head, core = cube.bit(0), cube.bit(1)
    place = jnp.stack([core, head])
    cores = core[None]

    part = run_pick_rows(cores, w_query, w_key, w_value)
    own_bias = jnp.concatenate([b_query, jnp.zeros_like(b_query), b_value])[None]
    n_seq = rows // seq
    marks = lax.dynamic_slice_in_dim(labels, head * n_seq, n_seq, 0)[:, :, None]
    own_w = w_query, w_key, w_value
    own_qkv, own_ctx, own_log = run_attend_forward(
        cores, tokens, own_w, own_bias, marks, seq, True
    )
    mine, peer_bias, own_ctx, own_w = lax.optimization_barrier(
        (cube.swap(part, 0), cube.swap(own_bias, 0), own_ctx, own_w)
    )
    other = cube.swap(mine, 1)
    peer_qkv, peer_ctx, peer_log = run_attend_forward(
        cores, tokens, (mine, other), peer_bias, marks, seq, False
    )
    vectors = jnp.stack(
        [b_out, gain_one, shift_one, b_down, gain_two, shift_two, b_down, b_down]
    )
    rows_dev = ff // cube.size
    (
        layer_output,
        *pieces,
        grad_first,
        own_grad_ctx,
        peer_grad_ctx,
        out_keep,
        out_send,
    ) = run_feed_layer(
        seq,
        place,
        micro_counts,
        (own_ctx, peer_ctx),
        tokens,
        cotangent,
        w_out,
        w_up,
        w_down,
        vectors,
        b_up[None],
        rows_dev,
    )

    stream = lambda steps: Stream(cube, steps)
    down = stream(cube.core_pieces(pieces[:2], pieces[2:4], rows_dev))
    up = stream(cube.core_pieces(pieces[4:6], pieces[6:], rows_dev))
    out = stream(cube.sum_out(out_keep, out_send))


    def backward(qkv, ctx, grad_ctx, logsum, first, count, lone=False):
        return tuple(
            run_attend_backward(
                cores, qkv, ctx, grad_ctx, marks, logsum, tokens, seq, first, count, lone
            )
        )

    def side_by_side(first, count, weights):
        cols = slice(first * 128, (first + count) * 128)
        return jnp.concatenate([weight[:, cols] for weight in weights], axis=1)

    def finish_out(mine, other):
        first = head == 0
        both = jnp.concatenate(
            [jnp.where(first, mine, other), jnp.where(first, other, mine)], axis=0
        ).astype(F32)
        side = (ff + 6 * width) // 256
        small = jnp.concatenate([both[:side, width:], both[half : half + side, width:]], axis=0)
        return both[:, :width], small.reshape(-1, width)

    far_bits = cube.upper[1:]
    found = backward(peer_qkv, peer_ctx, peer_grad_ctx, peer_log, pairs - 1, 1)
    (grads_b, keep_b, send_b, sums_b), peer_grad_ctx = tick(
        [down, out], found, peer_grad_ctx, wait=[up]
    )
    down_a = stream(cube.pieces(down.result[0], [0, 2]))
    down_b = stream(cube.pieces(down.result[1], [2, 0]))
    core_b = stream(cube.core_rows(keep_b, send_b))
    found = backward(peer_qkv, peer_ctx, peer_grad_ctx, peer_log, 0, pairs - 1)
    (grads_a, keep_a, send_a, sums_a), own_grad_ctx = tick(
        [core_b, up, out], found, own_grad_ctx, lazy=True
    )
    up_a = stream(cube.pieces(up.result[0], [3]))
    up_b = stream(cube.pieces(up.result[1], [3]))
    core_a = stream(cube.core_rows(keep_a, send_a))
    found = backward(own_qkv, own_ctx, own_grad_ctx, own_log, 0, pairs, True)
    (own_grads, keep, send, sums), grads_a, grads_b, grad_first, parts = tick(
        [core_a, down_a, down_b, up_a, out],
        found,
        grads_a,
        grads_b,
        grad_first,
        (mine, other),
        wait=[up_b],
        lazy=True,
    )
    peer = stream(cube.peer_rows([core_a.result, core_b.result]))
    own = stream(cube.own_rows(keep, send, peer))
    bias = stream(cube.sum_bias(sums, jnp.concatenate([sums_a, sums_b], axis=1)))
    own_grads, grads_a, grads_b, parts, own_w = tick(
        [own, down_b, out, peer], own_grads, grads_a, grads_b, parts, own_w, wait=[down_a, bias]
    )
    early = 3 * (half - 128)
    peer_w = [cube.join(*parts, 1)[:, i * half : (i + 1) * half] for i in range(3)]
    grad_tokens = grad_first + dims(grads_a, side_by_side(0, pairs - 1, peer_w), 1, 1)
    grad_tokens = grad_tokens + dims(grads_b, side_by_side(pairs - 1, 1, peer_w), 1, 1)
    grad_tokens, own_grads, own_w = tick(
        [bias, up_b, peer, own], grad_tokens, own_grads, own_w, wait=[down_a, out]
    )
    up_both = jnp.concatenate([up_a.result, up_b.result], axis=-1)
    up = stream(cube.pieces([up_both], [0, 2], far_bits[:1]))
    grad_tokens = grad_tokens + dims(own_grads[:, :early], side_by_side(0, pairs - 1, own_w), 1, 1)
    grad_tokens = grad_tokens + dims(own_grads[:, early:], side_by_side(pairs - 1, 1, own_w), 1, 1)
    (grad_tokens,) = tick([bias, out, down_a, own], grad_tokens)
    down_far = stream(cube.last_pieces([down_a.result, down_b.result], far_bits, far_bits))
    tick([bias, out, up, down_far, own], ())
    tick([bias, down_far, up, out, own], ())
    while any(stream.wants is not None for stream in (out, down_far)):
        tick([out, down_far], ())
    grad_w_out, small = finish_out(*out.result)
    rest = [small[i] for i in range(6)] + [small[6:].reshape(ff), down_far.result.astype(F32)]
    up_far = stream(cube.last_pieces([up.result], far_bits[1:], far_bits[1:]))
    ((grad_w_out, rest),) = tick([bias, up_far, own], (grad_w_out, rest))
    streams = [bias, own, up_far]
    while any(stream.wants is not None for stream in streams):
        tick(streams, ())
    grad_w_up = up_far.result

    grad_w_query, grad_w_key, grad_w_value = run_finish_own(cores, *own.result)
    total = bias.result[0]
    third = half - 128
    grad_b_query, grad_b_value = [
        jnp.concatenate(
            [total[i * third : (i + 1) * third], total[early + i * 128 : early + (i + 1) * 128]]
        )
        for i in (0, 2)
    ]
    return (
        layer_output,
        grad_tokens,
        grad_w_query,
        grad_b_query,
        grad_w_key,
        grad_w_value,
        grad_b_value,
        grad_w_out,
        rest[2],
        rest[0],
        rest[1],
        grad_w_up.astype(F32).T,
        rest[6],
        rest[7],
        rest[5],
        rest[3],
        rest[4],
    )


def solution(mesh):
    rows = P(("dp", "head"), None)
    placed = (rows, P("dp", None), P("dp"), P(None, "head"), P("head"), P(None, "head"))
    placed += (P(None, "head"), P("head")) + (P(),) * 10 + (rows,)
    columns = P(None, "head")
    out_specs = (rows, rows, columns, P("head"), columns, columns, P("head"))
    out_specs += (P(),) * 4 + (P(None, ("dp", "head")), P(), rows, P(), P(), P())
    return jax.shard_map(
        functools.partial(shards, mesh),
        mesh=mesh,
        in_specs=placed,
        out_specs=out_specs,
        check_vma=False,
    )
```

```python
import functools

import jax
import jax.numpy as jnp
from jax import lax
from jax.experimental import pallas as pl
from jax.experimental.pallas import tpu as pltpu
from jax.sharding import PartitionSpec as P

HEAD_DIM = 64
MICRO = 4
F32 = jnp.float32
BF16 = jnp.bfloat16
NORM_EPS = 1e-05
MASK = 2.0**30
AXES = ("dp", "head")


def dims(left, right, left_dim, right_dim):
    return lax.dot_general(
        left, right, (((left_dim,), (right_dim,)), ((), ())), preferred_element_type=F32
    )


def matmul(left, right):
    return jnp.dot(left, right, preferred_element_type=F32)


def far(value):
    return pltpu.with_memory_space_constraint(value, pltpu.HBM)


def query_marks(labels, shape):
    lane = lax.broadcasted_iota(jnp.int32, shape, 1)
    return jnp.where((lane & 63) == labels, 1.0, 0.0).astype(BF16)


def key_marks(labels, shape):
    lane = lax.broadcasted_iota(jnp.int32, shape, 1) & 63
    return jnp.where((lane < 4) & (lane != labels), -MASK, 0.0).astype(BF16)


def pick_rows(core_ref, w_query, w_key, w_value, out):
    half = w_query.shape[1]
    for i, weight in enumerate((w_query, w_key, w_value)):
        out[:, i * half : (i + 1) * half] = weight[...]


def run_pick_rows(core, w_query, w_key, w_value):
    width, half = w_query.shape
    rows = pl.BlockSpec((width // 2, half), lambda i, c: (c[0], 0))
    return pl.pallas_call(
        pick_rows,
        grid_spec=pltpu.PrefetchScalarGridSpec(
            num_scalar_prefetch=1,
            grid=(1,),
            in_specs=[rows] * 3,
            out_specs=pl.BlockSpec((width // 2, 3 * half), lambda i, c: (0, 0)),
        ),
        out_shape=jax.ShapeDtypeStruct((width // 2, 3 * half), BF16),
        name="pick_rows",
    )(core, far(w_query), far(w_key), far(w_value))


def attend_pairs(lab_ref, qkv_ref, out_ref, log_ref):
    labels = lab_ref[0]
    shape = (labels.shape[0], 128)
    half = out_ref.shape[1]
    low = lax.broadcasted_iota(jnp.int32, shape, 1) < HEAD_DIM
    q_extra, k_extra = query_marks(labels, shape), key_marks(labels, shape)
    for pair in range(half // 128):
        q, k, v = [
            qkv_ref[:, i * half + pair * 128 : i * half + (pair + 1) * 128] for i in range(3)
        ]
        q = q * jnp.asarray(0.125, BF16)
        outs = []
        for t in range(2):
            mine = low if t == 0 else jnp.logical_not(low)
            scores = dims(jnp.where(mine, k, k_extra), jnp.where(mine, q, q_extra), 1, 1)
            largest = jnp.max(scores, axis=0, keepdims=True)
            soft = jnp.exp(scores - largest)
            total = jnp.sum(soft, axis=0, keepdims=True)
            out = dims(v, soft.astype(BF16), 0, 0)
            outs.append(out[t * HEAD_DIM : (t + 1) * HEAD_DIM] * (1.0 / total))
            log_ref[0, pair, t : t + 1] = largest + jnp.log(total)
        out_ref[:, pair * 128 : (pair + 1) * 128] = jnp.concatenate(outs, axis=0).T.astype(BF16)


def attend_own(core_ref, x, w_query, w_key, w_value, bias, lab_ref, *outs):
    qkv_ref = outs[0]
    width = w_query.shape[1]
    for i, weight in enumerate((w_query, w_key, w_value)):
        cols = slice(i * width, (i + 1) * width)
        value = matmul(x[...], weight[...]) + bias[:, cols].astype(F32)
        qkv_ref[:, cols] = value.astype(BF16)
    attend_pairs(lab_ref, *outs)


def attend_peer(core_ref, x_mine, x_other, w_mine, w_other, bias, lab_ref, *outs):
    qkv_ref = outs[0]
    width = qkv_ref.shape[1] // 3
    for i in range(3):
        cols = slice(i * width, (i + 1) * width)
        value = matmul(x_mine[...], w_mine[:, cols]) + matmul(x_other[...], w_other[:, cols])
        qkv_ref[:, cols] = (value + bias[:, cols].astype(F32)).astype(BF16)
    attend_pairs(lab_ref, *outs)


def run_attend_forward(core, tokens, weights, bias, labels, seq, own):
    rows, depth = tokens.shape
    cols = bias.shape[1]
    pairs = cols // (3 * 128)
    if own:
        xs = [pl.BlockSpec((seq, depth), lambda s, c: (s, 0))]
    else:
        xs = [
            pl.BlockSpec((seq, depth // 2), lambda s, c: (s, c[0])),
            pl.BlockSpec((seq, depth // 2), lambda s, c: (s, 1 - c[0])),
        ]
    fixed = [
        pl.BlockSpec(weight.shape, lambda s, c: (0, 0), pipeline_mode=pl.Buffered(1))
        for weight in (*weights, bias)
    ]
    return pl.pallas_call(
        attend_own if own else attend_peer,
        grid_spec=pltpu.PrefetchScalarGridSpec(
            num_scalar_prefetch=1,
            grid=(rows // seq,),
            in_specs=xs + fixed + [pl.BlockSpec((1, seq, 1), lambda s, c: (s, 0, 0))],
            out_specs=[
                pl.BlockSpec((seq, cols), lambda s, c: (s, 0)),
                pl.BlockSpec((seq, cols // 3), lambda s, c: (s, 0)),
                pl.BlockSpec((1, pairs, 2, seq), lambda s, c: (s, 0, 0, 0)),
            ],
        ),
        out_shape=[
            pltpu.HBM((rows, cols), BF16),
            pltpu.HBM((rows, cols // 3), BF16),
            jax.ShapeDtypeStruct((rows // seq, pairs, 2, seq), F32),
        ],
        compiler_params=pltpu.CompilerParams(vmem_limit_bytes=24 << 20),
        cost_estimate=pl.CostEstimate(
            flops=rows * pairs * 2 * seq * 256 * 2 * 3, bytes_accessed=8 << 20, transcendentals=0
        ),
        name="attend_forward",
    )(core, *[tokens] * len(xs), *weights, bias, labels)


def attend_backward(
    first,
    count,
    lone,
    core_ref,
    q_ref,
    k_ref,
    v_ref,
    out_ref,
    grad_ref,
    lab_ref,
    log_ref,
    x_keep,
    x_send,
    *refs,
):
    grads_ref, keep_ref, send_ref, bias_ref, keep_sum, send_sum, bias_sum = refs
    early = count - 1 if lone else count
    step = pl.program_id(0)
    labels = lab_ref[0]
    shape = (labels.shape[0], 128)
    low = lax.broadcasted_iota(jnp.int32, shape, 1) < HEAD_DIM
    q_extra, k_extra = query_marks(labels, shape), key_marks(labels, shape)
    for pair in range(count):
        cols = slice((first + pair) * 128, (first + pair + 1) * 128)
        q = q_ref[:, cols] * jnp.asarray(0.125, BF16)
        k, v, grad = k_ref[:, cols], v_ref[:, cols], grad_ref[:, cols]
        zero = jnp.zeros_like(q)
        inner = (grad.astype(F32) * out_ref[:, cols].astype(F32)).T
        dqs, dks, dvs = [], [], []
        for t in range(2):
            mine = low if t == 0 else jnp.logical_not(low)
            half = slice(t * HEAD_DIM, (t + 1) * HEAD_DIM)
            scores = dims(jnp.where(mine, k, k_extra), jnp.where(mine, q, q_extra), 1, 1)
            soft = jnp.exp(scores - log_ref[0, first + pair, t : t + 1])
            grad_soft = dims(v, jnp.where(mine, grad, zero), 1, 1)
            row_inner = jnp.sum(inner[half], axis=0, keepdims=True)
            grad_scores = (soft * (grad_soft - row_inner)).astype(BF16)
            dvs.append(dims(soft.astype(BF16), grad, 1, 0))
            dks.append(dims(grad_scores, q, 1, 0))
            dqs.append(dims(k, grad_scores, 0, 0)[half])
        found = (
            (jnp.concatenate(dqs, axis=0).T * 0.125).astype(BF16),
            jnp.where(low, dks[0], dks[1]).astype(BF16),
            jnp.where(low, dvs[0], dvs[1]).astype(BF16),
        )
        for i, value in enumerate(found):
            place = i * early + pair if pair < early else 3 * early + i
            grads_ref[:, place * 128 : (place + 1) * 128] = value

    grads = grads_ref[...]
    keep, send = dims(x_keep[...], grads, 0, 0), dims(x_send[...], grads, 0, 0)
    bias = jnp.sum(grads.astype(F32), axis=0, keepdims=True)

    @pl.when(step == 0)
    def _():
        keep_sum[...] = keep
        send_sum[...] = send
        bias_sum[...] = bias

    @pl.when(step > 0)
    def _():
        keep_sum[...] += keep
        send_sum[...] += send
        bias_sum[...] += bias

    @pl.when(step == pl.num_programs(0) - 1)
    def _():
        bias_ref[...] = bias_sum[...]
        keep_ref[...] = keep_sum[...].astype(BF16)
        send_ref[...] = send_sum[...].astype(BF16)


def run_attend_backward(
    core, qkv, out, grad, labels, logsum, tokens, seq, first, count, lone=False
):
    rows = qkv.shape[0]
    pairs = qkv.shape[1] // (3 * 128)
    cols = 3 * 128 * count
    half = tokens.shape[1] // 2
    held_pairs, skip = (1, first) if count == 1 else (pairs, 0)
    part = lambda which: pl.BlockSpec(
        (seq, held_pairs * 128),
        lambda s, c: (s, (which * pairs + skip) // held_pairs),
    )
    weight = (jax.ShapeDtypeStruct if lone else pltpu.HBM)((half, cols), BF16)
    fixed = lambda shape: pl.BlockSpec(shape, lambda s, c: (0, 0))
    return pl.pallas_call(
        functools.partial(attend_backward, first - skip, count, lone),
        grid_spec=pltpu.PrefetchScalarGridSpec(
            num_scalar_prefetch=1,
            grid=(rows // seq,),
            in_specs=[
                part(0),
                part(1),
                part(2),
                part(0),
                part(0),
                pl.BlockSpec((1, seq, 1), lambda s, c: (s, 0, 0)),
                pl.BlockSpec((1, held_pairs, 2, seq), lambda s, c: (s, skip, 0, 0)),
                pl.BlockSpec((seq, half), lambda s, c: (s, c[0])),
                pl.BlockSpec((seq, half), lambda s, c: (s, 1 - c[0])),
            ],
            out_specs=[
                pl.BlockSpec((seq, cols), lambda s, c: (s, 0)),
                fixed((half, cols)),
                fixed((half, cols)),
                fixed((1, cols)),
            ],
            scratch_shapes=[
                pltpu.VMEM((half, cols), F32),
                pltpu.VMEM((half, cols), F32),
                pltpu.VMEM((1, cols), F32),
            ],
        ),
        out_shape=[
            pltpu.HBM((rows, cols), BF16),
            weight,
            weight,
            jax.ShapeDtypeStruct((1, cols), F32),
        ],
        compiler_params=pltpu.CompilerParams(vmem_limit_bytes=26 << 20),
        cost_estimate=pl.CostEstimate(
            flops=rows * count * 2 * seq * 256 * 2 * 3, bytes_accessed=8 << 20, transcendentals=0
        ),
        name="attend_backward",
    )(
        core,
        *[far(qkv)] * 3,
        far(out),
        far(grad),
        labels,
        logsum,
        tokens,
        tokens,
    )


def gelu_pair(inner):
    phi = 0.5 + 0.5 * lax.erf(inner * 0.7071067811865476)
    bell = jnp.exp(-0.5 * (inner * inner))
    return inner * phi, phi + inner * (bell * 0.3989422804014327)


def norm_parts(values):
    centered = values - jnp.mean(values, axis=-1, keepdims=True)
    factor = lax.rsqrt(jnp.mean(centered * centered, axis=-1, keepdims=True) + NORM_EPS)
    return centered * factor, factor


def norm_back(grad_out, normed, factor, gain):
    scaled = grad_out * gain
    return factor * (
        scaled
        - jnp.mean(scaled, axis=-1, keepdims=True)
        - normed * jnp.mean(scaled * normed, axis=-1, keepdims=True)
    )


def feed_layer(seq, chunk, n_tok, n_hid, n_ctx, place_ref, count_ref, *refs):
    contexts, refs = refs[:n_ctx], refs[n_ctx:]
    tokens, cotangent, w_out_mine, w_out_other, w_up, w_down, vectors, b_up = refs[:8]
    y_ref, down, up, first_ref = refs[8], refs[9:13], refs[13:17], refs[17]
    grad_ctxs, (out_keep, out_send) = refs[18 : 18 + n_ctx], refs[18 + n_ctx : 20 + n_ctx]
    act, slope, normed, factor, hidden, mid, mid_low, total, sums, b_up_sum = refs[
        20 + n_ctx : 30 + n_ctx
    ]
    far_up, far_down = w_up, w_down
    w_up, w_down, w_out, up_sem, down_sem = refs[30 + n_ctx :]
    step = pl.program_id(0)
    block = tokens.shape[0]
    core, head = place_ref[0], place_ref[1]
    b_out, gain_one, shift_one, b_down, gain_two, shift_two = [
        vectors[i : i + 1] for i in range(6)
    ]

    def add(row, *values):
        for i, value in enumerate(values):
            sums[row + i : row + i + 1] += jnp.sum(value, axis=0, keepdims=True)

    @pl.when(step == 0)
    def _():
        pltpu.make_async_copy(far_up, w_up, up_sem).start()
        pltpu.make_async_copy(far_down, w_down, down_sem).start()
        w_out[: w_out_mine.shape[0]] = w_out_mine[...]
        w_out[w_out_mine.shape[0] :] = w_out_other[...]
        sums[...] = jnp.zeros_like(sums)
        total[...] = jnp.zeros_like(total)

    @pl.when(step < n_tok)
    def _():
        start = pl.multiple_of(step * block, block)
        here = pl.ds(start, block)
        context = jnp.concatenate([ctx[...] for ctx in contexts], axis=1)
        normed_one, factor_one = norm_parts(
            tokens[...].astype(F32) + matmul(context, w_out[...]) + b_out
        )
        normed[here] = normed_one
        factor[here] = jnp.broadcast_to(factor_one, (block, 128))
        hidden_here = normed_one * gain_one + shift_one
        hidden_low = hidden_here.astype(BF16)
        hidden[here] = hidden_low
        sum_two = hidden_here + b_down

        @pl.when(step == 0)
        def _():
            pltpu.make_async_copy(far_up, w_up, up_sem).wait()
            pltpu.make_async_copy(far_down, w_down, down_sem).wait()

        for j in range(w_up.shape[1] // chunk):
            cols = slice(j * chunk, (j + 1) * chunk)
            activated, gradient = gelu_pair(matmul(hidden_low, w_up[:, cols]) + b_up[:, cols])
            activated = activated.astype(BF16)
            act[here, cols] = activated
            slope[here, cols] = gradient.astype(BF16)
            sum_two = sum_two + matmul(activated, w_down[cols, :])
        normed_two, factor_two = norm_parts(sum_two)
        y_ref[...] = (normed_two * gain_two + shift_two).astype(BF16)
        place = start + lax.broadcasted_iota(jnp.int32, (block, 1), 0)
        live = (place % seq // (seq // MICRO) < count_ref[0]).astype(F32)
        grad_y = cotangent[...].astype(F32) * live
        grad_mid = norm_back(grad_y, normed_two, factor_two, gain_two)
        mid[here] = grad_mid
        mid_low[here] = grad_mid.astype(BF16)
        add(3, grad_y * normed_two, grad_y, grad_mid)

    @pl.when((step >= n_tok) & (step < n_tok + n_hid))
    def _():
        width = act.shape[1] // n_hid
        here = pl.ds(pl.multiple_of((step - n_tok) * width, width), width)

        def put(result, pieces):
            groups, group_rows, cols = pieces[0].shape
            result = result.reshape(groups, 2, group_rows, 2 * cols)
            for i in range(2):
                side = result[..., i * cols : (i + 1) * cols]
                pieces[i][...] = jnp.where(core == 0, side[:, 0], side[:, 1]).astype(BF16)
                pieces[2 + i][...] = jnp.where(core == 0, side[:, 1], side[:, 0]).astype(BF16)

        put(dims(act[:, here], mid_low[...], 0, 0), down)
        grad = dims(mid_low[...], w_down[here, :], 1, 1) * slope[:, here].astype(F32)
        grad = grad.astype(BF16)
        slope[:, here] = grad
        b_up_sum[:, here] = jnp.sum(grad.astype(F32), axis=0, keepdims=True)
        put(dims(grad, hidden[...], 0, 0), up)

    @pl.when(step >= n_tok + n_hid)
    def _():
        start = pl.multiple_of((step - n_tok - n_hid) * block, block)
        here = pl.ds(start, block)
        grad = mid[here] + dims(slope[here], w_up[...], 1, 1)
        normed_one = normed[here]
        grad_first = norm_back(grad, normed_one, factor[here, :1], gain_one)
        first_ref[...] = grad_first
        add(0, grad * normed_one, grad, grad_first)
        first_low = grad_first.astype(BF16)
        grad_ctx = dims(first_low, w_out[...], 1, 1).astype(BF16)
        start = 0
        for ref in grad_ctxs:
            ref[...] = grad_ctx[:, start : start + ref.shape[1]]
            start += ref.shape[1]
        context = jnp.concatenate([ctx[...] for ctx in contexts], axis=1)
        total[...] += dims(context, first_low, 0, 0)

    @pl.when(step == pl.num_programs(0) - 1)
    def _():
        lanes = [sums[i : i + 1] for i in range(6)] + [b_up_sum[...]]
        lanes = [
            row[:, k * 128 : (k + 1) * 128] for row in lanes for k in range(row.shape[1] // 128)
        ]
        n_side = len(lanes) // 2
        rows, d = out_keep.shape[1], total.shape[1]
        fill = jnp.zeros((rows - n_side, 128), F32)
        sides = [
            jnp.concatenate(part + [fill], axis=0) for part in (lanes[:n_side], lanes[n_side:])
        ]
        for i in range(2):
            side = jnp.where(head == i, sides[0], sides[1]).astype(BF16)
            for ref, which in ((out_keep, core), (out_send, 1 - core)):
                place = pl.multiple_of((2 * i + which) * rows, rows)
                ref[i, :, :d] = total[pl.ds(place, rows)].astype(BF16)
                ref[i, :, d:] = side


def run_feed_layer(
    seq,
    place,
    count,
    contexts,
    tokens,
    cotangent,
    w_out,
    w_up,
    w_down,
    vectors,
    b_up,
    rows_dev,
    block=512,
    width=768,
    chunk=1024,
):
    rows, d = tokens.shape
    ff = w_up.shape[1]
    group_rows = 2 * rows_dev
    groups = width // (2 * group_rows)
    n_tok, n_hid = rows // block, ff // width
    held = lambda shape: pl.BlockSpec(
        shape, lambda i, *_: (0,) * len(shape), pipeline_mode=pl.Buffered(1)
    )
    early = lambda cols: pl.BlockSpec(
        (block, cols), lambda i, *_: (jnp.minimum(i, n_tok - 1), 0)
    )
    late = lambda cols: pl.BlockSpec(
        (block, cols), lambda i, *_: (jnp.maximum(i - n_tok - n_hid, 0), 0)
    )
    twice = lambda cols: pl.BlockSpec(
        (block, cols),
        lambda i, *_: (jnp.where(i < n_tok, i, jnp.maximum(i - n_tok - n_hid, 0)), 0),
    )
    half_rows = lambda which: pl.BlockSpec(
        (d // 2, d), lambda i, place, _: (which(place), 0), pipeline_mode=pl.Buffered(1)
    )
    piece = pl.BlockSpec(
        (groups, group_rows, d // 2), lambda i, *_: (jnp.clip(i - n_tok, 0, n_hid - 1), 0, 0)
    )
    out = jax.ShapeDtypeStruct
    shape = (ff // (2 * group_rows), group_rows, d // 2)
    pieces = [pltpu.HBM(shape, BF16)] * 4 + [pltpu.HBM(shape, BF16)] * 4
    widths = [ctx.shape[1] for ctx in contexts]
    out_half = (2, d // 4, d + 128)
    return pl.pallas_call(
        functools.partial(feed_layer, seq, chunk, n_tok, n_hid, len(contexts)),
        grid_spec=pltpu.PrefetchScalarGridSpec(
            num_scalar_prefetch=2,
            grid=(2 * n_tok + n_hid,),
            in_specs=[twice(w) for w in widths]
            + [early(d), early(d)]
            + [half_rows(lambda place: place[1]), half_rows(lambda place: 1 - place[1])]
            + [pl.BlockSpec(memory_space=pl.ANY)] * 2
            + [held(vectors.shape), held(b_up.shape)],
            out_specs=[early(d)]
            + [piece] * 8
            + [late(d)]
            + [late(w) for w in widths]
            + [held(out_half)] * 2,
            scratch_shapes=[
                pltpu.VMEM((rows, ff), BF16),
                pltpu.VMEM((rows, ff), BF16),
                pltpu.VMEM((rows, d), F32),
                pltpu.VMEM((rows, 128), F32),
                pltpu.VMEM((rows, d), BF16),
                pltpu.VMEM((rows, d), F32),
                pltpu.VMEM((rows, d), BF16),
                pltpu.VMEM((d, d), F32),
                pltpu.VMEM((8, d), F32),
                pltpu.VMEM((1, ff), F32),
                pltpu.VMEM(w_up.shape, BF16),
                pltpu.VMEM(w_down.shape, BF16),
                pltpu.VMEM(w_out.shape, BF16),
                pltpu.SemaphoreType.DMA,
                pltpu.SemaphoreType.DMA,
            ],
        ),
        out_shape=[out((rows, d), BF16)]
        + pieces
        + [pltpu.HBM((rows, d), F32)]
        + [pltpu.HBM((rows, w), BF16) for w in widths]
        + [pltpu.HBM(out_half, BF16)] * 2,
        compiler_params=pltpu.CompilerParams(vmem_limit_bytes=60 << 20),
        cost_estimate=pl.CostEstimate(
            flops=4 * rows * d * (3 * d + 6 * ff), bytes_accessed=60 << 20, transcendentals=0
        ),
        name="feed_layer",
    )(
        place,
        count,
        *[far(ctx) for ctx in contexts],
        tokens,
        cotangent,
        w_out,
        w_out,
        far(w_up),
        far(w_down),
        vectors,
        b_up,
    )


class Cube:
    def __init__(self, mesh):
        self.size = mesh.shape["dp"] * mesh.shape["head"]
        self.n_bits = self.size.bit_length() - 1
        self.upper = list(range(2, self.n_bits))
        self.index = lax.axis_index("dp") * mesh.shape["head"] + lax.axis_index("head")

    def bit(self, which):
        return (self.index >> which) & 1

    def swap(self, value, which):
        pairs = [(i, i ^ (1 << which)) for i in range(self.size)]
        return lax.ppermute(value, AXES, pairs)

    def half(self, value, axis, which, mine):
        bit = self.bit(which) if mine else 1 - self.bit(which)
        return lax.dynamic_index_in_dim(value, bit, axis, keepdims=False)

    def join(self, value, other, which):
        first = self.bit(which) == 0
        return jnp.concatenate(
            [jnp.where(first, value, other), jnp.where(first, other, value)], axis=0
        )


    def core_pieces(self, keep, send, rows_dev):
        others = yield [(part, 1) for part in send]
        shape = (2,) * (self.n_bits - 1) + (rows_dev, keep[0].shape[-1])
        return [[term.reshape(shape) for term in pair] for pair in zip(keep, others)]

    def pieces(self, terms, order, done=()):
        bits = [bit for bit in range(self.n_bits - 1, 1, -1) if bit not in done] + [0]
        for step in order:
            axis = bits.index(step)
            send, kept = [sum(self.half(term, axis, step, mine) for term in terms) for mine in (0, 1)]
            other, kept = yield [(send, step), (kept, None)]
            terms = [kept, other]
            bits.remove(step)
        return sum(terms)

    def last_pieces(self, values, order, bits):
        value = jnp.concatenate(values, axis=-1)
        bits = sorted(bits, reverse=True)
        for step in order:
            axis = bits.index(step)
            send, kept = [self.half(value, axis, step, mine) for mine in (0, 1)]
            other, kept = yield [(send, step), (kept, None)]
            value = kept + other
            bits.remove(step)
        return value

    def reduce_rows(self, value, order):
        halved = []
        for which in order:
            rows = value.shape[0]
            if rows % 32 == 0 and rows > 96:
                value = value.reshape(2, rows // 2, value.shape[1])
                (other,) = yield [(self.half(value, 0, which, False), which)]
                value = self.half(value, 0, which, True) + other
                halved.append(which)
            else:
                value = lax.optimization_barrier(value)
                (other,) = yield [(value, which)]
                value = value + other
        return value, halved

    def gather_rows(self, value, halved):
        for which in reversed(halved):
            (other,) = yield [(value, which)]
            value = self.join(value, other, which)
        return value

    def sum_out(self, keep, send):
        (other,) = yield [(send, 1)]
        (other_two,) = yield [(keep[1] + other[1], 0)]
        value, halved = yield from self.reduce_rows(keep[0] + other[0] + other_two, self.upper)
        value = yield from self.gather_rows(value, halved)
        (other,) = yield [(value, 0)]
        value = jnp.concatenate([value, other], axis=1)
        value = yield from self.gather_rows(value, [1])
        return value[:, : value.shape[1] // 2], value[:, value.shape[1] // 2 :]

    def core_rows(self, keep, send):
        (other,) = yield [(send, 1)]
        return keep + other

    def sum_bias(self, own, peer):
        value = jnp.concatenate([own, peer], axis=0)
        (other,) = yield [(value, 1)]
        value = value + other
        (other,) = yield [(value[1:], 0)]
        value = value[:1] + other
        for which in self.upper:
            (other,) = yield [(value, which)]
            value = value + other
        return value

    def peer_rows(self, parts):
        value = jnp.concatenate(parts, axis=1)
        value = value.reshape(2, value.shape[0] // 2, value.shape[1])
        (other,) = yield [(self.half(value, 0, 2, False), 2)]
        value = self.half(value, 0, 2, True) + other
        (other,) = yield [(value, 0)]
        return other

    def own_rows(self, keep, send, peer):
        (other,) = yield [(send, 1)]
        value = keep + other
        value = value.reshape(2, value.shape[0] // 2, value.shape[1])
        (other,) = yield [(self.half(value, 0, 2, False), 2)]
        value = self.half(value, 0, 2, True) + other + peer.result
        value, halved = yield from self.reduce_rows(value, self.upper[1:])
        value = yield from self.gather_rows(value, [2] + halved)
        (other,) = yield [(value, 1)]
        return value, other


class Stream:
    def __init__(self, cube, steps):
        self.cube, self.steps, self.result = cube, steps, None
        self.wants = None
        self.advance(None)

    def advance(self, got):
        try:
            self.wants = self.steps.send(got)
        except StopIteration as stop:
            self.wants, self.result = None, stop.value

    def values(self):
        return tuple(value for value, _ in self.wants)

    def swaps(self):
        return tuple(
            value if which is None else self.cube.swap(value, which) for value, which in self.wants
        )


def tick(streams, work, *carry, wait=(), lazy=False):
    streams = [stream for stream in streams if stream.wants is not None]
    wait = [stream for stream in wait if stream.wants is not None and stream not in streams]
    moved = [list(stream.swaps()) for stream in streams]
    aside = []
    if lazy:
        for stream, got in zip(streams, moved):
            aside.append(
                {i: got[i] for i, (_, which) in enumerate(stream.wants) if which is None}
            )
            for i in aside[-1]:
                got[i] = ()
    later = [stream.values() for stream in wait]
    moved, work, carry, later = lax.optimization_barrier((moved, work, carry, later))
    for i, (stream, got) in enumerate(zip(streams, moved)):
        for place, value in (aside[i] if lazy else {}).items():
            got[place] = value
        stream.advance(got)
    for stream, values in zip(wait, later):
        stream.wants = [(value, which) for value, (_, which) in zip(values, stream.wants)]
    return (work, *carry)


def finish_own(core_ref, mine, other, w_query, w_key, w_value):
    rows = mine.shape[0]
    early = w_query.shape[1] - 128
    for value, which in ((mine, core_ref[0]), (other, 1 - core_ref[0])):
        here = pl.ds(pl.multiple_of(which * rows, rows), rows)
        for i, out in enumerate((w_query, w_key, w_value)):
            last = 3 * early + i * 128
            out[here, :early] = value[:, i * early : (i + 1) * early].astype(F32)
            out[here, early:] = value[:, last : last + 128].astype(F32)


def run_finish_own(core, mine, other):
    rows, cols = mine.shape
    return pl.pallas_call(
        finish_own,
        grid_spec=pltpu.PrefetchScalarGridSpec(
            num_scalar_prefetch=1,
            grid=(1,),
            in_specs=[pl.BlockSpec(mine.shape, lambda i, c: (0, 0))] * 2,
            out_specs=[pl.BlockSpec((2 * rows, cols // 3), lambda i, c: (0, 0))] * 3,
        ),
        out_shape=[jax.ShapeDtypeStruct((2 * rows, cols // 3), F32)] * 3,
        compiler_params=pltpu.CompilerParams(vmem_limit_bytes=24 << 20),
        name="finish_own",
    )(core, mine, other)


def shards(
    mesh,
    tokens,
    labels,
    micro_counts,
    w_query,
    b_query,
    w_key,
    w_value,
    b_value,
    w_out,
    b_out,
    gain_one,
    shift_one,
    w_up,
    b_up,
    w_down,
    b_down,
    gain_two,
    shift_two,
    cotangent,
):
    cube = Cube(mesh)
    rows, width = tokens.shape
    seq = labels.shape[1]
    half = w_query.shape[1]
    pairs = half // 128
    ff = w_up.shape[1]
    head, core = cube.bit(0), cube.bit(1)
    place = jnp.stack([core, head])
    cores = core[None]

    part = run_pick_rows(cores, w_query, w_key, w_value)
    own_bias = jnp.concatenate([b_query, jnp.zeros_like(b_query), b_value])[None]
    n_seq = rows // seq
    marks = lax.dynamic_slice_in_dim(labels, head * n_seq, n_seq, 0)[:, :, None]
    own_w = w_query, w_key, w_value
    own_qkv, own_ctx, own_log = run_attend_forward(
        cores, tokens, own_w, own_bias, marks, seq, True
    )
    mine, peer_bias, own_ctx, own_w = lax.optimization_barrier(
        (cube.swap(part, 0), cube.swap(own_bias, 0), own_ctx, own_w)
    )
    other = cube.swap(mine, 1)
    peer_qkv, peer_ctx, peer_log = run_attend_forward(
        cores, tokens, (mine, other), peer_bias, marks, seq, False
    )
    vectors = jnp.stack(
        [b_out, gain_one, shift_one, b_down, gain_two, shift_two, b_down, b_down]
    )
    rows_dev = ff // cube.size
    (
        layer_output,
        *pieces,
        grad_first,
        own_grad_ctx,
        peer_grad_ctx,
        out_keep,
        out_send,
    ) = run_feed_layer(
        seq,
        place,
        micro_counts,
        (own_ctx, peer_ctx),
        tokens,
        cotangent,
        w_out,
        w_up,
        w_down,
        vectors,
        b_up[None],
        rows_dev,
    )

    stream = lambda steps: Stream(cube, steps)
    down = stream(cube.core_pieces(pieces[:2], pieces[2:4], rows_dev))
    up = stream(cube.core_pieces(pieces[4:6], pieces[6:], rows_dev))
    out = stream(cube.sum_out(out_keep, out_send))


    def backward(qkv, ctx, grad_ctx, logsum, first, count, lone=False):
        return tuple(
            run_attend_backward(
                cores, qkv, ctx, grad_ctx, marks, logsum, tokens, seq, first, count, lone
            )
        )

    def side_by_side(first, count, weights):
        cols = slice(first * 128, (first + count) * 128)
        return jnp.concatenate([weight[:, cols] for weight in weights], axis=1)

    def finish_out(mine, other):
        first = head == 0
        both = jnp.concatenate(
            [jnp.where(first, mine, other), jnp.where(first, other, mine)], axis=0
        ).astype(F32)
        side = (ff + 6 * width) // 256
        small = jnp.concatenate([both[:side, width:], both[half : half + side, width:]], axis=0)
        return both[:, :width], small.reshape(-1, width)

    far_bits = cube.upper[1:]
    found = backward(peer_qkv, peer_ctx, peer_grad_ctx, peer_log, pairs - 1, 1)
    (grads_b, keep_b, send_b, sums_b), peer_grad_ctx = tick(
        [down, out], found, peer_grad_ctx, wait=[up]
    )
    down_a = stream(cube.pieces(down.result[0], [0, 2]))
    down_b = stream(cube.pieces(down.result[1], [2, 0]))
    core_b = stream(cube.core_rows(keep_b, send_b))
    found = backward(peer_qkv, peer_ctx, peer_grad_ctx, peer_log, 0, pairs - 1)
    (grads_a, keep_a, send_a, sums_a), own_grad_ctx = tick(
        [core_b, up, out], found, own_grad_ctx, wait=[down_a], lazy=True
    )
    up_a = stream(cube.pieces(up.result[0], [3]))
    up_b = stream(cube.pieces(up.result[1], [3]))
    core_a = stream(cube.core_rows(keep_a, send_a))
    (_, own_grad_ctx) = tick([core_a], (), own_grad_ctx, wait=[up_b])
    peer = stream(cube.peer_rows([core_a.result, core_b.result]))
    found = backward(own_qkv, own_ctx, own_grad_ctx, own_log, 0, pairs, True)
    (own_grads, keep, send, sums), grads_a, grads_b, grad_first, parts = tick(
        [down_a, down_b, up_a, out, peer],
        found,
        grads_a,
        grads_b,
        grad_first,
        (mine, other),
        wait=[up_b],
        lazy=True,
    )
    own = stream(cube.own_rows(keep, send, peer))
    bias = stream(cube.sum_bias(sums, jnp.concatenate([sums_a, sums_b], axis=1)))
    own_grads, grads_a, grads_b, parts, own_w = tick(
        [bias, own], own_grads, grads_a, grads_b, parts, own_w, wait=[down_a, down_b, up_b]
    )
    early = 3 * (half - 128)
    peer_w = [cube.join(*parts, 1)[:, i * half : (i + 1) * half] for i in range(3)]
    grad_tokens = grad_first + dims(grads_a, side_by_side(0, pairs - 1, peer_w), 1, 1)
    grad_tokens = grad_tokens + dims(grads_b, side_by_side(pairs - 1, 1, peer_w), 1, 1)
    grad_tokens, own_grads, own_w = tick(
        [bias, out, peer, own], grad_tokens, own_grads, own_w, wait=[down_a, down_b]
    )
    grad_tokens = grad_tokens + dims(own_grads[:, :early], side_by_side(0, pairs - 1, own_w), 1, 1)
    grad_tokens = grad_tokens + dims(own_grads[:, early:], side_by_side(pairs - 1, 1, own_w), 1, 1)
    (grad_tokens,) = tick([out, down_a, down_b, up_b, own], grad_tokens, wait=[bias])
    up_both = jnp.concatenate([up_a.result, up_b.result], axis=-1)
    up = stream(cube.pieces([up_both], [0, 2], far_bits[:1]))
    down_far = stream(cube.last_pieces([down_a.result, down_b.result], far_bits, far_bits))
    tick([bias, out, up, down_far, own], ())
    tick([bias, down_far, up, out, own], ())
    while any(stream.wants is not None for stream in (out, down_far)):
        tick([out, down_far], ())
    grad_w_out, small = finish_out(*out.result)
    rest = [small[i] for i in range(6)] + [small[6:].reshape(ff), down_far.result.astype(F32)]
    up_far = stream(cube.last_pieces([up.result], far_bits[1:], far_bits[1:]))
    ((grad_w_out, rest),) = tick([bias, up_far, own], (grad_w_out, rest))
    streams = [bias, own, up_far]
    while any(stream.wants is not None for stream in streams):
        tick(streams, ())
    grad_w_up = up_far.result

    grad_w_query, grad_w_key, grad_w_value = run_finish_own(cores, *own.result)
    total = bias.result[0]
    third = half - 128
    grad_b_query, grad_b_value = [
        jnp.concatenate(
            [total[i * third : (i + 1) * third], total[early + i * 128 : early + (i + 1) * 128]]
        )
        for i in (0, 2)
    ]
    return (
        layer_output,
        grad_tokens,
        grad_w_query,
        grad_b_query,
        grad_w_key,
        grad_w_value,
        grad_b_value,
        grad_w_out,
        rest[2],
        rest[0],
        rest[1],
        grad_w_up.astype(F32).T,
        rest[6],
        rest[7],
        rest[5],
        rest[3],
        rest[4],
    )


def solution(mesh):
    rows = P(("dp", "head"), None)
    placed = (rows, P("dp", None), P("dp"), P(None, "head"), P("head"), P(None, "head"))
    placed += (P(None, "head"), P("head")) + (P(),) * 10 + (rows,)
    columns = P(None, "head")
    out_specs = (rows, rows, columns, P("head"), columns, columns, P("head"))
    out_specs += (P(),) * 4 + (P(None, ("dp", "head")), P(), rows, P(), P(), P())
    return jax.shard_map(
        functools.partial(shards, mesh),
        mesh=mesh,
        in_specs=placed,
        out_specs=out_specs,
        check_vma=False,
    )
```

```python
import functools

import jax
import jax.numpy as jnp
from jax import lax
from jax.experimental import pallas as pl
from jax.experimental.pallas import tpu as pltpu
from jax.sharding import PartitionSpec as P

HEAD_DIM = 64
MICRO = 4
F32 = jnp.float32
BF16 = jnp.bfloat16
NORM_EPS = 1e-05
MASK = 2.0**30
AXES = ("dp", "head")


def dims(left, right, left_dim, right_dim):
    return lax.dot_general(
        left, right, (((left_dim,), (right_dim,)), ((), ())), preferred_element_type=F32
    )


def matmul(left, right):
    return jnp.dot(left, right, preferred_element_type=F32)


def far(value):
    return pltpu.with_memory_space_constraint(value, pltpu.HBM)


def query_marks(labels, shape):
    lane = lax.broadcasted_iota(jnp.int32, shape, 1)
    return jnp.where((lane & 63) == labels, 1.0, 0.0).astype(BF16)


def key_marks(labels, shape):
    lane = lax.broadcasted_iota(jnp.int32, shape, 1) & 63
    return jnp.where((lane < 4) & (lane != labels), -MASK, 0.0).astype(BF16)


def pick_rows(core_ref, w_query, w_key, w_value, out):
    half = w_query.shape[1]
    for i, weight in enumerate((w_query, w_key, w_value)):
        out[:, i * half : (i + 1) * half] = weight[...]


def run_pick_rows(core, w_query, w_key, w_value):
    width, half = w_query.shape
    rows = pl.BlockSpec((width // 2, half), lambda i, c: (c[0], 0))
    return pl.pallas_call(
        pick_rows,
        grid_spec=pltpu.PrefetchScalarGridSpec(
            num_scalar_prefetch=1,
            grid=(1,),
            in_specs=[rows] * 3,
            out_specs=pl.BlockSpec((width // 2, 3 * half), lambda i, c: (0, 0)),
        ),
        out_shape=jax.ShapeDtypeStruct((width // 2, 3 * half), BF16),
        name="pick_rows",
    )(core, far(w_query), far(w_key), far(w_value))


def attend_pairs(lab_ref, qkv_ref, out_ref, log_ref):
    labels = lab_ref[0]
    shape = (labels.shape[0], 128)
    half = out_ref.shape[1]
    low = lax.broadcasted_iota(jnp.int32, shape, 1) < HEAD_DIM
    q_extra, k_extra = query_marks(labels, shape), key_marks(labels, shape)
    for pair in range(half // 128):
        q, k, v = [
            qkv_ref[:, i * half + pair * 128 : i * half + (pair + 1) * 128] for i in range(3)
        ]
        q = q * jnp.asarray(0.125, BF16)
        outs = []
        for t in range(2):
            mine = low if t == 0 else jnp.logical_not(low)
            scores = dims(jnp.where(mine, k, k_extra), jnp.where(mine, q, q_extra), 1, 1)
            largest = jnp.max(scores, axis=0, keepdims=True)
            soft = jnp.exp(scores - largest)
            total = jnp.sum(soft, axis=0, keepdims=True)
            out = dims(v, soft.astype(BF16), 0, 0)
            outs.append(out[t * HEAD_DIM : (t + 1) * HEAD_DIM] * (1.0 / total))
            log_ref[0, pair, t : t + 1] = largest + jnp.log(total)
        out_ref[:, pair * 128 : (pair + 1) * 128] = jnp.concatenate(outs, axis=0).T.astype(BF16)


def attend_own(core_ref, x, w_query, w_key, w_value, bias, lab_ref, *outs):
    qkv_ref = outs[0]
    width = w_query.shape[1]
    for i, weight in enumerate((w_query, w_key, w_value)):
        cols = slice(i * width, (i + 1) * width)
        value = matmul(x[...], weight[...]) + bias[:, cols].astype(F32)
        qkv_ref[:, cols] = value.astype(BF16)
    attend_pairs(lab_ref, *outs)


def attend_peer(core_ref, x_mine, x_other, w_mine, w_other, bias, lab_ref, *outs):
    qkv_ref = outs[0]
    width = qkv_ref.shape[1] // 3
    for i in range(3):
        cols = slice(i * width, (i + 1) * width)
        value = matmul(x_mine[...], w_mine[:, cols]) + matmul(x_other[...], w_other[:, cols])
        qkv_ref[:, cols] = (value + bias[:, cols].astype(F32)).astype(BF16)
    attend_pairs(lab_ref, *outs)


def run_attend_forward(core, tokens, weights, bias, labels, seq, own):
    rows, depth = tokens.shape
    cols = bias.shape[1]
    pairs = cols // (3 * 128)
    if own:
        xs = [pl.BlockSpec((seq, depth), lambda s, c: (s, 0))]
    else:
        xs = [
            pl.BlockSpec((seq, depth // 2), lambda s, c: (s, c[0])),
            pl.BlockSpec((seq, depth // 2), lambda s, c: (s, 1 - c[0])),
        ]
    fixed = [
        pl.BlockSpec(weight.shape, lambda s, c: (0, 0), pipeline_mode=pl.Buffered(1))
        for weight in (*weights, bias)
    ]
    return pl.pallas_call(
        attend_own if own else attend_peer,
        grid_spec=pltpu.PrefetchScalarGridSpec(
            num_scalar_prefetch=1,
            grid=(rows // seq,),
            in_specs=xs + fixed + [pl.BlockSpec((1, seq, 1), lambda s, c: (s, 0, 0))],
            out_specs=[
                pl.BlockSpec((seq, cols), lambda s, c: (s, 0)),
                pl.BlockSpec((seq, cols // 3), lambda s, c: (s, 0)),
                pl.BlockSpec((1, pairs, 2, seq), lambda s, c: (s, 0, 0, 0)),
            ],
        ),
        out_shape=[
            pltpu.HBM((rows, cols), BF16),
            pltpu.HBM((rows, cols // 3), BF16),
            jax.ShapeDtypeStruct((rows // seq, pairs, 2, seq), F32),
        ],
        compiler_params=pltpu.CompilerParams(vmem_limit_bytes=24 << 20),
        cost_estimate=pl.CostEstimate(
            flops=rows * pairs * 2 * seq * 256 * 2 * 3, bytes_accessed=8 << 20, transcendentals=0
        ),
        name="attend_forward",
    )(core, *[tokens] * len(xs), *weights, bias, labels)


def attend_backward(
    first,
    count,
    lone,
    core_ref,
    q_ref,
    k_ref,
    v_ref,
    out_ref,
    grad_ref,
    lab_ref,
    log_ref,
    x_keep,
    x_send,
    *refs,
):
    grads_ref, keep_ref, send_ref, bias_ref, keep_sum, send_sum, bias_sum = refs
    early = count - 1 if lone else count
    step = pl.program_id(0)
    labels = lab_ref[0]
    shape = (labels.shape[0], 128)
    low = lax.broadcasted_iota(jnp.int32, shape, 1) < HEAD_DIM
    q_extra, k_extra = query_marks(labels, shape), key_marks(labels, shape)
    for pair in range(count):
        cols = slice((first + pair) * 128, (first + pair + 1) * 128)
        q = q_ref[:, cols] * jnp.asarray(0.125, BF16)
        k, v, grad = k_ref[:, cols], v_ref[:, cols], grad_ref[:, cols]
        zero = jnp.zeros_like(q)
        inner = (grad.astype(F32) * out_ref[:, cols].astype(F32)).T
        dqs, dks, dvs = [], [], []
        for t in range(2):
            mine = low if t == 0 else jnp.logical_not(low)
            half = slice(t * HEAD_DIM, (t + 1) * HEAD_DIM)
            scores = dims(jnp.where(mine, k, k_extra), jnp.where(mine, q, q_extra), 1, 1)
            soft = jnp.exp(scores - log_ref[0, first + pair, t : t + 1])
            grad_soft = dims(v, jnp.where(mine, grad, zero), 1, 1)
            row_inner = jnp.sum(inner[half], axis=0, keepdims=True)
            grad_scores = (soft * (grad_soft - row_inner)).astype(BF16)
            dvs.append(dims(soft.astype(BF16), grad, 1, 0))
            dks.append(dims(grad_scores, q, 1, 0))
            dqs.append(dims(k, grad_scores, 0, 0)[half])
        found = (
            (jnp.concatenate(dqs, axis=0).T * 0.125).astype(BF16),
            jnp.where(low, dks[0], dks[1]).astype(BF16),
            jnp.where(low, dvs[0], dvs[1]).astype(BF16),
        )
        for i, value in enumerate(found):
            place = i * early + pair if pair < early else 3 * early + i
            grads_ref[:, place * 128 : (place + 1) * 128] = value

    grads = grads_ref[...]
    keep, send = dims(x_keep[...], grads, 0, 0), dims(x_send[...], grads, 0, 0)
    bias = jnp.sum(grads.astype(F32), axis=0, keepdims=True)

    @pl.when(step == 0)
    def _():
        keep_sum[...] = keep
        send_sum[...] = send
        bias_sum[...] = bias

    @pl.when(step > 0)
    def _():
        keep_sum[...] += keep
        send_sum[...] += send
        bias_sum[...] += bias

    @pl.when(step == pl.num_programs(0) - 1)
    def _():
        bias_ref[...] = bias_sum[...]
        keep_ref[...] = keep_sum[...].astype(BF16)
        send_ref[...] = send_sum[...].astype(BF16)


def run_attend_backward(
    core, qkv, out, grad, labels, logsum, tokens, seq, first, count, lone=False
):
    rows = qkv.shape[0]
    pairs = qkv.shape[1] // (3 * 128)
    cols = 3 * 128 * count
    half = tokens.shape[1] // 2
    held_pairs, skip = (1, first) if count == 1 else (pairs, 0)
    part = lambda which: pl.BlockSpec(
        (seq, held_pairs * 128),
        lambda s, c: (s, (which * pairs + skip) // held_pairs),
    )
    weight = (jax.ShapeDtypeStruct if lone else pltpu.HBM)((half, cols), BF16)
    fixed = lambda shape: pl.BlockSpec(shape, lambda s, c: (0, 0))
    return pl.pallas_call(
        functools.partial(attend_backward, first - skip, count, lone),
        grid_spec=pltpu.PrefetchScalarGridSpec(
            num_scalar_prefetch=1,
            grid=(rows // seq,),
            in_specs=[
                part(0),
                part(1),
                part(2),
                part(0),
                part(0),
                pl.BlockSpec((1, seq, 1), lambda s, c: (s, 0, 0)),
                pl.BlockSpec((1, held_pairs, 2, seq), lambda s, c: (s, skip, 0, 0)),
                pl.BlockSpec((seq, half), lambda s, c: (s, c[0])),
                pl.BlockSpec((seq, half), lambda s, c: (s, 1 - c[0])),
            ],
            out_specs=[
                pl.BlockSpec((seq, cols), lambda s, c: (s, 0)),
                fixed((half, cols)),
                fixed((half, cols)),
                fixed((1, cols)),
            ],
            scratch_shapes=[
                pltpu.VMEM((half, cols), F32),
                pltpu.VMEM((half, cols), F32),
                pltpu.VMEM((1, cols), F32),
            ],
        ),
        out_shape=[
            pltpu.HBM((rows, cols), BF16),
            weight,
            weight,
            jax.ShapeDtypeStruct((1, cols), F32),
        ],
        compiler_params=pltpu.CompilerParams(vmem_limit_bytes=26 << 20),
        cost_estimate=pl.CostEstimate(
            flops=rows * count * 2 * seq * 256 * 2 * 3, bytes_accessed=8 << 20, transcendentals=0
        ),
        name="attend_backward",
    )(
        core,
        *[far(qkv)] * 3,
        far(out),
        far(grad),
        labels,
        logsum,
        tokens,
        tokens,
    )


def gelu_pair(inner):
    phi = 0.5 + 0.5 * lax.erf(inner * 0.7071067811865476)
    bell = jnp.exp(-0.5 * (inner * inner))
    return inner * phi, phi + inner * (bell * 0.3989422804014327)


def norm_parts(values):
    centered = values - jnp.mean(values, axis=-1, keepdims=True)
    factor = lax.rsqrt(jnp.mean(centered * centered, axis=-1, keepdims=True) + NORM_EPS)
    return centered * factor, factor


def norm_back(grad_out, normed, factor, gain):
    scaled = grad_out * gain
    return factor * (
        scaled
        - jnp.mean(scaled, axis=-1, keepdims=True)
        - normed * jnp.mean(scaled * normed, axis=-1, keepdims=True)
    )


def feed_layer(seq, chunk, n_tok, n_hid, n_ctx, place_ref, count_ref, *refs):
    contexts, refs = refs[:n_ctx], refs[n_ctx:]
    tokens, cotangent, w_out_mine, w_out_other, w_up, w_down, vectors, b_up = refs[:8]
    y_ref, down, up, first_ref = refs[8], refs[9:13], refs[13:17], refs[17]
    grad_ctxs, (out_keep, out_send) = refs[18 : 18 + n_ctx], refs[18 + n_ctx : 20 + n_ctx]
    act, slope, normed, factor, hidden, mid, mid_low, total, sums, b_up_sum = refs[
        20 + n_ctx : 30 + n_ctx
    ]
    far_up, far_down = w_up, w_down
    w_up, w_down, w_out, up_sem, down_sem = refs[30 + n_ctx :]
    step = pl.program_id(0)
    block = tokens.shape[0]
    core, head = place_ref[0], place_ref[1]
    b_out, gain_one, shift_one, b_down, gain_two, shift_two = [
        vectors[i : i + 1] for i in range(6)
    ]

    def add(row, *values):
        for i, value in enumerate(values):
            sums[row + i : row + i + 1] += jnp.sum(value, axis=0, keepdims=True)

    @pl.when(step == 0)
    def _():
        pltpu.make_async_copy(far_up, w_up, up_sem).start()
        pltpu.make_async_copy(far_down, w_down, down_sem).start()
        w_out[: w_out_mine.shape[0]] = w_out_mine[...]
        w_out[w_out_mine.shape[0] :] = w_out_other[...]
        sums[...] = jnp.zeros_like(sums)
        total[...] = jnp.zeros_like(total)

    @pl.when(step < n_tok)
    def _():
        start = pl.multiple_of(step * block, block)
        here = pl.ds(start, block)
        context = jnp.concatenate([ctx[...] for ctx in contexts], axis=1)
        normed_one, factor_one = norm_parts(
            tokens[...].astype(F32) + matmul(context, w_out[...]) + b_out
        )
        normed[here] = normed_one
        factor[here] = jnp.broadcast_to(factor_one, (block, 128))
        hidden_here = normed_one * gain_one + shift_one
        hidden_low = hidden_here.astype(BF16)
        hidden[here] = hidden_low
        sum_two = hidden_here + b_down

        @pl.when(step == 0)
        def _():
            pltpu.make_async_copy(far_up, w_up, up_sem).wait()
            pltpu.make_async_copy(far_down, w_down, down_sem).wait()

        for j in range(w_up.shape[1] // chunk):
            cols = slice(j * chunk, (j + 1) * chunk)
            activated, gradient = gelu_pair(matmul(hidden_low, w_up[:, cols]) + b_up[:, cols])
            activated = activated.astype(BF16)
            act[here, cols] = activated
            slope[here, cols] = gradient.astype(BF16)
            sum_two = sum_two + matmul(activated, w_down[cols, :])
        normed_two, factor_two = norm_parts(sum_two)
        y_ref[...] = (normed_two * gain_two + shift_two).astype(BF16)
        place = start + lax.broadcasted_iota(jnp.int32, (block, 1), 0)
        live = (place % seq // (seq // MICRO) < count_ref[0]).astype(F32)
        grad_y = cotangent[...].astype(F32) * live
        grad_mid = norm_back(grad_y, normed_two, factor_two, gain_two)
        mid[here] = grad_mid
        mid_low[here] = grad_mid.astype(BF16)
        add(3, grad_y * normed_two, grad_y, grad_mid)

    @pl.when((step >= n_tok) & (step < n_tok + n_hid))
    def _():
        width = act.shape[1] // n_hid
        here = pl.ds(pl.multiple_of((step - n_tok) * width, width), width)

        def put(result, pieces):
            groups, group_rows, cols = pieces[0].shape
            result = result.reshape(groups, 2, group_rows, 2 * cols)
            for i in range(2):
                side = result[..., i * cols : (i + 1) * cols]
                pieces[i][...] = jnp.where(core == 0, side[:, 0], side[:, 1]).astype(BF16)
                pieces[2 + i][...] = jnp.where(core == 0, side[:, 1], side[:, 0]).astype(BF16)

        put(dims(act[:, here], mid_low[...], 0, 0), down)
        grad = dims(mid_low[...], w_down[here, :], 1, 1) * slope[:, here].astype(F32)
        grad = grad.astype(BF16)
        slope[:, here] = grad
        b_up_sum[:, here] = jnp.sum(grad.astype(F32), axis=0, keepdims=True)
        put(dims(grad, hidden[...], 0, 0), up)

    @pl.when(step >= n_tok + n_hid)
    def _():
        start = pl.multiple_of((step - n_tok - n_hid) * block, block)
        here = pl.ds(start, block)
        grad = mid[here] + dims(slope[here], w_up[...], 1, 1)
        normed_one = normed[here]
        grad_first = norm_back(grad, normed_one, factor[here, :1], gain_one)
        first_ref[...] = grad_first
        add(0, grad * normed_one, grad, grad_first)
        first_low = grad_first.astype(BF16)
        grad_ctx = dims(first_low, w_out[...], 1, 1).astype(BF16)
        start = 0
        for ref in grad_ctxs:
            ref[...] = grad_ctx[:, start : start + ref.shape[1]]
            start += ref.shape[1]
        context = jnp.concatenate([ctx[...] for ctx in contexts], axis=1)
        total[...] += dims(context, first_low, 0, 0)

    @pl.when(step == pl.num_programs(0) - 1)
    def _():
        lanes = [sums[i : i + 1] for i in range(6)] + [b_up_sum[...]]
        lanes = [
            row[:, k * 128 : (k + 1) * 128] for row in lanes for k in range(row.shape[1] // 128)
        ]
        n_side = len(lanes) // 2
        rows, d = out_keep.shape[1], total.shape[1]
        fill = jnp.zeros((rows - n_side, 128), F32)
        sides = [
            jnp.concatenate(part + [fill], axis=0) for part in (lanes[:n_side], lanes[n_side:])
        ]
        for i in range(2):
            side = jnp.where(head == i, sides[0], sides[1]).astype(BF16)
            for ref, which in ((out_keep, core), (out_send, 1 - core)):
                place = pl.multiple_of((2 * i + which) * rows, rows)
                ref[i, :, :d] = total[pl.ds(place, rows)].astype(BF16)
                ref[i, :, d:] = side


def run_feed_layer(
    seq,
    place,
    count,
    contexts,
    tokens,
    cotangent,
    w_out,
    w_up,
    w_down,
    vectors,
    b_up,
    rows_dev,
    block=512,
    width=768,
    chunk=1024,
):
    rows, d = tokens.shape
    ff = w_up.shape[1]
    group_rows = 2 * rows_dev
    groups = width // (2 * group_rows)
    n_tok, n_hid = rows // block, ff // width
    held = lambda shape: pl.BlockSpec(
        shape, lambda i, *_: (0,) * len(shape), pipeline_mode=pl.Buffered(1)
    )
    early = lambda cols: pl.BlockSpec(
        (block, cols), lambda i, *_: (jnp.minimum(i, n_tok - 1), 0)
    )
    late = lambda cols: pl.BlockSpec(
        (block, cols), lambda i, *_: (jnp.maximum(i - n_tok - n_hid, 0), 0)
    )
    twice = lambda cols: pl.BlockSpec(
        (block, cols),
        lambda i, *_: (jnp.where(i < n_tok, i, jnp.maximum(i - n_tok - n_hid, 0)), 0),
    )
    half_rows = lambda which: pl.BlockSpec(
        (d // 2, d), lambda i, place, _: (which(place), 0), pipeline_mode=pl.Buffered(1)
    )
    piece = pl.BlockSpec(
        (groups, group_rows, d // 2), lambda i, *_: (jnp.clip(i - n_tok, 0, n_hid - 1), 0, 0)
    )
    out = jax.ShapeDtypeStruct
    shape = (ff // (2 * group_rows), group_rows, d // 2)
    pieces = [pltpu.HBM(shape, BF16)] * 4 + [pltpu.HBM(shape, BF16)] * 4
    widths = [ctx.shape[1] for ctx in contexts]
    out_half = (2, d // 4, d + 128)
    return pl.pallas_call(
        functools.partial(feed_layer, seq, chunk, n_tok, n_hid, len(contexts)),
        grid_spec=pltpu.PrefetchScalarGridSpec(
            num_scalar_prefetch=2,
            grid=(2 * n_tok + n_hid,),
            in_specs=[twice(w) for w in widths]
            + [early(d), early(d)]
            + [half_rows(lambda place: place[1]), half_rows(lambda place: 1 - place[1])]
            + [pl.BlockSpec(memory_space=pl.ANY)] * 2
            + [held(vectors.shape), held(b_up.shape)],
            out_specs=[early(d)]
            + [piece] * 8
            + [late(d)]
            + [late(w) for w in widths]
            + [held(out_half)] * 2,
            scratch_shapes=[
                pltpu.VMEM((rows, ff), BF16),
                pltpu.VMEM((rows, ff), BF16),
                pltpu.VMEM((rows, d), F32),
                pltpu.VMEM((rows, 128), F32),
                pltpu.VMEM((rows, d), BF16),
                pltpu.VMEM((rows, d), F32),
                pltpu.VMEM((rows, d), BF16),
                pltpu.VMEM((d, d), F32),
                pltpu.VMEM((8, d), F32),
                pltpu.VMEM((1, ff), F32),
                pltpu.VMEM(w_up.shape, BF16),
                pltpu.VMEM(w_down.shape, BF16),
                pltpu.VMEM(w_out.shape, BF16),
                pltpu.SemaphoreType.DMA,
                pltpu.SemaphoreType.DMA,
            ],
        ),
        out_shape=[out((rows, d), BF16)]
        + pieces
        + [pltpu.HBM((rows, d), F32)]
        + [pltpu.HBM((rows, w), BF16) for w in widths]
        + [pltpu.HBM(out_half, BF16)] * 2,
        compiler_params=pltpu.CompilerParams(vmem_limit_bytes=60 << 20),
        cost_estimate=pl.CostEstimate(
            flops=4 * rows * d * (3 * d + 6 * ff), bytes_accessed=60 << 20, transcendentals=0
        ),
        name="feed_layer",
    )(
        place,
        count,
        *[far(ctx) for ctx in contexts],
        tokens,
        cotangent,
        w_out,
        w_out,
        far(w_up),
        far(w_down),
        vectors,
        b_up,
    )


class Cube:
    def __init__(self, mesh):
        self.size = mesh.shape["dp"] * mesh.shape["head"]
        self.n_bits = self.size.bit_length() - 1
        self.upper = list(range(2, self.n_bits))
        self.index = lax.axis_index("dp") * mesh.shape["head"] + lax.axis_index("head")

    def bit(self, which):
        return (self.index >> which) & 1

    def swap(self, value, which):
        pairs = [(i, i ^ (1 << which)) for i in range(self.size)]
        return lax.ppermute(value, AXES, pairs)

    def half(self, value, axis, which, mine):
        bit = self.bit(which) if mine else 1 - self.bit(which)
        return lax.dynamic_index_in_dim(value, bit, axis, keepdims=False)

    def join(self, value, other, which):
        first = self.bit(which) == 0
        return jnp.concatenate(
            [jnp.where(first, value, other), jnp.where(first, other, value)], axis=0
        )


    def core_pieces(self, keep, send, rows_dev):
        others = yield [(part, 1) for part in send]
        shape = (2,) * (self.n_bits - 1) + (rows_dev, keep[0].shape[-1])
        return [[term.reshape(shape) for term in pair] for pair in zip(keep, others)]

    def pieces(self, terms, order, done=()):
        bits = [bit for bit in range(self.n_bits - 1, 1, -1) if bit not in done] + [0]
        for step in order:
            axis = bits.index(step)
            send, kept = [sum(self.half(term, axis, step, mine) for term in terms) for mine in (0, 1)]
            other, kept = yield [(send, step), (kept, None)]
            terms = [kept, other]
            bits.remove(step)
        return sum(terms)

    def last_pieces(self, values, order, bits):
        value = jnp.concatenate(values, axis=-1)
        bits = sorted(bits, reverse=True)
        for step in order:
            axis = bits.index(step)
            send, kept = [self.half(value, axis, step, mine) for mine in (0, 1)]
            other, kept = yield [(send, step), (kept, None)]
            value = kept + other
            bits.remove(step)
        return value

    def reduce_rows(self, value, order):
        halved = []
        for which in order:
            rows = value.shape[0]
            if rows % 32 == 0 and rows > 96:
                value = value.reshape(2, rows // 2, value.shape[1])
                (other,) = yield [(self.half(value, 0, which, False), which)]
                value = self.half(value, 0, which, True) + other
                halved.append(which)
            else:
                value = lax.optimization_barrier(value)
                (other,) = yield [(value, which)]
                value = value + other
        return value, halved

    def gather_rows(self, value, halved):
        for which in reversed(halved):
            (other,) = yield [(value, which)]
            value = self.join(value, other, which)
        return value

    def sum_out(self, keep, send):
        (other,) = yield [(send, 1)]
        (other_two,) = yield [(keep[1] + other[1], 0)]
        value, halved = yield from self.reduce_rows(keep[0] + other[0] + other_two, self.upper)
        value = yield from self.gather_rows(value, halved)
        (other,) = yield [(value, 0)]
        value = jnp.concatenate([value, other], axis=1)
        value = yield from self.gather_rows(value, [1])
        return value[:, : value.shape[1] // 2], value[:, value.shape[1] // 2 :]

    def core_rows(self, keep, send):
        (other,) = yield [(send, 1)]
        return keep + other

    def sum_bias(self, own, peer):
        value = jnp.concatenate([own, peer], axis=0)
        (other,) = yield [(value, 1)]
        value = value + other
        (other,) = yield [(value[1:], 0)]
        value = value[:1] + other
        for which in self.upper:
            (other,) = yield [(value, which)]
            value = value + other
        return value

    def peer_rows(self, parts):
        value = jnp.concatenate(parts, axis=1)
        value = value.reshape(2, value.shape[0] // 2, value.shape[1])
        (other,) = yield [(self.half(value, 0, 2, False), 2)]
        value = self.half(value, 0, 2, True) + other
        (other,) = yield [(value, 0)]
        return other

    def own_rows(self, keep, send, peer):
        (other,) = yield [(send, 1)]
        value = keep + other
        value = value.reshape(2, value.shape[0] // 2, value.shape[1])
        (other,) = yield [(self.half(value, 0, 2, False), 2)]
        value = self.half(value, 0, 2, True) + other + peer.result
        value, halved = yield from self.reduce_rows(value, self.upper[1:])
        value = yield from self.gather_rows(value, [2] + halved)
        (other,) = yield [(value, 1)]
        return value, other


class Stream:
    def __init__(self, cube, steps):
        self.cube, self.steps, self.result = cube, steps, None
        self.wants = None
        self.advance(None)

    def advance(self, got):
        try:
            self.wants = self.steps.send(got)
        except StopIteration as stop:
            self.wants, self.result = None, stop.value

    def values(self):
        return tuple(value for value, _ in self.wants)

    def swaps(self):
        return tuple(
            value if which is None else self.cube.swap(value, which) for value, which in self.wants
        )


def tick(streams, work, *carry, wait=(), lazy=False):
    streams = [stream for stream in streams if stream.wants is not None]
    wait = [stream for stream in wait if stream.wants is not None and stream not in streams]
    moved = [list(stream.swaps()) for stream in streams]
    aside = []
    if lazy:
        for stream, got in zip(streams, moved):
            aside.append(
                {i: got[i] for i, (_, which) in enumerate(stream.wants) if which is None}
            )
            for i in aside[-1]:
                got[i] = ()
    later = [stream.values() for stream in wait]
    moved, work, carry, later = lax.optimization_barrier((moved, work, carry, later))
    for i, (stream, got) in enumerate(zip(streams, moved)):
        for place, value in (aside[i] if lazy else {}).items():
            got[place] = value
        stream.advance(got)
    for stream, values in zip(wait, later):
        stream.wants = [(value, which) for value, (_, which) in zip(values, stream.wants)]
    return (work, *carry)


def finish_own(core_ref, mine, other, w_query, w_key, w_value):
    rows = mine.shape[0]
    early = w_query.shape[1] - 128
    for value, which in ((mine, core_ref[0]), (other, 1 - core_ref[0])):
        here = pl.ds(pl.multiple_of(which * rows, rows), rows)
        for i, out in enumerate((w_query, w_key, w_value)):
            last = 3 * early + i * 128
            out[here, :early] = value[:, i * early : (i + 1) * early].astype(F32)
            out[here, early:] = value[:, last : last + 128].astype(F32)


def run_finish_own(core, mine, other):
    rows, cols = mine.shape
    return pl.pallas_call(
        finish_own,
        grid_spec=pltpu.PrefetchScalarGridSpec(
            num_scalar_prefetch=1,
            grid=(1,),
            in_specs=[pl.BlockSpec(mine.shape, lambda i, c: (0, 0))] * 2,
            out_specs=[pl.BlockSpec((2 * rows, cols // 3), lambda i, c: (0, 0))] * 3,
        ),
        out_shape=[jax.ShapeDtypeStruct((2 * rows, cols // 3), F32)] * 3,
        compiler_params=pltpu.CompilerParams(vmem_limit_bytes=24 << 20),
        name="finish_own",
    )(core, mine, other)


def shards(
    mesh,
    tokens,
    labels,
    micro_counts,
    w_query,
    b_query,
    w_key,
    w_value,
    b_value,
    w_out,
    b_out,
    gain_one,
    shift_one,
    w_up,
    b_up,
    w_down,
    b_down,
    gain_two,
    shift_two,
    cotangent,
):
    cube = Cube(mesh)
    rows, width = tokens.shape
    seq = labels.shape[1]
    half = w_query.shape[1]
    pairs = half // 128
    ff = w_up.shape[1]
    head, core = cube.bit(0), cube.bit(1)
    place = jnp.stack([core, head])
    cores = core[None]

    part = run_pick_rows(cores, w_query, w_key, w_value)
    own_bias = jnp.concatenate([b_query, jnp.zeros_like(b_query), b_value])[None]
    n_seq = rows // seq
    marks = lax.dynamic_slice_in_dim(labels, head * n_seq, n_seq, 0)[:, :, None]
    own_w = w_query, w_key, w_value
    own_qkv, own_ctx, own_log = run_attend_forward(
        cores, tokens, own_w, own_bias, marks, seq, True
    )
    mine, peer_bias, own_ctx, own_w = lax.optimization_barrier(
        (cube.swap(part, 0), cube.swap(own_bias, 0), own_ctx, own_w)
    )
    other = cube.swap(mine, 1)
    peer_qkv, peer_ctx, peer_log = run_attend_forward(
        cores, tokens, (mine, other), peer_bias, marks, seq, False
    )
    vectors = jnp.stack(
        [b_out, gain_one, shift_one, b_down, gain_two, shift_two, b_down, b_down]
    )
    rows_dev = ff // cube.size
    (
        layer_output,
        *pieces,
        grad_first,
        own_grad_ctx,
        peer_grad_ctx,
        out_keep,
        out_send,
    ) = run_feed_layer(
        seq,
        place,
        micro_counts,
        (own_ctx, peer_ctx),
        tokens,
        cotangent,
        w_out,
        w_up,
        w_down,
        vectors,
        b_up[None],
        rows_dev,
    )

    stream = lambda steps: Stream(cube, steps)
    down = stream(cube.core_pieces(pieces[:2], pieces[2:4], rows_dev))
    up = stream(cube.core_pieces(pieces[4:6], pieces[6:], rows_dev))
    out = stream(cube.sum_out(out_keep, out_send))


    def backward(qkv, ctx, grad_ctx, logsum, first, count, lone=False):
        return tuple(
            run_attend_backward(
                cores, qkv, ctx, grad_ctx, marks, logsum, tokens, seq, first, count, lone
            )
        )

    def side_by_side(first, count, weights):
        cols = slice(first * 128, (first + count) * 128)
        return jnp.concatenate([weight[:, cols] for weight in weights], axis=1)

    def finish_out(mine, other):
        first = head == 0
        both = jnp.concatenate(
            [jnp.where(first, mine, other), jnp.where(first, other, mine)], axis=0
        ).astype(F32)
        side = (ff + 6 * width) // 256
        small = jnp.concatenate([both[:side, width:], both[half : half + side, width:]], axis=0)
        return both[:, :width], small.reshape(-1, width)

    far_bits = cube.upper[1:]
    found = backward(peer_qkv, peer_ctx, peer_grad_ctx, peer_log, pairs - 1, 1)
    (grads_b, keep_b, send_b, sums_b), peer_grad_ctx = tick(
        [down, out], found, peer_grad_ctx, wait=[up]
    )
    down_a = stream(cube.pieces(down.result[0], [0, 2]))
    down_b = stream(cube.pieces(down.result[1], [2, 0]))
    core_b = stream(cube.core_rows(keep_b, send_b))
    found = backward(peer_qkv, peer_ctx, peer_grad_ctx, peer_log, 0, pairs - 1)
    (grads_a, keep_a, send_a, sums_a), own_grad_ctx = tick(
        [core_b, up, out], found, own_grad_ctx, wait=[down_a], lazy=True
    )
    up_a = stream(cube.pieces(up.result[0], [3]))
    up_b = stream(cube.pieces(up.result[1], [3]))
    core_a = stream(cube.core_rows(keep_a, send_a))
    (_, own_grad_ctx) = tick([core_a], (), own_grad_ctx, wait=[up_b])
    peer = stream(cube.peer_rows([core_a.result, core_b.result]))
    found = backward(own_qkv, own_ctx, own_grad_ctx, own_log, 0, pairs, True)
    (own_grads, keep, send, sums), grads_a, grads_b, grad_first, parts = tick(
        [down_a, down_b, up_a, out, peer],
        found,
        grads_a,
        grads_b,
        grad_first,
        (mine, other),
        wait=[up_b],
        lazy=True,
    )
    own = stream(cube.own_rows(keep, send, peer))
    bias = stream(cube.sum_bias(sums, jnp.concatenate([sums_a, sums_b], axis=1)))
    own_grads, grads_a, grads_b, parts, own_w = tick(
        [bias, own], own_grads, grads_a, grads_b, parts, own_w, wait=[down_a, down_b, up_b]
    )
    own_grads, grads_a, grads_b, parts, own_w = tick(
        [bias, out, peer, own], own_grads, grads_a, grads_b, parts, own_w, wait=[down_a, down_b]
    )
    early = 3 * (half - 128)
    peer_w = [cube.join(*parts, 1)[:, i * half : (i + 1) * half] for i in range(3)]
    grad_tokens = grad_first + dims(grads_a, side_by_side(0, pairs - 1, peer_w), 1, 1)
    grad_tokens = grad_tokens + dims(grads_b, side_by_side(pairs - 1, 1, peer_w), 1, 1)
    grad_tokens, own_grads, own_w = tick(
        [out, down_a, down_b, up_b, own], grad_tokens, own_grads, own_w, wait=[bias]
    )
    up_both = jnp.concatenate([up_a.result, up_b.result], axis=-1)
    up = stream(cube.pieces([up_both], [0, 2], far_bits[:1]))
    grad_tokens = grad_tokens + dims(own_grads[:, :early], side_by_side(0, pairs - 1, own_w), 1, 1)
    grad_tokens = grad_tokens + dims(own_grads[:, early:], side_by_side(pairs - 1, 1, own_w), 1, 1)
    down_far = stream(cube.last_pieces([down_a.result, down_b.result], far_bits, far_bits))
    (grad_tokens,) = tick([bias, out, up, down_far, own], grad_tokens)
    tick([bias, down_far, up, out, own], ())
    while any(stream.wants is not None for stream in (out, down_far)):
        tick([out, down_far], ())
    grad_w_out, small = finish_out(*out.result)
    rest = [small[i] for i in range(6)] + [small[6:].reshape(ff), down_far.result.astype(F32)]
    up_far = stream(cube.last_pieces([up.result], far_bits[1:], far_bits[1:]))
    ((grad_w_out, rest),) = tick([bias, up_far, own], (grad_w_out, rest))
    streams = [bias, own, up_far]
    while any(stream.wants is not None for stream in streams):
        tick(streams, ())
    grad_w_up = up_far.result

    grad_w_query, grad_w_key, grad_w_value = run_finish_own(cores, *own.result)
    total = bias.result[0]
    third = half - 128
    grad_b_query, grad_b_value = [
        jnp.concatenate(
            [total[i * third : (i + 1) * third], total[early + i * 128 : early + (i + 1) * 128]]
        )
        for i in (0, 2)
    ]
    return (
        layer_output,
        grad_tokens,
        grad_w_query,
        grad_b_query,
        grad_w_key,
        grad_w_value,
        grad_b_value,
        grad_w_out,
        rest[2],
        rest[0],
        rest[1],
        grad_w_up.astype(F32).T,
        rest[6],
        rest[7],
        rest[5],
        rest[3],
        rest[4],
    )


def solution(mesh):
    rows = P(("dp", "head"), None)
    placed = (rows, P("dp", None), P("dp"), P(None, "head"), P("head"), P(None, "head"))
    placed += (P(None, "head"), P("head")) + (P(),) * 10 + (rows,)
    columns = P(None, "head")
    out_specs = (rows, rows, columns, P("head"), columns, columns, P("head"))
    out_specs += (P(),) * 4 + (P(None, ("dp", "head")), P(), rows, P(), P(), P())
    return jax.shard_map(
        functools.partial(shards, mesh),
        mesh=mesh,
        in_specs=placed,
        out_specs=out_specs,
        check_vma=False,
    )
```

```python
import functools

import jax
import jax.numpy as jnp
from jax import lax
from jax.experimental import pallas as pl
from jax.experimental.pallas import tpu as pltpu
from jax.sharding import PartitionSpec as P

HEAD_DIM = 64
MICRO = 4
F32 = jnp.float32
BF16 = jnp.bfloat16
NORM_EPS = 1e-05
MASK = 2.0**30
AXES = ("dp", "head")


def dims(left, right, left_dim, right_dim):
    return lax.dot_general(
        left, right, (((left_dim,), (right_dim,)), ((), ())), preferred_element_type=F32
    )


def matmul(left, right):
    return jnp.dot(left, right, preferred_element_type=F32)


def far(value):
    return pltpu.with_memory_space_constraint(value, pltpu.HBM)


def query_marks(labels, shape):
    lane = lax.broadcasted_iota(jnp.int32, shape, 1)
    return jnp.where((lane & 63) == labels, 1.0, 0.0).astype(BF16)


def key_marks(labels, shape):
    lane = lax.broadcasted_iota(jnp.int32, shape, 1) & 63
    return jnp.where((lane < 4) & (lane != labels), -MASK, 0.0).astype(BF16)


def pick_rows(core_ref, w_query, w_key, w_value, out):
    half = w_query.shape[1]
    for i, weight in enumerate((w_query, w_key, w_value)):
        out[:, i * half : (i + 1) * half] = weight[...]


def run_pick_rows(core, w_query, w_key, w_value):
    width, half = w_query.shape
    rows = pl.BlockSpec((width // 2, half), lambda i, c: (c[0], 0))
    return pl.pallas_call(
        pick_rows,
        grid_spec=pltpu.PrefetchScalarGridSpec(
            num_scalar_prefetch=1,
            grid=(1,),
            in_specs=[rows] * 3,
            out_specs=pl.BlockSpec((width // 2, 3 * half), lambda i, c: (0, 0)),
        ),
        out_shape=jax.ShapeDtypeStruct((width // 2, 3 * half), BF16),
        name="pick_rows",
    )(core, far(w_query), far(w_key), far(w_value))


def attend_pairs(lab_ref, qkv_ref, out_ref, log_ref):
    labels = lab_ref[0]
    shape = (labels.shape[0], 128)
    half = out_ref.shape[1]
    low = lax.broadcasted_iota(jnp.int32, shape, 1) < HEAD_DIM
    q_extra, k_extra = query_marks(labels, shape), key_marks(labels, shape)
    for pair in range(half // 128):
        q, k, v = [
            qkv_ref[:, i * half + pair * 128 : i * half + (pair + 1) * 128] for i in range(3)
        ]
        q = q * jnp.asarray(0.125, BF16)
        outs = []
        for t in range(2):
            mine = low if t == 0 else jnp.logical_not(low)
            scores = dims(jnp.where(mine, k, k_extra), jnp.where(mine, q, q_extra), 1, 1)
            largest = jnp.max(scores, axis=0, keepdims=True)
            soft = jnp.exp(scores - largest)
            total = jnp.sum(soft, axis=0, keepdims=True)
            out = dims(v, soft.astype(BF16), 0, 0)
            outs.append(out[t * HEAD_DIM : (t + 1) * HEAD_DIM] * (1.0 / total))
            log_ref[0, pair, t : t + 1] = largest + jnp.log(total)
        out_ref[:, pair * 128 : (pair + 1) * 128] = jnp.concatenate(outs, axis=0).T.astype(BF16)


def attend_own(core_ref, x, w_query, w_key, w_value, bias, lab_ref, *outs):
    qkv_ref = outs[0]
    width = w_query.shape[1]
    for i, weight in enumerate((w_query, w_key, w_value)):
        cols = slice(i * width, (i + 1) * width)
        value = matmul(x[...], weight[...]) + bias[:, cols].astype(F32)
        qkv_ref[:, cols] = value.astype(BF16)
    attend_pairs(lab_ref, *outs)


def attend_peer(core_ref, x_mine, x_other, w_mine, w_other, bias, lab_ref, *outs):
    qkv_ref = outs[0]
    width = qkv_ref.shape[1] // 3
    for i in range(3):
        cols = slice(i * width, (i + 1) * width)
        value = matmul(x_mine[...], w_mine[:, cols]) + matmul(x_other[...], w_other[:, cols])
        qkv_ref[:, cols] = (value + bias[:, cols].astype(F32)).astype(BF16)
    attend_pairs(lab_ref, *outs)


def run_attend_forward(core, tokens, weights, bias, labels, seq, own):
    rows, depth = tokens.shape
    cols = bias.shape[1]
    pairs = cols // (3 * 128)
    if own:
        xs = [pl.BlockSpec((seq, depth), lambda s, c: (s, 0))]
    else:
        xs = [
            pl.BlockSpec((seq, depth // 2), lambda s, c: (s, c[0])),
            pl.BlockSpec((seq, depth // 2), lambda s, c: (s, 1 - c[0])),
        ]
    fixed = [
        pl.BlockSpec(weight.shape, lambda s, c: (0, 0), pipeline_mode=pl.Buffered(1))
        for weight in (*weights, bias)
    ]
    return pl.pallas_call(
        attend_own if own else attend_peer,
        grid_spec=pltpu.PrefetchScalarGridSpec(
            num_scalar_prefetch=1,
            grid=(rows // seq,),
            in_specs=xs + fixed + [pl.BlockSpec((1, seq, 1), lambda s, c: (s, 0, 0))],
            out_specs=[
                pl.BlockSpec((seq, cols), lambda s, c: (s, 0)),
                pl.BlockSpec((seq, cols // 3), lambda s, c: (s, 0)),
                pl.BlockSpec((1, pairs, 2, seq), lambda s, c: (s, 0, 0, 0)),
            ],
        ),
        out_shape=[
            pltpu.HBM((rows, cols), BF16),
            pltpu.HBM((rows, cols // 3), BF16),
            jax.ShapeDtypeStruct((rows // seq, pairs, 2, seq), F32),
        ],
        compiler_params=pltpu.CompilerParams(vmem_limit_bytes=24 << 20),
        cost_estimate=pl.CostEstimate(
            flops=rows * pairs * 2 * seq * 256 * 2 * 3, bytes_accessed=8 << 20, transcendentals=0
        ),
        name="attend_forward",
    )(core, *[tokens] * len(xs), *weights, bias, labels)


def attend_backward(
    first,
    count,
    lone,
    core_ref,
    q_ref,
    k_ref,
    v_ref,
    out_ref,
    grad_ref,
    lab_ref,
    log_ref,
    x_keep,
    x_send,
    *refs,
):
    grads_ref, keep_ref, send_ref, bias_ref, keep_sum, send_sum, bias_sum = refs
    early = count - 1 if lone else count
    step = pl.program_id(0)
    labels = lab_ref[0]
    shape = (labels.shape[0], 128)
    low = lax.broadcasted_iota(jnp.int32, shape, 1) < HEAD_DIM
    q_extra, k_extra = query_marks(labels, shape), key_marks(labels, shape)
    for pair in range(count):
        cols = slice((first + pair) * 128, (first + pair + 1) * 128)
        q = q_ref[:, cols] * jnp.asarray(0.125, BF16)
        k, v, grad = k_ref[:, cols], v_ref[:, cols], grad_ref[:, cols]
        zero = jnp.zeros_like(q)
        inner = (grad.astype(F32) * out_ref[:, cols].astype(F32)).T
        dqs, dks, dvs = [], [], []
        for t in range(2):
            mine = low if t == 0 else jnp.logical_not(low)
            half = slice(t * HEAD_DIM, (t + 1) * HEAD_DIM)
            scores = dims(jnp.where(mine, k, k_extra), jnp.where(mine, q, q_extra), 1, 1)
            soft = jnp.exp(scores - log_ref[0, first + pair, t : t + 1])
            grad_soft = dims(v, jnp.where(mine, grad, zero), 1, 1)
            row_inner = jnp.sum(inner[half], axis=0, keepdims=True)
            grad_scores = (soft * (grad_soft - row_inner)).astype(BF16)
            dvs.append(dims(soft.astype(BF16), grad, 1, 0))
            dks.append(dims(grad_scores, q, 1, 0))
            dqs.append(dims(k, grad_scores, 0, 0)[half])
        found = (
            (jnp.concatenate(dqs, axis=0).T * 0.125).astype(BF16),
            jnp.where(low, dks[0], dks[1]).astype(BF16),
            jnp.where(low, dvs[0], dvs[1]).astype(BF16),
        )
        for i, value in enumerate(found):
            place = i * early + pair if pair < early else 3 * early + i
            grads_ref[:, place * 128 : (place + 1) * 128] = value

    grads = grads_ref[...]
    keep, send = dims(x_keep[...], grads, 0, 0), dims(x_send[...], grads, 0, 0)
    bias = jnp.sum(grads.astype(F32), axis=0, keepdims=True)

    @pl.when(step == 0)
    def _():
        keep_sum[...] = keep
        send_sum[...] = send
        bias_sum[...] = bias

    @pl.when(step > 0)
    def _():
        keep_sum[...] += keep
        send_sum[...] += send
        bias_sum[...] += bias

    @pl.when(step == pl.num_programs(0) - 1)
    def _():
        bias_ref[...] = bias_sum[...]
        keep_ref[...] = keep_sum[...].astype(BF16)
        send_ref[...] = send_sum[...].astype(BF16)


def run_attend_backward(
    core, qkv, out, grad, labels, logsum, tokens, seq, first, count, lone=False
):
    rows = qkv.shape[0]
    pairs = qkv.shape[1] // (3 * 128)
    cols = 3 * 128 * count
    half = tokens.shape[1] // 2
    held_pairs, skip = (1, first) if count == 1 else (pairs, 0)
    part = lambda which: pl.BlockSpec(
        (seq, held_pairs * 128),
        lambda s, c: (s, (which * pairs + skip) // held_pairs),
    )
    weight = jax.ShapeDtypeStruct((half, cols), BF16)
    fixed = lambda shape: pl.BlockSpec(shape, lambda s, c: (0, 0))
    return pl.pallas_call(
        functools.partial(attend_backward, first - skip, count, lone),
        grid_spec=pltpu.PrefetchScalarGridSpec(
            num_scalar_prefetch=1,
            grid=(rows // seq,),
            in_specs=[
                part(0),
                part(1),
                part(2),
                part(0),
                part(0),
                pl.BlockSpec((1, seq, 1), lambda s, c: (s, 0, 0)),
                pl.BlockSpec((1, held_pairs, 2, seq), lambda s, c: (s, skip, 0, 0)),
                pl.BlockSpec((seq, half), lambda s, c: (s, c[0])),
                pl.BlockSpec((seq, half), lambda s, c: (s, 1 - c[0])),
            ],
            out_specs=[
                pl.BlockSpec((seq, cols), lambda s, c: (s, 0)),
                fixed((half, cols)),
                fixed((half, cols)),
                fixed((1, cols)),
            ],
            scratch_shapes=[
                pltpu.VMEM((half, cols), F32),
                pltpu.VMEM((half, cols), F32),
                pltpu.VMEM((1, cols), F32),
            ],
        ),
        out_shape=[
            pltpu.HBM((rows, cols), BF16),
            weight,
            weight,
            jax.ShapeDtypeStruct((1, cols), F32),
        ],
        compiler_params=pltpu.CompilerParams(vmem_limit_bytes=26 << 20),
        cost_estimate=pl.CostEstimate(
            flops=rows * count * 2 * seq * 256 * 2 * 3, bytes_accessed=8 << 20, transcendentals=0
        ),
        name="attend_backward",
    )(
        core,
        *[far(qkv)] * 3,
        far(out),
        far(grad),
        labels,
        logsum,
        tokens,
        tokens,
    )


def gelu_pair(inner):
    phi = 0.5 + 0.5 * lax.erf(inner * 0.7071067811865476)
    bell = jnp.exp(-0.5 * (inner * inner))
    return inner * phi, phi + inner * (bell * 0.3989422804014327)


def norm_parts(values):
    centered = values - jnp.mean(values, axis=-1, keepdims=True)
    factor = lax.rsqrt(jnp.mean(centered * centered, axis=-1, keepdims=True) + NORM_EPS)
    return centered * factor, factor


def norm_back(grad_out, normed, factor, gain):
    scaled = grad_out * gain
    return factor * (
        scaled
        - jnp.mean(scaled, axis=-1, keepdims=True)
        - normed * jnp.mean(scaled * normed, axis=-1, keepdims=True)
    )


def feed_layer(seq, chunk, n_tok, n_hid, n_ctx, place_ref, count_ref, *refs):
    contexts, refs = refs[:n_ctx], refs[n_ctx:]
    tokens, cotangent, w_out_mine, w_out_other, w_up, w_down, vectors, b_up = refs[:8]
    y_ref, down, up, first_ref = refs[8], refs[9:13], refs[13:17], refs[17]
    grad_ctxs, (out_keep, out_send) = refs[18 : 18 + n_ctx], refs[18 + n_ctx : 20 + n_ctx]
    act, slope, normed, factor, hidden, mid, mid_low, total, sums, b_up_sum = refs[
        20 + n_ctx : 30 + n_ctx
    ]
    far_up, far_down = w_up, w_down
    w_up, w_down, w_out, up_sem, down_sem = refs[30 + n_ctx :]
    step = pl.program_id(0)
    block = tokens.shape[0]
    core, head = place_ref[0], place_ref[1]
    b_out, gain_one, shift_one, b_down, gain_two, shift_two = [
        vectors[i : i + 1] for i in range(6)
    ]

    def add(row, *values):
        for i, value in enumerate(values):
            sums[row + i : row + i + 1] += jnp.sum(value, axis=0, keepdims=True)

    @pl.when(step == 0)
    def _():
        pltpu.make_async_copy(far_up, w_up, up_sem).start()
        pltpu.make_async_copy(far_down, w_down, down_sem).start()
        w_out[: w_out_mine.shape[0]] = w_out_mine[...]
        w_out[w_out_mine.shape[0] :] = w_out_other[...]
        sums[...] = jnp.zeros_like(sums)
        total[...] = jnp.zeros_like(total)

    @pl.when(step < n_tok)
    def _():
        start = pl.multiple_of(step * block, block)
        here = pl.ds(start, block)
        context = jnp.concatenate([ctx[...] for ctx in contexts], axis=1)
        normed_one, factor_one = norm_parts(
            tokens[...].astype(F32) + matmul(context, w_out[...]) + b_out
        )
        normed[here] = normed_one
        factor[here] = jnp.broadcast_to(factor_one, (block, 128))
        hidden_here = normed_one * gain_one + shift_one
        hidden_low = hidden_here.astype(BF16)
        hidden[here] = hidden_low
        sum_two = hidden_here + b_down

        @pl.when(step == 0)
        def _():
            pltpu.make_async_copy(far_up, w_up, up_sem).wait()
            pltpu.make_async_copy(far_down, w_down, down_sem).wait()

        for j in range(w_up.shape[1] // chunk):
            cols = slice(j * chunk, (j + 1) * chunk)
            activated, gradient = gelu_pair(matmul(hidden_low, w_up[:, cols]) + b_up[:, cols])
            activated = activated.astype(BF16)
            act[here, cols] = activated
            slope[here, cols] = gradient.astype(BF16)
            sum_two = sum_two + matmul(activated, w_down[cols, :])
        normed_two, factor_two = norm_parts(sum_two)
        y_ref[...] = (normed_two * gain_two + shift_two).astype(BF16)
        place = start + lax.broadcasted_iota(jnp.int32, (block, 1), 0)
        live = (place % seq // (seq // MICRO) < count_ref[0]).astype(F32)
        grad_y = cotangent[...].astype(F32) * live
        grad_mid = norm_back(grad_y, normed_two, factor_two, gain_two)
        mid[here] = grad_mid
        mid_low[here] = grad_mid.astype(BF16)
        add(3, grad_y * normed_two, grad_y, grad_mid)

    @pl.when((step >= n_tok) & (step < n_tok + n_hid))
    def _():
        width = act.shape[1] // n_hid
        here = pl.ds(pl.multiple_of((step - n_tok) * width, width), width)

        def put(result, pieces):
            groups, group_rows, cols = pieces[0].shape
            result = result.reshape(groups, 2, group_rows, 2 * cols)
            for i in range(2):
                side = result[..., i * cols : (i + 1) * cols]
                pieces[i][...] = jnp.where(core == 0, side[:, 0], side[:, 1]).astype(BF16)
                pieces[2 + i][...] = jnp.where(core == 0, side[:, 1], side[:, 0]).astype(BF16)

        put(dims(act[:, here], mid_low[...], 0, 0), down)
        grad = dims(mid_low[...], w_down[here, :], 1, 1) * slope[:, here].astype(F32)
        grad = grad.astype(BF16)
        slope[:, here] = grad
        b_up_sum[:, here] = jnp.sum(grad.astype(F32), axis=0, keepdims=True)
        put(dims(grad, hidden[...], 0, 0), up)

    @pl.when(step >= n_tok + n_hid)
    def _():
        start = pl.multiple_of((step - n_tok - n_hid) * block, block)
        here = pl.ds(start, block)
        grad = mid[here] + dims(slope[here], w_up[...], 1, 1)
        normed_one = normed[here]
        grad_first = norm_back(grad, normed_one, factor[here, :1], gain_one)
        first_ref[...] = grad_first
        add(0, grad * normed_one, grad, grad_first)
        first_low = grad_first.astype(BF16)
        grad_ctx = dims(first_low, w_out[...], 1, 1).astype(BF16)
        start = 0
        for ref in grad_ctxs:
            ref[...] = grad_ctx[:, start : start + ref.shape[1]]
            start += ref.shape[1]
        context = jnp.concatenate([ctx[...] for ctx in contexts], axis=1)
        total[...] += dims(context, first_low, 0, 0)

    @pl.when(step == pl.num_programs(0) - 1)
    def _():
        lanes = [sums[i : i + 1] for i in range(6)] + [b_up_sum[...]]
        lanes = [
            row[:, k * 128 : (k + 1) * 128] for row in lanes for k in range(row.shape[1] // 128)
        ]
        n_side = len(lanes) // 2
        rows, d = out_keep.shape[1], total.shape[1]
        fill = jnp.zeros((rows - n_side, 128), F32)
        sides = [
            jnp.concatenate(part + [fill], axis=0) for part in (lanes[:n_side], lanes[n_side:])
        ]
        for i in range(2):
            side = jnp.where(head == i, sides[0], sides[1]).astype(BF16)
            for ref, which in ((out_keep, core), (out_send, 1 - core)):
                place = pl.multiple_of((2 * i + which) * rows, rows)
                ref[i, :, :d] = total[pl.ds(place, rows)].astype(BF16)
                ref[i, :, d:] = side


def run_feed_layer(
    seq,
    place,
    count,
    contexts,
    tokens,
    cotangent,
    w_out,
    w_up,
    w_down,
    vectors,
    b_up,
    rows_dev,
    block=512,
    width=768,
    chunk=1024,
):
    rows, d = tokens.shape
    ff = w_up.shape[1]
    group_rows = 2 * rows_dev
    groups = width // (2 * group_rows)
    n_tok, n_hid = rows // block, ff // width
    held = lambda shape: pl.BlockSpec(
        shape, lambda i, *_: (0,) * len(shape), pipeline_mode=pl.Buffered(1)
    )
    early = lambda cols: pl.BlockSpec(
        (block, cols), lambda i, *_: (jnp.minimum(i, n_tok - 1), 0)
    )
    late = lambda cols: pl.BlockSpec(
        (block, cols), lambda i, *_: (jnp.maximum(i - n_tok - n_hid, 0), 0)
    )
    twice = lambda cols: pl.BlockSpec(
        (block, cols),
        lambda i, *_: (jnp.where(i < n_tok, i, jnp.maximum(i - n_tok - n_hid, 0)), 0),
    )
    half_rows = lambda which: pl.BlockSpec(
        (d // 2, d), lambda i, place, _: (which(place), 0), pipeline_mode=pl.Buffered(1)
    )
    piece = pl.BlockSpec(
        (groups, group_rows, d // 2), lambda i, *_: (jnp.clip(i - n_tok, 0, n_hid - 1), 0, 0)
    )
    out = jax.ShapeDtypeStruct
    shape = (ff // (2 * group_rows), group_rows, d // 2)
    pieces = [pltpu.HBM(shape, BF16)] * 4 + [pltpu.HBM(shape, BF16)] * 4
    widths = [ctx.shape[1] for ctx in contexts]
    out_half = (2, d // 4, d + 128)
    return pl.pallas_call(
        functools.partial(feed_layer, seq, chunk, n_tok, n_hid, len(contexts)),
        grid_spec=pltpu.PrefetchScalarGridSpec(
            num_scalar_prefetch=2,
            grid=(2 * n_tok + n_hid,),
            in_specs=[twice(w) for w in widths]
            + [early(d), early(d)]
            + [half_rows(lambda place: place[1]), half_rows(lambda place: 1 - place[1])]
            + [pl.BlockSpec(memory_space=pl.ANY)] * 2
            + [held(vectors.shape), held(b_up.shape)],
            out_specs=[early(d)]
            + [piece] * 8
            + [late(d)]
            + [late(w) for w in widths]
            + [held(out_half)] * 2,
            scratch_shapes=[
                pltpu.VMEM((rows, ff), BF16),
                pltpu.VMEM((rows, ff), BF16),
                pltpu.VMEM((rows, d), F32),
                pltpu.VMEM((rows, 128), F32),
                pltpu.VMEM((rows, d), BF16),
                pltpu.VMEM((rows, d), F32),
                pltpu.VMEM((rows, d), BF16),
                pltpu.VMEM((d, d), F32),
                pltpu.VMEM((8, d), F32),
                pltpu.VMEM((1, ff), F32),
                pltpu.VMEM(w_up.shape, BF16),
                pltpu.VMEM(w_down.shape, BF16),
                pltpu.VMEM(w_out.shape, BF16),
                pltpu.SemaphoreType.DMA,
                pltpu.SemaphoreType.DMA,
            ],
        ),
        out_shape=[out((rows, d), BF16)]
        + pieces
        + [pltpu.HBM((rows, d), F32)]
        + [pltpu.HBM((rows, w), BF16) for w in widths]
        + [pltpu.HBM(out_half, BF16)] * 2,
        compiler_params=pltpu.CompilerParams(vmem_limit_bytes=60 << 20),
        cost_estimate=pl.CostEstimate(
            flops=4 * rows * d * (3 * d + 6 * ff), bytes_accessed=60 << 20, transcendentals=0
        ),
        name="feed_layer",
    )(
        place,
        count,
        *[far(ctx) for ctx in contexts],
        tokens,
        cotangent,
        w_out,
        w_out,
        far(w_up),
        far(w_down),
        vectors,
        b_up,
    )


class Cube:
    def __init__(self, mesh):
        self.size = mesh.shape["dp"] * mesh.shape["head"]
        self.n_bits = self.size.bit_length() - 1
        self.upper = list(range(2, self.n_bits))
        self.index = lax.axis_index("dp") * mesh.shape["head"] + lax.axis_index("head")

    def bit(self, which):
        return (self.index >> which) & 1

    def swap(self, value, which):
        pairs = [(i, i ^ (1 << which)) for i in range(self.size)]
        return lax.ppermute(value, AXES, pairs)

    def half(self, value, axis, which, mine):
        bit = self.bit(which) if mine else 1 - self.bit(which)
        return lax.dynamic_index_in_dim(value, bit, axis, keepdims=False)

    def join(self, value, other, which):
        first = self.bit(which) == 0
        return jnp.concatenate(
            [jnp.where(first, value, other), jnp.where(first, other, value)], axis=0
        )


    def core_pieces(self, keep, send, rows_dev):
        others = yield [(part, 1) for part in send]
        shape = (2,) * (self.n_bits - 1) + (rows_dev, keep[0].shape[-1])
        return [[term.reshape(shape) for term in pair] for pair in zip(keep, others)]

    def pieces(self, terms, order, done=()):
        bits = [bit for bit in range(self.n_bits - 1, 1, -1) if bit not in done] + [0]
        for step in order:
            axis = bits.index(step)
            send, kept = [sum(self.half(term, axis, step, mine) for term in terms) for mine in (0, 1)]
            other, kept = yield [(send, step), (kept, None)]
            terms = [kept, other]
            bits.remove(step)
        return sum(terms)

    def last_pieces(self, values, order, bits):
        value = jnp.concatenate(values, axis=-1)
        bits = sorted(bits, reverse=True)
        for step in order:
            axis = bits.index(step)
            send, kept = [self.half(value, axis, step, mine) for mine in (0, 1)]
            other, kept = yield [(send, step), (kept, None)]
            value = kept + other
            bits.remove(step)
        return value

    def reduce_rows(self, value, order):
        halved = []
        for which in order:
            rows = value.shape[0]
            if rows % 32 == 0 and rows > 96:
                value = value.reshape(2, rows // 2, value.shape[1])
                (other,) = yield [(self.half(value, 0, which, False), which)]
                value = self.half(value, 0, which, True) + other
                halved.append(which)
            else:
                value = lax.optimization_barrier(value)
                (other,) = yield [(value, which)]
                value = value + other
        return value, halved

    def gather_rows(self, value, halved):
        for which in reversed(halved):
            (other,) = yield [(value, which)]
            value = self.join(value, other, which)
        return value

    def sum_out(self, keep, send):
        (other,) = yield [(send, 1)]
        (other_two,) = yield [(keep[1] + other[1], 0)]
        value, halved = yield from self.reduce_rows(keep[0] + other[0] + other_two, self.upper)
        value = yield from self.gather_rows(value, halved)
        (other,) = yield [(value, 0)]
        value = jnp.concatenate([value, other], axis=1)
        value = yield from self.gather_rows(value, [1])
        return value[:, : value.shape[1] // 2], value[:, value.shape[1] // 2 :]

    def core_rows(self, keep, send):
        (other,) = yield [(send, 1)]
        return keep + other

    def sum_bias(self, own, peer):
        value = jnp.concatenate([own, peer], axis=0)
        (other,) = yield [(value, 1)]
        value = value + other
        (other,) = yield [(value[1:], 0)]
        value = value[:1] + other
        for which in self.upper:
            (other,) = yield [(value, which)]
            value = value + other
        return value

    def peer_rows(self, parts):
        value = jnp.concatenate(parts, axis=1)
        value = value.reshape(2, value.shape[0] // 2, value.shape[1])
        (other,) = yield [(self.half(value, 0, 2, False), 2)]
        value = self.half(value, 0, 2, True) + other
        (other,) = yield [(value, 0)]
        return other

    def own_rows(self, keep, send, peer):
        (other,) = yield [(send, 1)]
        value = keep + other
        value = value.reshape(2, value.shape[0] // 2, value.shape[1])
        (other,) = yield [(self.half(value, 0, 2, False), 2)]
        value = self.half(value, 0, 2, True) + other + peer.result
        value, halved = yield from self.reduce_rows(value, self.upper[1:])
        value = yield from self.gather_rows(value, [2] + halved)
        (other,) = yield [(value, 1)]
        return value, other


class Stream:
    def __init__(self, cube, steps):
        self.cube, self.steps, self.result = cube, steps, None
        self.wants = None
        self.advance(None)

    def advance(self, got):
        try:
            self.wants = self.steps.send(got)
        except StopIteration as stop:
            self.wants, self.result = None, stop.value

    def values(self):
        return tuple(value for value, _ in self.wants)

    def swaps(self):
        return tuple(
            value if which is None else self.cube.swap(value, which) for value, which in self.wants
        )


def tick(streams, work, *carry, wait=(), lazy=False):
    streams = [stream for stream in streams if stream.wants is not None]
    wait = [stream for stream in wait if stream.wants is not None and stream not in streams]
    moved = [list(stream.swaps()) for stream in streams]
    aside = []
    if lazy:
        for stream, got in zip(streams, moved):
            aside.append(
                {i: got[i] for i, (_, which) in enumerate(stream.wants) if which is None}
            )
            for i in aside[-1]:
                got[i] = ()
    later = [stream.values() for stream in wait]
    moved, work, carry, later = lax.optimization_barrier((moved, work, carry, later))
    for i, (stream, got) in enumerate(zip(streams, moved)):
        for place, value in (aside[i] if lazy else {}).items():
            got[place] = value
        stream.advance(got)
    for stream, values in zip(wait, later):
        stream.wants = [(value, which) for value, (_, which) in zip(values, stream.wants)]
    return (work, *carry)


def finish_own(core_ref, mine, other, w_query, w_key, w_value):
    rows = mine.shape[0]
    early = w_query.shape[1] - 128
    for value, which in ((mine, core_ref[0]), (other, 1 - core_ref[0])):
        here = pl.ds(pl.multiple_of(which * rows, rows), rows)
        for i, out in enumerate((w_query, w_key, w_value)):
            last = 3 * early + i * 128
            out[here, :early] = value[:, i * early : (i + 1) * early].astype(F32)
            out[here, early:] = value[:, last : last + 128].astype(F32)


def run_finish_own(core, mine, other):
    rows, cols = mine.shape
    return pl.pallas_call(
        finish_own,
        grid_spec=pltpu.PrefetchScalarGridSpec(
            num_scalar_prefetch=1,
            grid=(1,),
            in_specs=[pl.BlockSpec(mine.shape, lambda i, c: (0, 0))] * 2,
            out_specs=[pl.BlockSpec((2 * rows, cols // 3), lambda i, c: (0, 0))] * 3,
        ),
        out_shape=[jax.ShapeDtypeStruct((2 * rows, cols // 3), F32)] * 3,
        compiler_params=pltpu.CompilerParams(vmem_limit_bytes=24 << 20),
        name="finish_own",
    )(core, mine, other)


def shards(
    mesh,
    tokens,
    labels,
    micro_counts,
    w_query,
    b_query,
    w_key,
    w_value,
    b_value,
    w_out,
    b_out,
    gain_one,
    shift_one,
    w_up,
    b_up,
    w_down,
    b_down,
    gain_two,
    shift_two,
    cotangent,
):
    cube = Cube(mesh)
    rows, width = tokens.shape
    seq = labels.shape[1]
    half = w_query.shape[1]
    pairs = half // 128
    ff = w_up.shape[1]
    head, core = cube.bit(0), cube.bit(1)
    place = jnp.stack([core, head])
    cores = core[None]

    part = run_pick_rows(cores, w_query, w_key, w_value)
    own_bias = jnp.concatenate([b_query, jnp.zeros_like(b_query), b_value])[None]
    n_seq = rows // seq
    marks = lax.dynamic_slice_in_dim(labels, head * n_seq, n_seq, 0)[:, :, None]
    own_w = w_query, w_key, w_value
    own_qkv, own_ctx, own_log = run_attend_forward(
        cores, tokens, own_w, own_bias, marks, seq, True
    )
    mine, peer_bias, own_ctx, own_w = lax.optimization_barrier(
        (cube.swap(part, 0), cube.swap(own_bias, 0), own_ctx, own_w)
    )
    other = cube.swap(mine, 1)
    peer_qkv, peer_ctx, peer_log = run_attend_forward(
        cores, tokens, (mine, other), peer_bias, marks, seq, False
    )
    vectors = jnp.stack(
        [b_out, gain_one, shift_one, b_down, gain_two, shift_two, b_down, b_down]
    )
    rows_dev = ff // cube.size
    (
        layer_output,
        *pieces,
        grad_first,
        own_grad_ctx,
        peer_grad_ctx,
        out_keep,
        out_send,
    ) = run_feed_layer(
        seq,
        place,
        micro_counts,
        (own_ctx, peer_ctx),
        tokens,
        cotangent,
        w_out,
        w_up,
        w_down,
        vectors,
        b_up[None],
        rows_dev,
    )

    stream = lambda steps: Stream(cube, steps)
    down = stream(cube.core_pieces(pieces[:2], pieces[2:4], rows_dev))
    up = stream(cube.core_pieces(pieces[4:6], pieces[6:], rows_dev))
    out = stream(cube.sum_out(out_keep, out_send))


    def backward(qkv, ctx, grad_ctx, logsum, first, count, lone=False):
        return tuple(
            run_attend_backward(
                cores, qkv, ctx, grad_ctx, marks, logsum, tokens, seq, first, count, lone
            )
        )

    def side_by_side(first, count, weights):
        cols = slice(first * 128, (first + count) * 128)
        return jnp.concatenate([weight[:, cols] for weight in weights], axis=1)

    def finish_out(mine, other):
        first = head == 0
        both = jnp.concatenate(
            [jnp.where(first, mine, other), jnp.where(first, other, mine)], axis=0
        ).astype(F32)
        side = (ff + 6 * width) // 256
        small = jnp.concatenate([both[:side, width:], both[half : half + side, width:]], axis=0)
        return both[:, :width], small.reshape(-1, width)

    far_bits = cube.upper[1:]
    found = backward(peer_qkv, peer_ctx, peer_grad_ctx, peer_log, pairs - 1, 1)
    (grads_b, keep_b, send_b, sums_b), peer_grad_ctx = tick(
        [down, out], found, peer_grad_ctx, wait=[up]
    )
    down_a = stream(cube.pieces(down.result[0], [0, 2]))
    down_b = stream(cube.pieces(down.result[1], [2, 0]))
    core_b = stream(cube.core_rows(keep_b, send_b))
    found = backward(peer_qkv, peer_ctx, peer_grad_ctx, peer_log, 0, pairs - 1)
    (grads_a, keep_a, send_a, sums_a), own_grad_ctx = tick(
        [core_b, up, out], found, own_grad_ctx, wait=[down_a], lazy=True
    )
    up_a = stream(cube.pieces(up.result[0], [3]))
    up_b = stream(cube.pieces(up.result[1], [3]))
    core_a = stream(cube.core_rows(keep_a, send_a))
    (_, own_grad_ctx) = tick([core_a], (), own_grad_ctx, wait=[up_b])
    peer = stream(cube.peer_rows([core_a.result, core_b.result]))
    found = backward(own_qkv, own_ctx, own_grad_ctx, own_log, 0, pairs, True)
    (own_grads, keep, send, sums), grads_a, grads_b, grad_first, parts = tick(
        [down_a, down_b, up_a, out, peer],
        found,
        grads_a,
        grads_b,
        grad_first,
        (mine, other),
        wait=[up_b],
        lazy=True,
    )
    own = stream(cube.own_rows(keep, send, peer))
    bias = stream(cube.sum_bias(sums, jnp.concatenate([sums_a, sums_b], axis=1)))
    own_grads, grads_a, grads_b, parts, own_w = tick(
        [bias, own], own_grads, grads_a, grads_b, parts, own_w, wait=[down_a, down_b, up_b]
    )
    own_grads, grads_a, grads_b, parts, own_w = tick(
        [bias, out, peer, own], own_grads, grads_a, grads_b, parts, own_w, wait=[down_a, down_b]
    )
    early = 3 * (half - 128)
    peer_w = [cube.join(*parts, 1)[:, i * half : (i + 1) * half] for i in range(3)]
    grad_tokens = grad_first + dims(grads_a, side_by_side(0, pairs - 1, peer_w), 1, 1)
    grad_tokens = grad_tokens + dims(grads_b, side_by_side(pairs - 1, 1, peer_w), 1, 1)
    grad_tokens, own_grads, own_w = tick(
        [out, down_a, down_b, up_b, own], grad_tokens, own_grads, own_w, wait=[bias]
    )
    up_both = jnp.concatenate([up_a.result, up_b.result], axis=-1)
    up = stream(cube.pieces([up_both], [0, 2], far_bits[:1]))
    grad_tokens = grad_tokens + dims(own_grads[:, :early], side_by_side(0, pairs - 1, own_w), 1, 1)
    grad_tokens = grad_tokens + dims(own_grads[:, early:], side_by_side(pairs - 1, 1, own_w), 1, 1)
    down_far = stream(cube.last_pieces([down_a.result, down_b.result], far_bits, far_bits))
    (grad_tokens,) = tick([bias, out, up, down_far, own], grad_tokens)
    tick([bias, down_far, up, out, own], ())
    while any(stream.wants is not None for stream in (out, down_far)):
        tick([out, down_far], ())
    grad_w_out, small = finish_out(*out.result)
    rest = [small[i] for i in range(6)] + [small[6:].reshape(ff), down_far.result.astype(F32)]
    up_far = stream(cube.last_pieces([up.result], far_bits[1:], far_bits[1:]))
    ((grad_w_out, rest),) = tick([bias, up_far, own], (grad_w_out, rest))
    streams = [bias, own, up_far]
    while any(stream.wants is not None for stream in streams):
        tick(streams, ())
    grad_w_up = up_far.result

    grad_w_query, grad_w_key, grad_w_value = run_finish_own(cores, *own.result)
    total = bias.result[0]
    third = half - 128
    grad_b_query, grad_b_value = [
        jnp.concatenate(
            [total[i * third : (i + 1) * third], total[early + i * 128 : early + (i + 1) * 128]]
        )
        for i in (0, 2)
    ]
    return (
        layer_output,
        grad_tokens,
        grad_w_query,
        grad_b_query,
        grad_w_key,
        grad_w_value,
        grad_b_value,
        grad_w_out,
        rest[2],
        rest[0],
        rest[1],
        grad_w_up.astype(F32).T,
        rest[6],
        rest[7],
        rest[5],
        rest[3],
        rest[4],
    )


def solution(mesh):
    rows = P(("dp", "head"), None)
    placed = (rows, P("dp", None), P("dp"), P(None, "head"), P("head"), P(None, "head"))
    placed += (P(None, "head"), P("head")) + (P(),) * 10 + (rows,)
    columns = P(None, "head")
    out_specs = (rows, rows, columns, P("head"), columns, columns, P("head"))
    out_specs += (P(),) * 4 + (P(None, ("dp", "head")), P(), rows, P(), P(), P())
    return jax.shard_map(
        functools.partial(shards, mesh),
        mesh=mesh,
        in_specs=placed,
        out_specs=out_specs,
        check_vma=False,
    )
```
